32 devices in a mesh: section: 2 (over core), shard: 4 (over y, x), dp: 4 (over z).
Axes of the slice: x: 2, y: 2, z: 4, core: 2. Of those that a mesh axis runs over, the one named last changes fastest.
Arguments:
- ends_in: bfloat16 [2, 2048, 2048], P('section', ('shard', 'dp')), may hold values from -6 to 6
- in_weight: bfloat16 [2, 2048, 19456], P('section', 'shard'), may hold values from -0.125 to 0.125
- out_weight: bfloat16 [2, 2048, 10240], P('section', 'shard')
- norm_gain: float32 [2, 2, 2048], P('section'), may hold values from 0.5 to 1.5
- seq_len: int32 [32], P(('shard', 'dp')), may hold values from 1 to 64, as said below
Outputs:
- ends_out: bfloat16 [2, 2048, 2048], P('section', ('shard', 'dp'))
- in_grad: float32 [2, 2048, 19456], P('section', ('shard', 'dp'))
- out_grad: float32 [2, 2048, 10240], P('section', ('shard', 'dp'))
- gain_grad: float32 [2, 2, 2048], P('section', None, ('shard', 'dp'))
The draws below stay inside these ranges and needn't reach their ends.
Inputs may be any that keep to these rules, and one draw needn't show every extreme that they name: `seq_len`: each value is the live length of one slot of 64 positions; lengths differ from slot to slot and from device to device, and some slot is full in every draw.
All inputs are finite; a program needn't handle non-finite values.
Results may differ from the reference program's by a relative error of at most 0.02.
Values may be sent and summed in bfloat16 or wider, within the bound.
A program may use at most 960 MiB of HBM per device.

```python
import jax
import jax.numpy as jnp
from jax import lax

D = 2048
HEADS = 32
KV_HEADS = 8
HEAD_DIM = 64
FF = 8192
MICRO = 2
SEQ_SLOT = 64
TOKENS = 2048
SEQS = 32
QKV_COLS = 3072
IN_COLS = 19456
OUT_COLS = 10240
N_SECTION = 2


def draw_out_weight(key, part):
    key = jax.random.fold_in(key, 7)
    shape = (N_SECTION, D, OUT_COLS)
    columns = jnp.arange(OUT_COLS)[None, None, :]
    scale = jnp.where(columns < HEADS * HEAD_DIM, jnp.sqrt(SEQ_SLOT / (4.0 * HEADS * HEAD_DIM)), FF ** (-0.5))
    base = jax.random.normal(key, shape, jnp.float32)
    return (base * scale).astype(jnp.bfloat16)


def draw_seq_len(key, part):
    key = jax.random.fold_in(key, 11)
    key_base, key_load, key_pick = jax.random.split(key, 3)
    base = jax.random.randint(key_base, (SEQS,), SEQ_SLOT // 2, SEQ_SLOT + 1)
    load = jax.random.randint(key_load, (SEQS // MICRO, 1), 2, 5)
    scaled = jnp.maximum(1, base.reshape(SEQS // MICRO, MICRO) * load // 4).reshape(SEQS)
    pick = jax.random.randint(key_pick, (), 0, SEQS)
    return jnp.where(jnp.arange(SEQS) == pick, SEQ_SLOT, scaled).astype(jnp.int32)


def steps_of(own_key, extent, cuts, low, top_value):
    def one(position, shards_of):
        steps = jax.random.uniform(jax.random.fold_in(jax.random.fold_in(own_key, 6), position), (shards_of,), jnp.float32, low / len(cuts), top_value / len(cuts))
        return jnp.repeat(jnp.exp(steps), extent[position] // shards_of).reshape((-1,) + (1,) * (len(extent) - position - 1))

    factor_of = one(*cuts[0])
    for cut in cuts[1:]:
        factor_of = factor_of * one(*cut)
    return factor_of


def gaussian(stream_key, dims, spread, reach, pieces=(), kind=jnp.bfloat16):
    entries = jax.random.normal(stream_key, dims, jnp.float32) * spread
    if len(pieces) > 0:
        entries = steps_of(stream_key, dims, pieces, -0.22, 0.18) * entries
    return jnp.clip(entries, min=-reach, max=reach).astype(kind)


def setup_inputs(seed: int = 0) -> dict:
    streams_of = jax.random.split(jax.random.key(seed), 6)
    return {
        "ends_in": gaussian(streams_of[0], (N_SECTION, TOKENS, D), 1.0, 6.0, ((0, 2), (1, 16))),
        "in_weight": gaussian(streams_of[1], (N_SECTION, D, IN_COLS), D ** -0.5, 0.125, ((0, 2), (1, 4))),
        "out_weight": draw_out_weight(jax.random.fold_in(streams_of[5], 71), 0),
        "norm_gain": jnp.clip(1.0 + 0.1 * jax.random.normal(streams_of[3], (N_SECTION, 2, D), jnp.float32), 0.5, 1.5),
        "seq_len": draw_seq_len(jax.random.fold_in(streams_of[5], 71), 0),
    }


@jax.custom_vjp
def low(v):
    return lax.optimization_barrier(v.astype(jnp.bfloat16)).astype(jnp.float32)

@jax.custom_vjp
def low_back(v):
    return v

def low_keep(v):
    return (low(v), None)

def low_pass(kept, grad):
    return (grad,)

def back_keep(v):
    return (v, None)

def back_low(kept, grad):
    return (low(grad),)
low.defvjp(low_keep, low_pass)
low_back.defvjp(back_keep, back_low)

def matmul(left_side, right_side):
    return jnp.dot(left_side, right_side, precision=lax.Precision.HIGHEST, preferred_element_type=jnp.float32)

def matmul_last(left_side, right_side):
    return lax.dot_general(left_side, right_side, (((1,), (1,)), ((), ())), precision=lax.Precision.HIGHEST, preferred_element_type=jnp.float32)

def rms_norm(values, gain_row):
    return values * lax.rsqrt(lax.optimization_barrier(jnp.mean(values * values, -1, keepdims=True)) + 1e-05) * gain_row

def rope_tables():
    half_dim = HEAD_DIM // 2
    inverse = 500000.0 ** (-(jnp.arange(half_dim, dtype=jnp.float32) * 2.0 / HEAD_DIM))
    angles = jnp.arange(SEQ_SLOT, dtype=jnp.float32)[:, None] * inverse[None, :]
    return (jnp.cos(angles)[None, :, None, :], jnp.sin(angles)[None, :, None, :])

def rotate(values, cosine, sine):
    half_dim = HEAD_DIM // 2
    first_half = values[..., :half_dim]
    second_half = values[..., half_dim:]
    return jnp.concatenate([first_half * cosine - second_half * sine, second_half * cosine + first_half * sine], -1)

def attend(queries, keys_rot, values_kv, lengths):
    seq_count = queries.shape[0]
    grouped = queries.reshape(seq_count, SEQ_SLOT, KV_HEADS, HEADS // KV_HEADS, HEAD_DIM)
    scores = jnp.einsum('sqkgd,spkd->skgqp', grouped, keys_rot, precision=lax.Precision.HIGHEST) * HEAD_DIM ** (-0.5)
    scores = low_back(scores)
    places = jnp.arange(SEQ_SLOT).astype(jnp.int32)
    allowed = (places[None, :, None] >= places[None, None, :]) & (places[None, None, :] < lengths[:, None, None])
    scores = jnp.where(allowed[:, None, None], scores, -1e+30)
    row_top = lax.optimization_barrier(jnp.max(scores, -1, keepdims=True))
    exp_terms = jnp.exp(scores - row_top)
    weights = exp_terms / lax.optimization_barrier(jnp.sum(exp_terms, -1, keepdims=True))
    context = jnp.einsum('skgqp,spkd->sqkgd', low(weights), values_kv, precision=lax.Precision.HIGHEST)
    return context.reshape(seq_count * SEQ_SLOT, HEADS * HEAD_DIM)

def layer(inputs, w_in, w_out, gain_pair, lengths, cosine, sine):
    q_width = HEADS * HEAD_DIM
    kv_width = KV_HEADS * HEAD_DIM
    seq_count = lengths.shape[0]
    normed = low(rms_norm(inputs, gain_pair[0]))
    projected = low_back(matmul(normed, w_in[:, :QKV_COLS]))
    queries = projected[:, :q_width].reshape(seq_count, SEQ_SLOT, HEADS, HEAD_DIM)
    keys_raw = projected[:, q_width:q_width + kv_width].reshape(seq_count, SEQ_SLOT, KV_HEADS, HEAD_DIM)
    values_raw = projected[:, q_width + kv_width:].reshape(seq_count, SEQ_SLOT, KV_HEADS, HEAD_DIM)
    queries = low(rotate(queries, cosine, sine))
    keys_rot = low(rotate(keys_raw, cosine, sine))
    values_kv = low(values_raw)
    context = low(low_back(attend(queries, keys_rot, values_kv, lengths)))
    middle = inputs + low_back(matmul_last(context, w_out[:, :q_width]))
    normed_two = low(rms_norm(middle, gain_pair[1]))
    gate_up = low_back(matmul(normed_two, w_in[:, QKV_COLS:]))
    hidden = low(jax.nn.silu(gate_up[:, :FF]) * gate_up[:, FF:])
    return middle + low_back(matmul_last(hidden, w_out[:, q_width:]))

def reference(ends_in, in_weight, out_weight, norm_gain, seq_len):
    cosine, sine = rope_tables()
    lengths = seq_len.astype(jnp.int32)
    places = jnp.arange(SEQ_SLOT).astype(jnp.int32)
    valid = (places[None, :] < lengths[:, None]).reshape(-1, 1).astype(jnp.float32)
    inputs = ends_in[0].astype(jnp.float32)
    cotangent = ends_in[1].astype(jnp.float32) * valid

    def forward(first_in, w_in_all, w_out_all, gains_all):
        between = layer(first_in, w_in_all[0], w_out_all[0], gains_all[0], lengths, cosine, sine)
        between = low(low_back(between))
        return layer(between, w_in_all[1], w_out_all[1], gains_all[1], lengths, cosine, sine)
    result, pullback = jax.vjp(forward, inputs, in_weight.astype(jnp.float32), out_weight.astype(jnp.float32), norm_gain.astype(jnp.float32))
    grad_x, grad_in, grad_out, grad_gain = pullback(cotangent)
    ends_out = jnp.stack([grad_x.astype(jnp.bfloat16), result.astype(jnp.bfloat16)])
    return (ends_out, grad_in, grad_out, grad_gain)
```

```python
import functools

import jax
import jax.numpy as jnp
from jax import lax
from jax.experimental import pallas as pl
from jax.experimental.pallas import tpu as pltpu
from jax.sharding import PartitionSpec as P

HEADS = 32
KV_HEADS = 8
GROUP = HEADS // KV_HEADS
HEAD_DIM = 64
FF = 8192
EPSILON = 1e-05
BF16 = jnp.bfloat16
F32 = jnp.float32
CORES = 2
LINE = KV_HEADS // CORES
Q_SLAB = GROUP * HEAD_DIM
QKV_SLAB = Q_SLAB + 2 * HEAD_DIM
FF_SLAB = FF // KV_HEADS
Q_COLS = HEADS * HEAD_DIM
KV_COLS = KV_HEADS * HEAD_DIM


def line_place():
    core = lax.axis_index("section")
    depth = lax.axis_index("dp")
    return core, depth, lax.rem(depth, LINE)


def greet(core, depth, place):
    barrier = pltpu.get_barrier_semaphore()
    pl.semaphore_signal(barrier, inc=1, device_id={"section": 1 - core})

    @pl.when(place < LINE - 1)
    def _():
        pl.semaphore_signal(barrier, inc=1, device_id={"dp": depth + 1})

    @pl.when(place > 0)
    def _():
        pl.semaphore_signal(barrier, inc=1, device_id={"dp": depth - 1})

    both = jnp.where((place > 0) & (place < LINE - 1), 3, 2)
    pl.semaphore_wait(barrier, both)


def gather_body(x_ref, o_ref, up_send, dn_send, sib_send, z_recv, sib_recv):
    core, depth, place = line_place()
    greet(core, depth, place)
    own = place * CORES + core
    o_ref[own] = x_ref[...]

    def up(where):
        index = where * CORES + core
        return pltpu.make_async_remote_copy(
            o_ref.at[index], o_ref.at[index], up_send.at[where], z_recv.at[where],
            device_id={"dp": depth + 1},
        )

    def down(where):
        index = where * CORES + core
        return pltpu.make_async_remote_copy(
            o_ref.at[index], o_ref.at[index], dn_send.at[where], z_recv.at[where],
            device_id={"dp": depth - 1},
        )

    def across(where):
        index = where * CORES + core
        return pltpu.make_async_remote_copy(
            o_ref.at[index], o_ref.at[index], sib_send.at[where], sib_recv.at[where],
            device_id={"section": 1 - core},
        )

    def arrived(where, other):
        index = where * CORES + other
        sem = z_recv if other is core else sib_recv
        return pltpu.make_async_remote_copy(
            o_ref.at[index], o_ref.at[index], up_send.at[where], sem.at[where],
            device_id={"section": 1 - core},
        )

    @pl.when(place < LINE - 1)
    def _():
        up(place).start()

    @pl.when(place > 0)
    def _():
        down(place).start()

    across(place).start()
    for step in range(1, LINE):
        @pl.when(place >= step)
        def _():
            arrived(place - step, core).wait_recv()

            @pl.when(place < LINE - 1)
            def _():
                up(place - step).start()

            across(place - step).start()

        @pl.when(place + step < LINE)
        def _():
            arrived(place + step, core).wait_recv()

            @pl.when(place > 0)
            def _():
                down(place + step).start()

            across(place + step).start()

    for where in range(LINE):
        arrived(where, 1 - core).wait_recv()
        across(where).wait_send()

        @pl.when((where <= place) & (place < LINE - 1))
        def _():
            up(where).wait_send()

        @pl.when((where >= place) & (place > 0))
        def _():
            down(where).wait_send()


def gather_line(block):
    rows, width = block.shape
    blocks = LINE * CORES
    sems = pltpu.SemaphoreType.DMA((LINE,))
    out = pl.pallas_call(
        gather_body,
        out_shape=jax.ShapeDtypeStruct((blocks, rows, width), block.dtype),
        in_specs=[pl.BlockSpec(memory_space=pltpu.VMEM)],
        out_specs=pl.BlockSpec(memory_space=pltpu.VMEM),
        scratch_shapes=[sems] * 5,
        compiler_params=pltpu.CompilerParams(
            collective_id=0, has_side_effects=True, vmem_limit_bytes=16 * 2**20
        ),
        name="gather_line",
        cost_estimate=pl.CostEstimate(flops=0, bytes_accessed=60_000_000, transcendentals=0),
    )(block)
    return out.reshape(blocks * rows, width)


def scatter_body(p_ref, o_ref, sib_buf, rx_up, rx_dn, tx_up, tx_dn,
                 sib_send, sib_recv, up_send, up_recv, dn_send, dn_recv):
    core, depth, place = line_place()
    greet(core, depth, place)

    def across(where):
        return pltpu.make_async_remote_copy(
            p_ref.at[where * CORES + 1 - core], sib_buf.at[where],
            sib_send.at[where], sib_recv.at[where], device_id={"section": 1 - core},
        )

    def up(where):
        return pltpu.make_async_remote_copy(
            tx_up.at[where], rx_up.at[where], up_send.at[where], up_recv.at[where],
            device_id={"dp": depth + 1},
        )

    def down(where):
        return pltpu.make_async_remote_copy(
            tx_dn.at[where], rx_dn.at[where], dn_send.at[where], dn_recv.at[where],
            device_id={"dp": depth - 1},
        )

    def summed(where):
        return p_ref[where * CORES + core].astype(F32) + sib_buf[where].astype(F32)

    for step in range(LINE - 1, 0, -1):
        @pl.when(place + step < LINE)
        def _():
            across(place + step).start()

        @pl.when(place >= step)
        def _():
            across(place - step).start()

    across(place).start()
    for step in range(LINE - 1, 0, -1):
        @pl.when(place + step < LINE)
        def _():
            where = place + step
            across(where).wait_recv()

            @pl.when(place > 0)
            def _():
                up(where).wait_recv()
                tx_up[where] = (summed(where) + rx_up[where].astype(F32)).astype(BF16)

            @pl.when(place == 0)
            def _():
                tx_up[where] = summed(where).astype(BF16)

            up(where).start()

        @pl.when(place >= step)
        def _():
            where = place - step
            across(where).wait_recv()

            @pl.when(place < LINE - 1)
            def _():
                down(where).wait_recv()
                tx_dn[where] = (summed(where) + rx_dn[where].astype(F32)).astype(BF16)

            @pl.when(place == LINE - 1)
            def _():
                tx_dn[where] = summed(where).astype(BF16)

            down(where).start()

    across(place).wait_recv()
    o_ref[...] = summed(place)

    @pl.when(place > 0)
    def _():
        up(place).wait_recv()
        o_ref[...] += rx_up[place].astype(F32)

    @pl.when(place < LINE - 1)
    def _():
        down(place).wait_recv()
        o_ref[...] += rx_dn[place].astype(F32)

    for where in range(LINE):
        across(where).wait_send()

        @pl.when(where > place)
        def _():
            up(where).wait_send()

        @pl.when(where < place)
        def _():
            down(where).wait_send()


def scatter_line(partial):
    blocks = LINE * CORES
    rows = partial.shape[0] // blocks
    width = partial.shape[1]
    sems = pltpu.SemaphoreType.DMA((LINE,))
    buffer = pltpu.VMEM((LINE, rows, width), BF16)
    return pl.pallas_call(
        scatter_body,
        out_shape=jax.ShapeDtypeStruct((rows, width), F32),
        in_specs=[pl.BlockSpec(memory_space=pltpu.VMEM)],
        out_specs=pl.BlockSpec(memory_space=pltpu.VMEM),
        scratch_shapes=[buffer] * 5 + [sems] * 6,
        compiler_params=pltpu.CompilerParams(
            collective_id=1, has_side_effects=True, vmem_limit_bytes=24 * 2**20
        ),
        name="scatter_line",
        cost_estimate=pl.CostEstimate(flops=0, bytes_accessed=60_000_000, transcendentals=0),
    )(partial.reshape(blocks, rows, width))


def swap_cores(value):
    return lax.ppermute(value, "section", [(0, 1), (1, 0)])


def hop(value, bit):
    peers = lax.axis_size("shard")
    return lax.ppermute(value, "shard", [(i, i ^ bit) for i in range(peers)])


def gather_rows(block):
    half = block.shape[0] // 2
    one = hop(block, 1)
    two = hop(block, 2)
    top = hop(two[:half], 1)
    bottom = hop(one[half:], 2)
    return jnp.concatenate([block, one, two, top, bottom], 0)


def reduce_rows(term):
    far = term(3)
    half = far.shape[0] // 2
    via_one = hop(far[:half], 1).astype(F32)
    via_two = hop(far[half:], 2).astype(F32)
    first = term(1).astype(F32)
    one = hop(jnp.concatenate([first[:half], first[half:] + via_two], 0).astype(BF16), 1)
    second = term(2).astype(F32)
    two = hop(jnp.concatenate([second[:half] + via_one, second[half:]], 0).astype(BF16), 2)
    return (term(0).astype(F32) + one.astype(F32) + two.astype(F32)).astype(BF16)


def relative(values, shard):
    blocks = jnp.split(values, 4, -1)
    odd = (shard & 1) == 1
    high = (shard & 2) == 2
    blocks = [jnp.where(odd, blocks[i ^ 1], blocks[i]) for i in range(4)]
    blocks = [jnp.where(high, blocks[i ^ 2], blocks[i]) for i in range(4)]
    return jnp.concatenate(blocks, -1)


def rope_tables(rows):
    half_dim = HEAD_DIM // 2
    inverse = 500000.0 ** (-(jnp.arange(half_dim, dtype=F32) * 2.0 / HEAD_DIM))
    angles = jnp.arange(rows, dtype=F32)[:, None] * inverse[None, :]
    return (jnp.cos(angles)[None, :, None, :], jnp.sin(angles)[None, :, None, :])


def rotate(values, cosine, sine):
    a, b = jnp.split(values, 2, -1)
    return jnp.concatenate([a * cosine - b * sine, b * cosine + a * sine], -1)


def unrotate(grads, cosine, sine):
    a, b = jnp.split(grads, 2, -1)
    return jnp.concatenate([a * cosine + b * sine, b * cosine - a * sine], -1)


def rms_scale(values):
    return lax.rsqrt(jnp.mean(values * values, -1, keepdims=True) + EPSILON)


def rms_back(values, scale, gain_row, grad_norm):
    grad_hat = grad_norm * gain_row
    grad_gain = jnp.sum(grad_norm * values * scale, 0)
    inner = jnp.mean(grad_hat * values, -1, keepdims=True)
    return (scale * grad_hat - values * scale * scale * scale * inner, grad_gain)


def mm(a, b):
    return jnp.dot(a, b, preferred_element_type=F32)


def mm_last(a, b):
    return lax.dot_general(a, b, (((1,), (1,)), ((), ())), preferred_element_type=F32)


def mm_rows(a, b):
    return lax.dot_general(a, b, (((0,), (0,)), ((), ())), preferred_element_type=F32)


def masked_scores(queries, keys, lengths):
    rows = queries.shape[1]
    places = jnp.arange(rows)
    allowed = (places[:, None] >= places[None, :])[None] & (
        places[None, None, :] < lengths[:, None, None]
    )
    scores = jnp.einsum("sqgd,spd->sgqp", queries, keys, preferred_element_type=F32)
    return jnp.where(allowed[:, None], scores * HEAD_DIM**-0.5, -1e30)


def forward_layer(x, weights, gains, lengths, tables):
    w_qkv, w_attn, w_gu, w_down = weights
    slots = lengths.shape[0]
    rows = x.shape[0]
    scale_one = rms_scale(x)
    normed = gather_line((x * scale_one * gains[0]).astype(BF16))
    projected = mm(normed, w_qkv)
    queries = rotate(projected[:, :Q_SLAB].reshape(slots, rows, GROUP, HEAD_DIM), *tables).astype(BF16)
    keys = rotate(
        projected[:, Q_SLAB:Q_SLAB + HEAD_DIM].reshape(slots, rows, 1, HEAD_DIM), *tables
    ).astype(BF16)[:, :, 0]
    values = projected[:, Q_SLAB + HEAD_DIM:].reshape(slots, rows, HEAD_DIM).astype(BF16)
    scores = masked_scores(queries, keys, lengths)
    top = jnp.max(scores, -1, keepdims=True)
    terms = jnp.exp(scores - top)
    total = jnp.sum(terms, -1, keepdims=True)
    log_total = top + jnp.log(total)
    probs = (terms / total).astype(BF16)
    context = jnp.einsum("sgqp,spd->sqgd", probs, values, preferred_element_type=F32)
    context = context.reshape(slots * rows, Q_SLAB).astype(BF16)
    middle = x + scatter_line(mm_last(context, w_attn).astype(BF16))
    scale_two = rms_scale(middle)
    normed_two = gather_line((middle * scale_two * gains[1]).astype(BF16))
    gate_up = mm(normed_two, w_gu)
    gate, up = gate_up[:, :FF_SLAB], gate_up[:, FF_SLAB:]
    hidden = (jax.nn.silu(gate) * up).astype(BF16)
    output = middle + scatter_line(mm_last(hidden, w_down).astype(BF16))
    return output, (x, scale_one, normed, queries, keys, values, log_total, context,
                    middle, scale_two, normed_two, gate, up, hidden)


def backward_layer(kept, grad_out, weights, gains, lengths, tables):
    (x, scale_one, normed, queries, keys, values, log_total, context,
     middle, scale_two, normed_two, gate, up, hidden) = kept
    w_qkv, w_attn, w_gu, w_down = weights
    slots = lengths.shape[0]
    rows = x.shape[0]
    grad_mlp = gather_line(grad_out.astype(BF16))
    grad_hidden = mm(grad_mlp, w_down)
    sig = jax.nn.sigmoid(gate)
    grad_gate = grad_hidden * up * sig * (1.0 + gate * (1.0 - sig))
    grad_up = grad_hidden * gate * sig
    grad_gu = jnp.concatenate([grad_gate, grad_up], 1).astype(BF16)
    grad_normed = scatter_line(mm_last(grad_gu, w_gu).astype(BF16))
    back, gain_two = rms_back(middle, scale_two, gains[1], grad_normed)
    grad_mid = grad_out + back
    grad_attn = gather_line(grad_mid.astype(BF16))
    grad_context = mm(grad_attn, w_attn).astype(BF16).reshape(slots, rows, GROUP, HEAD_DIM)
    probs = jnp.exp(masked_scores(queries, keys, lengths) - log_total)
    grad_values = jnp.einsum("sgqp,sqgd->spd", probs.astype(BF16), grad_context, preferred_element_type=F32)
    grad_probs = jnp.einsum("sqgd,spd->sgqp", grad_context, values, preferred_element_type=F32)
    inner = jnp.sum(grad_probs * probs, -1, keepdims=True)
    grad_scores = (probs * (grad_probs - inner)).astype(BF16)
    grad_queries = jnp.einsum("sgqp,spd->sqgd", grad_scores, keys, preferred_element_type=F32)
    grad_keys = jnp.einsum("sgqp,sqgd->spd", grad_scores, queries, preferred_element_type=F32)
    grad_queries = unrotate(grad_queries * HEAD_DIM**-0.5, *tables)
    grad_keys = unrotate(grad_keys[:, :, None] * HEAD_DIM**-0.5, *tables)
    grad_proj = jnp.concatenate(
        [
            grad_queries.reshape(slots * rows, Q_SLAB),
            grad_keys.reshape(slots * rows, HEAD_DIM),
            grad_values.reshape(slots * rows, HEAD_DIM),
        ],
        1,
    ).astype(BF16)
    grad_normed = scatter_line(mm_last(grad_proj, w_qkv).astype(BF16))
    back, gain_one = rms_back(x, scale_one, gains[0], grad_normed)
    mlp = ((normed_two, grad_gu), (grad_mlp, hidden))
    attn = ((normed, grad_proj), (grad_attn, context))
    return grad_mid + back, mlp, attn, jnp.stack([gain_one, gain_two])


def slab(weight, start, size):
    return lax.dynamic_slice_in_dim(weight, start, size, 1)


def attn_slab(w_in, w_out, head):
    return jnp.concatenate(
        [
            slab(w_in, head * Q_SLAB, Q_SLAB),
            slab(w_in, Q_COLS + head * HEAD_DIM, HEAD_DIM),
            slab(w_in, Q_COLS + KV_COLS + head * HEAD_DIM, HEAD_DIM),
            slab(w_out, head * Q_SLAB, Q_SLAB),
        ],
        1,
    )


def mlp_slab(w_in, w_out, head):
    base = Q_COLS + 2 * KV_COLS
    return jnp.concatenate(
        [
            slab(w_in, base + head * FF_SLAB, FF_SLAB),
            slab(w_in, base + FF + head * FF_SLAB, FF_SLAB),
            slab(w_out, Q_COLS + head * FF_SLAB, FF_SLAB),
        ],
        1,
    )


def line_pairs(shift):
    peers = lax.axis_size("dp")
    return [(i, i // LINE * LINE + (i % LINE + shift) % LINE) for i in range(peers)]


def line_exchange(blocks, place):
    got = [lax.dynamic_index_in_dim(blocks, place, 0, False)]
    for shift in range(1, LINE):
        to = lax.rem(place + shift, LINE)
        got.append(lax.ppermute(lax.dynamic_index_in_dim(blocks, to, 0, False), "dp", line_pairs(shift)))
    return got


def local(ends_in, in_weight, out_weight, norm_gain, seq_len):
    core = lax.axis_index("section")
    shard = lax.axis_index("shard")
    depth = lax.axis_index("dp")
    place = lax.rem(depth, LINE)
    first = core == 0
    replicas = lax.axis_size("dp") // LINE
    w_in, w_out = in_weight[0], out_weight[0]
    head = place * CORES + core
    sibling = place * CORES + 1 - core
    rows = ends_in.shape[1] // CORES

    def by_layer(mine, others):
        return jnp.where(first, mine, others), jnp.where(first, others, mine)

    attn = by_layer(attn_slab(w_in, w_out, head), swap_cores(attn_slab(w_in, w_out, sibling)))
    mlp = by_layer(mlp_slab(w_in, w_out, head), swap_cores(mlp_slab(w_in, w_out, sibling)))

    def layer_weights(index):
        a = gather_rows(attn[index])
        m = gather_rows(mlp[index])
        return (a[:, :QKV_SLAB], a[:, QKV_SLAB:], m[:, :2 * FF_SLAB], m[:, 2 * FF_SLAB:])

    weights = [layer_weights(0), layer_weights(1)]
    own_gain = relative(norm_gain[0], shard)
    gains = by_layer(own_gain, swap_cores(own_gain))
    ends = relative(ends_in[0], shard)
    mine, others = ends[:rows], ends[rows:]
    crossed = swap_cores(jnp.where(first, others, mine))
    x = jnp.where(first, mine, crossed).astype(F32)
    cot = jnp.where(first, crossed, others).astype(F32)
    line_groups = [
        [r * LINE + p for p in range(LINE)] for r in range(replicas)
    ]
    lengths = lax.all_gather(seq_len, "dp", tiled=True, axis_index_groups=line_groups if replicas > 1 else None)
    own_length = jnp.where(first, seq_len[0], seq_len[1])
    valid = (jnp.arange(rows) < own_length).astype(F32)[:, None]
    tables = rope_tables(rows)

    y0, kept0 = forward_layer(x, weights[0], gains[0], lengths, tables)
    y1, kept1 = forward_layer(y0.astype(BF16).astype(F32), weights[1], gains[1], lengths, tables)
    dx1, mlp1, attn1, gain1 = backward_layer(kept1, cot * valid, weights[1], gains[1], lengths, tables)
    dx0, mlp0, attn0, gain0 = backward_layer(
        kept0, dx1.astype(BF16).astype(F32), weights[0], gains[0], lengths, tables
    )

    def reduced(pairs):
        (in_rows, in_cols), (out_rows, out_cols) = pairs

        def term(k):
            part = slice(k * in_rows.shape[1] // 4, (k + 1) * in_rows.shape[1] // 4)
            return jnp.concatenate(
                [mm_rows(in_rows[:, part], in_cols), mm_rows(out_rows[:, part], out_cols)], 1
            ).astype(BF16)

        total = reduce_rows(term)
        if replicas > 1:
            groups = [[r * LINE + p for r in range(replicas)] for p in range(LINE)]
            total = lax.psum_scatter(total, "dp", scatter_dimension=0, tiled=True, axis_index_groups=groups)
        blocks = total.reshape(LINE, total.shape[0] // LINE, total.shape[1])
        got = line_exchange(blocks, place)
        order = [lax.rem(place - shift + LINE, LINE) for shift in range(LINE)]
        return got

    grads = []
    for pairs in ((mlp1, attn1), (mlp0, attn0)):
        grads.append([jnp.stack(reduced(part)) for part in pairs])
    (m1, a1), (m0, a0) = grads

    def place_order(pieces):
        index = jnp.array([0], jnp.int32)
        index = jnp.remainder(place - jnp.arange(LINE), LINE)
        return jnp.take(pieces, index, axis=0)

    def to_layer_core(zero, one):
        zero, one = place_order(zero), place_order(one)
        mine = jnp.where(first, zero, one)
        others = swap_cores(jnp.where(first, one, zero))
        both = jnp.stack([jnp.where(first, mine, others), jnp.where(first, others, mine)], 1)
        return both.reshape(KV_HEADS, both.shape[2], both.shape[3]).astype(F32)

    grad_attn = to_layer_core(a0, a1)
    grad_mlp = to_layer_core(m0, m1)

    def columns(values, lo, hi):
        part = values[:, :, lo:hi].transpose(1, 0, 2)
        return part.reshape(part.shape[0], -1)

    in_grad = jnp.concatenate(
        [
            columns(grad_attn, 0, Q_SLAB),
            columns(grad_attn, Q_SLAB, Q_SLAB + HEAD_DIM),
            columns(grad_attn, Q_SLAB + HEAD_DIM, QKV_SLAB),
            columns(grad_mlp, 0, FF_SLAB),
            columns(grad_mlp, FF_SLAB, 2 * FF_SLAB),
        ],
        1,
    )
    out_grad = jnp.concatenate(
        [columns(grad_attn, QKV_SLAB, QKV_SLAB + Q_SLAB), columns(grad_mlp, 2 * FF_SLAB, 3 * FF_SLAB)], 1
    )
    own_gains = jnp.where(first, gain0, gain1) + swap_cores(jnp.where(first, gain1, gain0))
    gain_rows = lax.psum_scatter(relative(own_gains, shard), ("shard", "dp"), scatter_dimension=1, tiled=True)
    dx0, y1 = dx0.astype(BF16), y1.astype(BF16)
    crossed = swap_cores(jnp.where(first, y1, dx0))
    ends_mine = jnp.where(first, dx0, crossed)
    ends_others = jnp.where(first, crossed, y1)
    ends_out = relative(jnp.concatenate([ends_mine, ends_others], 0), shard)
    return ends_out[None], in_grad[None], out_grad[None], gain_rows[None]


def solution(mesh):
    in_specs = (
        P("section", ("shard", "dp"), None),
        P("section", "shard", None),
        P("section", "shard", None),
        P("section", None, None),
        P(("shard", "dp")),
    )
    out_specs = (
        P("section", ("shard", "dp"), None),
        P("section", ("shard", "dp"), None),
        P("section", ("shard", "dp"), None),
        P("section", None, ("shard", "dp")),
    )
    return jax.shard_map(local, mesh=mesh, in_specs=in_specs, out_specs=out_specs, check_vma=False)
```

```python
import functools

import jax
import jax.numpy as jnp
from jax import lax
from jax.experimental import pallas as pl
from jax.experimental.pallas import tpu as pltpu
from jax.sharding import PartitionSpec as P

HEADS = 32
KV_HEADS = 8
GROUP = HEADS // KV_HEADS
HEAD_DIM = 64
FF = 8192
EPSILON = 1e-05
BF16 = jnp.bfloat16
F32 = jnp.float32
CORES = 2
LINE = KV_HEADS // CORES
SHARDS = 4
SLOT = 64
Q_SLAB = GROUP * HEAD_DIM
QKV_SLAB = Q_SLAB + 2 * HEAD_DIM
FF_SLAB = FF // KV_HEADS
Q_COLS = HEADS * HEAD_DIM
KV_COLS = KV_HEADS * HEAD_DIM


def line_place():
    core = lax.axis_index("section")
    depth = lax.axis_index("dp")
    return core, depth, lax.rem(depth, LINE)


def greet(core, depth, place):
    barrier = pltpu.get_barrier_semaphore()
    pl.semaphore_signal(barrier, inc=1, device_id={"section": 1 - core})

    @pl.when(place < LINE - 1)
    def _():
        pl.semaphore_signal(barrier, inc=1, device_id={"dp": depth + 1})

    @pl.when(place > 0)
    def _():
        pl.semaphore_signal(barrier, inc=1, device_id={"dp": depth - 1})

    both = jnp.where((place > 0) & (place < LINE - 1), 3, 2)
    pl.semaphore_wait(barrier, both)


def gather_body(x_ref, o_ref, up_send, dn_send, sib_send, z_recv, sib_recv):
    core, depth, place = line_place()
    greet(core, depth, place)
    own = core * LINE + place
    o_ref[own] = x_ref[...]

    def up(where):
        index = core * LINE + where
        return pltpu.make_async_remote_copy(
            o_ref.at[index], o_ref.at[index], up_send.at[where], z_recv.at[where],
            device_id={"dp": depth + 1},
        )

    def down(where):
        index = core * LINE + where
        return pltpu.make_async_remote_copy(
            o_ref.at[index], o_ref.at[index], dn_send.at[where], z_recv.at[where],
            device_id={"dp": depth - 1},
        )

    def across(where):
        index = core * LINE + where
        return pltpu.make_async_remote_copy(
            o_ref.at[index], o_ref.at[index], sib_send.at[where], sib_recv.at[where],
            device_id={"section": 1 - core},
        )

    def arrived(where, other):
        index = other * LINE + where
        sem = z_recv if other is core else sib_recv
        return pltpu.make_async_remote_copy(
            o_ref.at[index], o_ref.at[index], up_send.at[where], sem.at[where],
            device_id={"section": 1 - core},
        )

    @pl.when(place < LINE - 1)
    def _():
        up(place).start()

    @pl.when(place > 0)
    def _():
        down(place).start()

    across(place).start()
    for step in range(1, LINE):
        @pl.when(place >= step)
        def _():
            arrived(place - step, core).wait_recv()

            @pl.when(place < LINE - 1)
            def _():
                up(place - step).start()

            across(place - step).start()

        @pl.when(place + step < LINE)
        def _():
            arrived(place + step, core).wait_recv()

            @pl.when(place > 0)
            def _():
                down(place + step).start()

            across(place + step).start()

    for where in range(LINE):
        arrived(where, 1 - core).wait_recv()
        across(where).wait_send()

        @pl.when((where <= place) & (place < LINE - 1))
        def _():
            up(where).wait_send()

        @pl.when((where >= place) & (place > 0))
        def _():
            down(where).wait_send()


def gather_line(block):
    rows, width = block.shape
    blocks = LINE * CORES
    sems = pltpu.SemaphoreType.DMA((LINE,))
    out = pl.pallas_call(
        gather_body,
        out_shape=jax.ShapeDtypeStruct((blocks, rows, width), block.dtype),
        in_specs=[pl.BlockSpec(memory_space=pltpu.VMEM)],
        out_specs=pl.BlockSpec(memory_space=pltpu.VMEM),
        scratch_shapes=[sems] * 5,
        compiler_params=pltpu.CompilerParams(
            collective_id=1, has_side_effects=True, vmem_limit_bytes=16 * 2**20
        ),
        name="gather_line",
        cost_estimate=pl.CostEstimate(flops=0, bytes_accessed=60_000_000, transcendentals=0),
    )(block)
    return out.reshape(blocks * rows, width)


def scatter_body(p_ref, o_ref, sib_buf, rx_up, rx_dn, tx_up, tx_dn,
                 sib_send, sib_recv, up_send, up_recv, dn_send, dn_recv):
    core, depth, place = line_place()
    greet(core, depth, place)

    def across(where):
        return pltpu.make_async_remote_copy(
            p_ref.at[(1 - core) * LINE + where], sib_buf.at[where],
            sib_send.at[where], sib_recv.at[where], device_id={"section": 1 - core},
        )

    def up(where):
        return pltpu.make_async_remote_copy(
            tx_up.at[where], rx_up.at[where], up_send.at[where], up_recv.at[where],
            device_id={"dp": depth + 1},
        )

    def down(where):
        return pltpu.make_async_remote_copy(
            tx_dn.at[where], rx_dn.at[where], dn_send.at[where], dn_recv.at[where],
            device_id={"dp": depth - 1},
        )

    def summed(where):
        return p_ref[core * LINE + where].astype(F32) + sib_buf[where].astype(F32)

    for step in range(LINE - 1, 0, -1):
        @pl.when(place + step < LINE)
        def _():
            across(place + step).start()

        @pl.when(place >= step)
        def _():
            across(place - step).start()

    across(place).start()
    for step in range(LINE - 1, 0, -1):
        @pl.when(place + step < LINE)
        def _():
            where = place + step
            across(where).wait_recv()

            @pl.when(place > 0)
            def _():
                up(where).wait_recv()
                tx_up[where] = (summed(where) + rx_up[where].astype(F32)).astype(BF16)

            @pl.when(place == 0)
            def _():
                tx_up[where] = summed(where).astype(BF16)

            up(where).start()

        @pl.when(place >= step)
        def _():
            where = place - step
            across(where).wait_recv()

            @pl.when(place < LINE - 1)
            def _():
                down(where).wait_recv()
                tx_dn[where] = (summed(where) + rx_dn[where].astype(F32)).astype(BF16)

            @pl.when(place == LINE - 1)
            def _():
                tx_dn[where] = summed(where).astype(BF16)

            down(where).start()

    across(place).wait_recv()
    o_ref[...] = summed(place)

    @pl.when(place > 0)
    def _():
        up(place).wait_recv()
        o_ref[...] += rx_up[place].astype(F32)

    @pl.when(place < LINE - 1)
    def _():
        down(place).wait_recv()
        o_ref[...] += rx_dn[place].astype(F32)

    for where in range(LINE):
        across(where).wait_send()

        @pl.when(where > place)
        def _():
            up(where).wait_send()

        @pl.when(where < place)
        def _():
            down(where).wait_send()


def scatter_line(partial):
    blocks = LINE * CORES
    rows = partial.shape[0] // blocks
    width = partial.shape[1]
    sems = pltpu.SemaphoreType.DMA((LINE,))
    buffer = pltpu.VMEM((LINE, rows, width), BF16)
    return pl.pallas_call(
        scatter_body,
        out_shape=jax.ShapeDtypeStruct((rows, width), F32),
        in_specs=[pl.BlockSpec(memory_space=pltpu.VMEM)],
        out_specs=pl.BlockSpec(memory_space=pltpu.VMEM),
        scratch_shapes=[buffer] * 5 + [sems] * 6,
        compiler_params=pltpu.CompilerParams(
            collective_id=2, has_side_effects=True, vmem_limit_bytes=24 * 2**20
        ),
        name="scatter_line",
        cost_estimate=pl.CostEstimate(flops=0, bytes_accessed=60_000_000, transcendentals=0),
    )(partial.reshape(blocks, rows, width))


class Here:
    def __init__(self):
        self.core = lax.axis_index("section")
        self.shard = lax.axis_index("shard")
        self.depth = lax.axis_index("dp")
        self.place = lax.rem(self.depth, LINE)
        self.twin = {"section": 1 - self.core}
        self.x_shard = self.shard + 1 - 2 * lax.rem(self.shard, 2)
        self.y_shard = lax.rem(self.shard + 2, SHARDS)
        self.far_shard = SHARDS - 1 - self.shard
        self.x_peer = {"shard": self.x_shard}
        self.y_peer = {"shard": self.y_shard}
        self.above = {"dp": self.depth + 1}
        self.below = {"dp": self.depth - 1}
        self.has_above = self.place < LINE - 1
        self.has_below = self.place > 0

    def greet(self):
        barrier = pltpu.get_barrier_semaphore()
        for peer in (self.twin, self.x_peer, self.y_peer):
            pl.semaphore_signal(barrier, inc=1, device_id=peer)

        @pl.when(self.has_above)
        def _():
            pl.semaphore_signal(barrier, inc=1, device_id=self.above)

        @pl.when(self.has_below)
        def _():
            pl.semaphore_signal(barrier, inc=1, device_id=self.below)

        pl.semaphore_wait(barrier, jnp.where(self.has_above & self.has_below, 5, 4))


def remote(src, dst, send, recv, device):
    return pltpu.make_async_remote_copy(src, dst, send, recv, device_id=device)


def rows_at(ref, start, size):
    return ref.at[pl.ds(pl.multiple_of(start, size), size)]


def line_gather(here, buf, sems, meanwhile=()):
    up_send, dn_send, sib_send, z_recv, sib_recv = sems
    rows = buf.shape[0] // (LINE * CORES)
    core, place = here.core, here.place
    meanwhile = list(meanwhile) + [None] * LINE

    def part(where, whose):
        return rows_at(buf, (whose * LINE + where) * rows, rows)

    def up(where):
        mine = part(where, core)
        return remote(mine, mine, up_send.at[where], z_recv.at[where], here.above)

    def down(where):
        mine = part(where, core)
        return remote(mine, mine, dn_send.at[where], z_recv.at[where], here.below)

    def across(where, whose):
        mine = part(where, whose)
        return remote(mine, mine, sib_send.at[where], sib_recv.at[where], here.twin)

    @pl.when(here.has_above)
    def _():
        up(place).start()

    @pl.when(here.has_below)
    def _():
        down(place).start()

    across(place, core).start()
    for step in range(1, LINE):
        if meanwhile[step - 1] is not None:
            meanwhile[step - 1]()

        @pl.when(place >= step)
        def _():
            up(place - step).wait_recv()

            @pl.when(here.has_above)
            def _():
                up(place - step).start()

            across(place - step, core).start()

        @pl.when(place + step < LINE)
        def _():
            down(place + step).wait_recv()

            @pl.when(here.has_below)
            def _():
                down(place + step).start()

            across(place + step, core).start()

    if meanwhile[LINE - 1] is not None:
        meanwhile[LINE - 1]()
    for where in range(LINE):
        across(where, 1 - core).wait_recv()
        across(where, core).wait_send()

        @pl.when((where <= place) & here.has_above)
        def _():
            up(where).wait_send()

        @pl.when((where >= place) & here.has_below)
        def _():
            down(where).wait_send()


def line_reduce(here, out, ours, theirs, bufs, sems, own_terms=None, meanwhile=()):
    sib_buf, rx_up, rx_dn, tx_up, tx_dn = bufs
    sib_send, sib_recv, up_send, up_recv, dn_send, dn_recv = sems
    rows = out.shape[0]
    place = here.place
    meanwhile = list(meanwhile) + [None] * LINE

    def part(ref, where):
        return rows_at(ref, where * rows, rows)

    def read(ref, where):
        return ref[pl.ds(pl.multiple_of(where * rows, rows), rows), :].astype(F32)

    def across(where):
        return remote(part(theirs, where), part(sib_buf, where), sib_send.at[where], sib_recv.at[where], here.twin)

    def up(where):
        return remote(part(tx_up, where), part(rx_up, where), up_send.at[where], up_recv.at[where], here.above)

    def down(where):
        return remote(part(tx_dn, where), part(rx_dn, where), dn_send.at[where], dn_recv.at[where], here.below)

    def summed(where):
        return read(ours, where) + read(sib_buf, where)

    def put(ref, where, value):
        ref[pl.ds(pl.multiple_of(where * rows, rows), rows), :] = value.astype(BF16)

    for step in range(LINE - 1, 0, -1):
        @pl.when(place + step < LINE)
        def _():
            across(place + step).start()

        @pl.when(place >= step)
        def _():
            across(place - step).start()

    across(place).start()
    if own_terms is not None:
        own_terms()
    for step in range(LINE - 1, 0, -1):
        @pl.when(place + step < LINE)
        def _():
            where = place + step
            across(where).wait_recv()

            @pl.when(here.has_below)
            def _():
                up(where).wait_recv()
                put(tx_up, where, summed(where) + read(rx_up, where))

            @pl.when(place == 0)
            def _():
                put(tx_up, where, summed(where))

            up(where).start()

        @pl.when(place >= step)
        def _():
            where = place - step
            across(where).wait_recv()

            @pl.when(here.has_above)
            def _():
                down(where).wait_recv()
                put(tx_dn, where, summed(where) + read(rx_dn, where))

            @pl.when(place == LINE - 1)
            def _():
                put(tx_dn, where, summed(where))

            down(where).start()

        if meanwhile[LINE - 1 - step] is not None:
            meanwhile[LINE - 1 - step]()

    across(place).wait_recv()
    out[...] = summed(place)

    @pl.when(here.has_below)
    def _():
        up(place).wait_recv()
        out[...] += read(rx_up, place)

    @pl.when(here.has_above)
    def _():
        down(place).wait_recv()
        out[...] += read(rx_dn, place)

    for where in range(LINE):
        across(where).wait_send()

        @pl.when(where > place)
        def _():
            up(where).wait_send()

        @pl.when(where < place)
        def _():
            down(where).wait_send()


def dot(a, b):
    return jnp.dot(a, b, preferred_element_type=F32)


def dot_last(a, b):
    return lax.dot_general(a, b, (((1,), (1,)), ((), ())), preferred_element_type=F32)


def dot_rows(a, b):
    return lax.dot_general(a, b, (((0,), (0,)), ((), ())), preferred_element_type=F32)


def low_lanes(shape, size=HEAD_DIM):
    return lax.rem(lax.broadcasted_iota(jnp.int32, shape, 1), 2 * size) < size


def turn(block, cosine, sine):
    half = HEAD_DIM // 2
    other = jnp.where(low_lanes(block.shape, half), pltpu.roll(block, 128 - half, 1), pltpu.roll(block, half, 1))
    return block * cosine + other * sine


def spread_heads(wide):
    low = low_lanes((wide.shape[0], 128))
    parts = []
    for pair in range(GROUP // 2):
        block = wide[:, pair * 128:(pair + 1) * 128]
        parts.append(jnp.where(low, block, 0.0))
        parts.append(jnp.where(low, pltpu.roll(block, 64, 1), 0.0))
    return jnp.concatenate(parts, 0)


def join_heads(tall, from_high):
    rows = tall.shape[0] // GROUP
    low = low_lanes((rows, 128))
    parts = []
    for pair in range(GROUP // 2):
        one = tall[2 * pair * rows:(2 * pair + 1) * rows]
        two = tall[(2 * pair + 1) * rows:(2 * pair + 2) * rows]
        if from_high:
            parts.append(jnp.where(low, pltpu.roll(one, 64, 1), two))
        else:
            parts.append(jnp.where(low, one, pltpu.roll(two, 64, 1)))
    return jnp.concatenate(parts, 1)


def two_slot_probs(spread, kv, lens, pair):
    rows = 2 * SLOT
    q_at = lax.broadcasted_iota(jnp.int32, (rows, rows), 0)
    k_at = lax.broadcasted_iota(jnp.int32, (rows, rows), 1)
    first = lens[pl.ds(pl.multiple_of(16 * pair, 8), 8), :][:1]
    second = lens[pl.ds(pl.multiple_of(16 * pair + 8, 8), 8), :][:1]
    k_len = jnp.where(lax.broadcasted_iota(jnp.int32, (1, rows), 1) < SLOT, first, second)
    k_pos = jnp.where(k_at < SLOT, k_at, k_at - SLOT).astype(F32)
    allowed = (q_at >= k_at) & ((q_at < SLOT) | (k_at >= SLOT)) & (k_pos < k_len)
    allowed = jnp.concatenate([jnp.where(allowed, 1.0, 0.0)] * GROUP, 0)
    scores = dot_last(spread, kv) * HEAD_DIM**-0.5
    scores = jnp.where(allowed > 0.5, scores, -1e30)
    terms = jnp.exp(scores - jnp.max(scores, -1, keepdims=True))
    return terms / jnp.sum(terms, -1, keepdims=True)


def root(values):
    return lax.rsqrt(jnp.mean(values * values, -1, keepdims=True) + EPSILON)


Q_AT, KV_AT, AO_AT = 0, Q_SLAB, Q_SLAB + 2 * HEAD_DIM
A_COLS = AO_AT + Q_SLAB


def forward_body(
    ends, lens_in, gain_in, tables, w_in, w_out,
    wa, wg, wd, xn_out, hn_out, qkv_out, ctx_out, gu_out, hid_out, res_out, y_out, cot_out, gain_out, lens,
    cross, k_pair, v_pair, kv_mine, kv_twin, wa_v, wg_v, wd_v, seq, hnb, qkv, ctx, gu, hid, theirs, ours, res, total,
    sib_buf, rx_up, rx_dn, tx_up, tx_dn,
    loc_sem, push_send, push_recv, hop_send, hop_recv, misc, misc_send, misc_recv, save,
    *line_sems,
):
    gather_sems, len_sems, reduce_sems = line_sems[:5], line_sems[5:10], line_sems[10:]
    here = Here()
    core, shard, place = here.core, here.shard, here.place
    width = ends.shape[1]
    part = w_in.shape[0]
    here.greet()

    own_rows = pl.ds(pl.multiple_of(shard * part, part), part)

    def cut(ref, base, size, head):
        return ref.at[:, pl.ds(pl.multiple_of(base + head * size, size), size)]

    ff0 = Q_COLS + 2 * KV_COLS
    slabs = [
        (lambda h: cut(w_in, 0, Q_SLAB, h), lambda l: wa.at[l, own_rows, pl.ds(Q_AT, Q_SLAB)]),
        (lambda h: cut(w_out, 0, Q_SLAB, h), lambda l: wa.at[l, own_rows, pl.ds(AO_AT, Q_SLAB)]),
        (None, lambda l: wa.at[l, own_rows, pl.ds(KV_AT, 2 * HEAD_DIM)]),
        (lambda h: cut(w_in, ff0, FF_SLAB, h), lambda l: wg.at[l, own_rows, pl.ds(0, FF_SLAB)]),
        (lambda h: cut(w_in, ff0 + FF, FF_SLAB, h), lambda l: wg.at[l, own_rows, pl.ds(FF_SLAB, FF_SLAB)]),
        (lambda h: cut(w_out, Q_COLS, FF_SLAB, h), lambda l: wd.at[l, own_rows]),
    ]
    my_head, twin_head = place * CORES + core, place * CORES + 1 - core

    def own_copy(i, layer):
        src, dst = slabs[i]
        return pltpu.make_async_copy(kv_mine if src is None else src(my_head), dst(layer), loc_sem.at[i])

    def twin_copy(i, layer):
        src, dst = slabs[i]
        return remote(kv_twin if src is None else src(twin_head), dst(layer), push_send.at[i], push_recv.at[i], here.twin)

    k_copy = pltpu.make_async_copy(cut(w_in, Q_COLS, 128, place), k_pair, misc.at[0])
    v_copy = pltpu.make_async_copy(cut(w_in, Q_COLS + KV_COLS, 128, place), v_pair, misc.at[1])
    k_copy.start()
    v_copy.start()
    for i in (0, 1):
        twin_copy(i, core).start()
        own_copy(i, core).start()
    other_rows = pl.ds(pl.multiple_of((1 - core) * SLOT, SLOT), SLOT)
    cross_copy = remote(ends.at[other_rows], cross, misc_send.at[0], misc_recv.at[0], here.twin)
    cross_copy.start()
    gain_copy = remote(gain_in, gain_out.at[core], misc_send.at[1], misc_recv.at[1], here.twin)
    gain_copy.start()
    gain_out[core] = gain_in[...]
    k_copy.wait()
    v_copy.wait()
    low = low_lanes(k_pair.shape)
    k, v = k_pair[...].astype(F32), v_pair[...].astype(F32)
    kv0 = jnp.where(low, k, pltpu.roll(v, 64, 1)).astype(BF16)
    kv1 = jnp.where(low, pltpu.roll(k, 64, 1), v).astype(BF16)
    kv_mine[...] = jnp.where(core == 0, kv0, kv1)
    kv_twin[...] = jnp.where(core == 0, kv1, kv0)
    for i in (2, 3, 4, 5):
        twin_copy(i, core).start()
        own_copy(i, core).start()

    PIECES = ((wa, (0, 1, 2)), (wg, (3, 4)), (wd, (5,)))
    half = part // 2

    def own_ready(layer, piece):
        @pl.when(core == layer)
        def _():
            for i in PIECES[piece][1]:
                own_copy(i, layer).wait()

        @pl.when(core != layer)
        def _():
            for i in PIECES[piece][1]:
                twin_copy(i, layer).wait_recv()

    def hop(layer, piece, which, rows, size, peer):
        ref = PIECES[piece][0].at[layer, pl.ds(pl.multiple_of(rows, size), size)]
        return remote(ref, ref, hop_send.at[layer, piece, which], hop_recv.at[layer, piece, which], peer)

    def hops(layer, piece):
        return (
            hop(layer, piece, 0, shard * part, part, here.x_peer),
            hop(layer, piece, 1, shard * part, part, here.y_peer),
            hop(layer, piece, 2, here.x_shard * part, half, here.y_peer),
            hop(layer, piece, 3, here.y_shard * part + half, half, here.x_peer),
        )

    def hop_one(layer, piece):
        own_ready(layer, piece)
        one, two, _, _ = hops(layer, piece)
        one.start()
        two.start()

    def hop_two(layer, piece):
        one, two, three, four = hops(layer, piece)
        one.wait_recv()
        three.start()
        two.wait_recv()
        four.start()

    def all_in(layer, piece):
        _, _, three, four = hops(layer, piece)
        three.wait_recv()
        four.wait_recv()

    hop_one(0, 0)

    rows8 = lens_in.shape[0]
    lens[pl.ds(pl.multiple_of((core * LINE + place) * rows8, rows8), rows8), :] = lens_in[...]
    line_gather(here, lens, len_sems)
    cross_copy.wait()
    gain_copy.wait()
    first = core == 0
    ours0, others0 = ends[:SLOT].astype(F32), ends[SLOT:].astype(F32)
    crossed = cross[...].astype(F32)
    x = jnp.where(first, ours0, crossed)
    cot_out[...] = jnp.where(first, crossed, others0).astype(BF16)
    res[0] = x

    def own_block(ref):
        return ref.at[pl.ds(pl.multiple_of((core * LINE + place) * SLOT, SLOT), SLOT), :]

    def load(src, dst, i):
        copy = pltpu.make_async_copy(src, dst, misc.at[i])
        copy.start()
        copy.wait()

    reduce_bufs = (sib_buf, rx_up, rx_dn, tx_up, tx_dn)
    half_rows = LINE * SLOT

    def layer(index):
        saves = []

        def keep(src, dst):
            copy = pltpu.make_async_copy(src, dst, save.at[index, len(saves)])
            copy.start()
            saves.append(copy)

        if index == 0:
            x = res[0]
        else:
            x = y_out[...].astype(F32)
            res[2] = x
        own_block(seq)[...] = (x * root(x) * gain_out[index, 0:1]).astype(BF16)
        line_gather(here, seq, gather_sems)
        keep(seq, xn_out.at[index])
        hop_two(index, 0)
        hop_one(index, 1 if index == 0 else 2)
        all_in(index, 0)
        load(wa.at[index], wa_v, 0)

        def attend(pair, _):
            at = pl.ds(pl.multiple_of(pair * 2 * SLOT, 2 * SLOT), 2 * SLOT)
            wide = dot(seq[at, :], wa_v[:, :AO_AT])
            kv = turn(wide[:, KV_AT:AO_AT], tables[2], tables[3])
            q = jnp.concatenate(
                [turn(wide[:, 128 * i:128 * (i + 1)], tables[0], tables[1]) for i in range(GROUP // 2)], 1
            )
            kv_low = kv.astype(BF16)
            qkv[at, :Q_SLAB] = q.astype(BF16)
            qkv[at, KV_AT:AO_AT] = kv_low
            probs = two_slot_probs(spread_heads(q).astype(BF16), kv_low, lens, pair).astype(BF16)
            ctx[at, :] = join_heads(dot(probs, kv_low), True).astype(BF16)
            return 0

        lax.fori_loop(0, LINE, attend, 0)
        keep(qkv, qkv_out.at[index])
        keep(ctx, ctx_out.at[index])
        if index == 0:
            hop_one(0, 2)

        def terms(whose, src, weights, cols, dst):
            rows = pl.ds(pl.multiple_of(whose * half_rows, half_rows), half_rows)

            def tile(n, _):
                at = pl.ds(pl.multiple_of(n * 512, 512), 512)
                dst[:, at] = dot_last(src[rows, :], weights[at, cols]).astype(dst.dtype)
                return 0

            lax.fori_loop(0, width // 512, tile, 0)

        def reduce(src, weights, cols):
            terms(1 - core, src, weights, cols, theirs)
            line_reduce(here, total, ours, theirs, reduce_bufs, reduce_sems,
                        lambda: terms(core, src, weights, cols, ours))

        saves[0].wait()
        reduce(ctx, wa_v, slice(AO_AT, A_COLS))
        middle = x + total[...]
        res[1 + 2 * index] = middle
        own_block(hnb)[...] = (middle * root(middle) * gain_out[index, 1:2]).astype(BF16)
        line_gather(here, hnb, gather_sems)
        keep(hnb, hn_out.at[index])
        hop_two(index, 1)
        if index == 0:
            hop_one(1, 0)
        all_in(index, 1)
        load(wg.at[index], wg_v, 0)

        def gate_up(n, _):
            at = pl.ds(pl.multiple_of(n * 256, 256), 256)
            at_up = pl.ds(pl.multiple_of(FF_SLAB + n * 256, 256), 256)
            gate = dot(hnb[...], wg_v[:, at])
            up = dot(hnb[...], wg_v[:, at_up])
            gu[:, at] = gate
            gu[:, at_up] = up
            hid[:, at] = (gate * jax.nn.sigmoid(gate) * up).astype(BF16)
            return 0

        lax.fori_loop(0, FF_SLAB // 256, gate_up, 0)
        keep(gu, gu_out.at[index])
        keep(hid, hid_out.at[index])
        hop_two(index, 2)
        if index == 0:
            hop_one(1, 1)
        all_in(index, 2)
        load(wd.at[index], wd_v, 0)
        saves[3].wait()
        reduce(hid, wd_v, slice(None))
        y_out[...] = (res[1 + 2 * index] + total[...]).astype(BF16)
        for i in (1, 2, 4, 5):
            saves[i].wait()

    layer(0)
    layer(1)
    for i in range(4):
        pltpu.make_async_copy(res.at[i], res_out.at[i], misc.at[i]).start()
    for i in range(4):
        pltpu.make_async_copy(res.at[i], res_out.at[i], misc.at[i]).wait()
    for i in range(6):
        twin_copy(i, core).wait_send()
    for index in range(2):
        for piece in range(3):
            for move in hops(index, piece):
                move.wait_send()


def forward_call(ends, lens, gain, tables, w_in, w_out):
    width = ends.shape[1]
    rows = LINE * CORES * SLOT
    hbm = pl.BlockSpec(memory_space=pl.ANY)
    vmem = pl.BlockSpec(memory_space=pltpu.VMEM)
    shape = jax.ShapeDtypeStruct
    dma = pltpu.SemaphoreType.DMA
    line = dma((LINE,))
    block = pltpu.VMEM((LINE * SLOT, width), BF16)
    return pl.pallas_call(
        forward_body,
        out_shape=[
            shape((2, width, A_COLS), BF16),
            shape((2, width, 2 * FF_SLAB), BF16),
            shape((2, width, FF_SLAB), BF16),
            shape((2, rows, width), BF16),
            shape((2, rows, width), BF16),
            shape((2, rows, AO_AT), BF16),
            shape((2, rows, Q_SLAB), BF16),
            shape((2, rows, 2 * FF_SLAB), F32),
            shape((2, rows, FF_SLAB), BF16),
            shape((4, SLOT, width), F32),
            shape((SLOT, width), BF16),
            shape((SLOT, width), BF16),
            shape((2, 2, width), F32),
            shape((LINE * CORES * 8, 128), F32),
        ],
        in_specs=[vmem, vmem, vmem, vmem, hbm, hbm],
        out_specs=[hbm] * 10 + [vmem] * 4,
        scratch_shapes=[
            pltpu.VMEM((SLOT, width), BF16),
            pltpu.VMEM((w_in.shape[0], 128), BF16),
            pltpu.VMEM((w_in.shape[0], 128), BF16),
            pltpu.VMEM((w_in.shape[0], 128), BF16),
            pltpu.VMEM((w_in.shape[0], 128), BF16),
            pltpu.VMEM((width, A_COLS), BF16),
            pltpu.VMEM((width, 2 * FF_SLAB), BF16),
            pltpu.VMEM((width, FF_SLAB), BF16),
            pltpu.VMEM((rows, width), BF16),
            pltpu.VMEM((rows, width), BF16),
            pltpu.VMEM((rows, AO_AT), BF16),
            pltpu.VMEM((rows, Q_SLAB), BF16),
            pltpu.VMEM((rows, 2 * FF_SLAB), F32),
            pltpu.VMEM((rows, FF_SLAB), BF16),
            block,
            pltpu.VMEM((LINE * SLOT, width), F32),
            pltpu.VMEM((4, SLOT, width), F32),
            pltpu.VMEM((SLOT, width), F32),
            block, block, block, block, block,
            dma((6,)), dma((6,)), dma((6,)), dma((2, 3, 4)), dma((2, 3, 4)),
            dma((4,)), dma((2,)), dma((2,)), dma((2, 6)),
        ] + [line] * 16,
        compiler_params=pltpu.CompilerParams(
            collective_id=0, has_side_effects=True, vmem_limit_bytes=56 * 2**20
        ),
        name="forward_two_layers",
        cost_estimate=pl.CostEstimate(flops=16_000_000_000, bytes_accessed=600_000_000, transcendentals=0),
    )(ends, lens, gain, tables, w_in, w_out)


def swap_cores(value):
    return lax.ppermute(value, "section", [(0, 1), (1, 0)])


def hop(value, bit):
    peers = lax.axis_size("shard")
    return lax.ppermute(value, "shard", [(i, i ^ bit) for i in range(peers)])


def gather_rows(block):
    half = block.shape[0] // 2
    one = hop(block, 1)
    two = hop(block, 2)
    top = hop(two[:half], 1)
    bottom = hop(one[half:], 2)
    return jnp.concatenate([block, one, two, top, bottom], 0)


def reduce_rows(term):
    far = term(3)
    half = far.shape[0] // 2
    via_one = hop(far[:half], 1).astype(F32)
    via_two = hop(far[half:], 2).astype(F32)
    first = term(1).astype(F32)
    one = hop(jnp.concatenate([first[:half], first[half:] + via_two], 0).astype(BF16), 1)
    second = term(2).astype(F32)
    two = hop(jnp.concatenate([second[:half] + via_one, second[half:]], 0).astype(BF16), 2)
    return (term(0).astype(F32) + one.astype(F32) + two.astype(F32)).astype(BF16)


def relative(values, shard):
    blocks = jnp.split(values, 4, -1)
    odd = (shard & 1) == 1
    high = (shard & 2) == 2
    blocks = [jnp.where(odd, blocks[i ^ 1], blocks[i]) for i in range(4)]
    blocks = [jnp.where(high, blocks[i ^ 2], blocks[i]) for i in range(4)]
    return jnp.concatenate(blocks, -1)


def rope_tables(rows):
    half_dim = HEAD_DIM // 2
    inverse = 500000.0 ** (-(jnp.arange(half_dim, dtype=F32) * 2.0 / HEAD_DIM))
    angles = jnp.arange(rows, dtype=F32)[:, None] * inverse[None, :]
    return (jnp.cos(angles)[None, :, None, :], jnp.sin(angles)[None, :, None, :])


def rotate(values, cosine, sine):
    a, b = jnp.split(values, 2, -1)
    return jnp.concatenate([a * cosine - b * sine, b * cosine + a * sine], -1)


def unrotate(grads, cosine, sine):
    a, b = jnp.split(grads, 2, -1)
    return jnp.concatenate([a * cosine + b * sine, b * cosine - a * sine], -1)


def rms_scale(values):
    return lax.rsqrt(jnp.mean(values * values, -1, keepdims=True) + EPSILON)


def rms_back(values, scale, gain_row, grad_norm):
    grad_hat = grad_norm * gain_row
    grad_gain = jnp.sum(grad_norm * values * scale, 0)
    inner = jnp.mean(grad_hat * values, -1, keepdims=True)
    return (scale * grad_hat - values * scale * scale * scale * inner, grad_gain)


def mm(a, b):
    return jnp.dot(a, b, preferred_element_type=F32)


def mm_last(a, b):
    return lax.dot_general(a, b, (((1,), (1,)), ((), ())), preferred_element_type=F32)


def mm_rows(a, b):
    return lax.dot_general(a, b, (((0,), (0,)), ((), ())), preferred_element_type=F32)


def masked_scores(queries, keys, lengths):
    rows = queries.shape[1]
    places = jnp.arange(rows)
    allowed = (places[:, None] >= places[None, :])[None] & (
        places[None, None, :] < lengths[:, None, None]
    )
    scores = jnp.einsum("sqgd,spd->sgqp", queries, keys, preferred_element_type=F32)
    return jnp.where(allowed[:, None], scores * HEAD_DIM**-0.5, -1e30)


def forward_layer(x, weights, gains, lengths, tables):
    w_qkv, w_attn, w_gu, w_down = weights
    slots = lengths.shape[0]
    rows = x.shape[0]
    scale_one = rms_scale(x)
    normed = gather_line((x * scale_one * gains[0]).astype(BF16))
    projected = mm(normed, w_qkv)
    queries = rotate(projected[:, :Q_SLAB].reshape(slots, rows, GROUP, HEAD_DIM), *tables).astype(BF16)
    keys = rotate(
        projected[:, Q_SLAB:Q_SLAB + HEAD_DIM].reshape(slots, rows, 1, HEAD_DIM), *tables
    ).astype(BF16)[:, :, 0]
    values = projected[:, Q_SLAB + HEAD_DIM:].reshape(slots, rows, HEAD_DIM).astype(BF16)
    scores = masked_scores(queries, keys, lengths)
    top = jnp.max(scores, -1, keepdims=True)
    terms = jnp.exp(scores - top)
    total = jnp.sum(terms, -1, keepdims=True)
    log_total = top + jnp.log(total)
    probs = (terms / total).astype(BF16)
    context = jnp.einsum("sgqp,spd->sqgd", probs, values, preferred_element_type=F32)
    context = context.reshape(slots * rows, Q_SLAB).astype(BF16)
    middle = x + scatter_line(mm_last(context, w_attn).astype(BF16))
    scale_two = rms_scale(middle)
    normed_two = gather_line((middle * scale_two * gains[1]).astype(BF16))
    gate_up = mm(normed_two, w_gu)
    gate, up = gate_up[:, :FF_SLAB], gate_up[:, FF_SLAB:]
    hidden = (jax.nn.silu(gate) * up).astype(BF16)
    output = middle + scatter_line(mm_last(hidden, w_down).astype(BF16))
    return output, (x, scale_one, normed, queries, keys, values, log_total, context,
                    middle, scale_two, normed_two, gate, up, hidden)


def backward_layer(kept, grad_out, weights, gains, lengths, tables):
    (x, scale_one, normed, queries, keys, values, log_total, context,
     middle, scale_two, normed_two, gate, up, hidden) = kept
    w_qkv, w_attn, w_gu, w_down = weights
    slots = lengths.shape[0]
    rows = x.shape[0]
    grad_mlp = gather_line(grad_out.astype(BF16))
    grad_hidden = mm(grad_mlp, w_down)
    sig = jax.nn.sigmoid(gate)
    grad_gate = grad_hidden * up * sig * (1.0 + gate * (1.0 - sig))
    grad_up = grad_hidden * gate * sig
    grad_gu = jnp.concatenate([grad_gate, grad_up], 1).astype(BF16)
    grad_normed = scatter_line(mm_last(grad_gu, w_gu).astype(BF16))
    back, gain_two = rms_back(middle, scale_two, gains[1], grad_normed)
    grad_mid = grad_out + back
    grad_attn = gather_line(grad_mid.astype(BF16))
    grad_context = mm(grad_attn, w_attn).astype(BF16).reshape(slots, rows, GROUP, HEAD_DIM)
    probs = jnp.exp(masked_scores(queries, keys, lengths) - log_total)
    grad_values = jnp.einsum("sgqp,sqgd->spd", probs.astype(BF16), grad_context, preferred_element_type=F32)
    grad_probs = jnp.einsum("sqgd,spd->sgqp", grad_context, values, preferred_element_type=F32)
    inner = jnp.sum(grad_probs * probs, -1, keepdims=True)
    grad_scores = (probs * (grad_probs - inner)).astype(BF16)
    grad_queries = jnp.einsum("sgqp,spd->sqgd", grad_scores, keys, preferred_element_type=F32)
    grad_keys = jnp.einsum("sgqp,sqgd->spd", grad_scores, queries, preferred_element_type=F32)
    grad_queries = unrotate(grad_queries * HEAD_DIM**-0.5, *tables)
    grad_keys = unrotate(grad_keys[:, :, None] * HEAD_DIM**-0.5, *tables)
    grad_proj = jnp.concatenate(
        [
            grad_queries.reshape(slots * rows, Q_SLAB),
            grad_keys.reshape(slots * rows, HEAD_DIM),
            grad_values.reshape(slots * rows, HEAD_DIM),
        ],
        1,
    ).astype(BF16)
    grad_normed = scatter_line(mm_last(grad_proj, w_qkv).astype(BF16))
    back, gain_one = rms_back(x, scale_one, gains[0], grad_normed)
    mlp = ((normed_two, grad_gu), (grad_mlp, hidden))
    attn = ((normed, grad_proj), (grad_attn, context))
    return grad_mid + back, mlp, attn, jnp.stack([gain_one, gain_two])


def slab(weight, start, size):
    return lax.dynamic_slice_in_dim(weight, start, size, 1)


def attn_slab(w_in, w_out, head):
    return jnp.concatenate(
        [
            slab(w_in, head * Q_SLAB, Q_SLAB),
            slab(w_in, Q_COLS + head * HEAD_DIM, HEAD_DIM),
            slab(w_in, Q_COLS + KV_COLS + head * HEAD_DIM, HEAD_DIM),
            slab(w_out, head * Q_SLAB, Q_SLAB),
        ],
        1,
    )


def mlp_slab(w_in, w_out, head):
    base = Q_COLS + 2 * KV_COLS
    return jnp.concatenate(
        [
            slab(w_in, base + head * FF_SLAB, FF_SLAB),
            slab(w_in, base + FF + head * FF_SLAB, FF_SLAB),
            slab(w_out, Q_COLS + head * FF_SLAB, FF_SLAB),
        ],
        1,
    )


def line_pairs(shift):
    peers = lax.axis_size("dp")
    return [(i, i // LINE * LINE + (i % LINE + shift) % LINE) for i in range(peers)]


def line_exchange(blocks, place):
    got = [lax.dynamic_index_in_dim(blocks, place, 0, False)]
    for shift in range(1, LINE):
        to = lax.rem(place + shift, LINE)
        got.append(lax.ppermute(lax.dynamic_index_in_dim(blocks, to, 0, False), "dp", line_pairs(shift)))
    return got


def local(ends_in, in_weight, out_weight, norm_gain, seq_len):
    core = lax.axis_index("section")
    shard = lax.axis_index("shard")
    depth = lax.axis_index("dp")
    place = lax.rem(depth, LINE)
    first = core == 0
    replicas = lax.axis_size("dp") // LINE
    w_in, w_out = in_weight[0], out_weight[0]
    rows = ends_in.shape[1] // CORES

    def by_layer(mine, others):
        return jnp.where(first, mine, others), jnp.where(first, others, mine)

    own_length = jnp.where(first, seq_len[0], seq_len[1])
    valid = (jnp.arange(rows) < own_length).astype(F32)[:, None]
    tables = rope_tables(rows)
    cos, sin = tables[0][0, :, 0], tables[1][0, :, 0]
    one, zero = jnp.ones((rows, HEAD_DIM), F32), jnp.zeros((rows, HEAD_DIM), F32)
    rope = jnp.stack([
        jnp.tile(jnp.concatenate([cos] * 4, 1), (2, 1)),
        jnp.tile(jnp.concatenate([-sin, sin] * 2, 1), (2, 1)),
        jnp.tile(jnp.concatenate([cos, cos, one], 1), (2, 1)),
        jnp.tile(jnp.concatenate([-sin, sin, zero], 1), (2, 1)),
    ])
    lens_block = jnp.full((8, 128), own_length.astype(F32))
    (wa, wg, wd, xn, hn, qkv, ctx, gu, hid, res, y1, cot, gains, lens) = forward_call(
        ends_in[0], lens_block, norm_gain[0], rope, w_in, w_out
    )
    lengths = lens[::8, 0].astype(jnp.int32)
    cot = cot.astype(F32)
    slots = LINE * CORES
    weights = [(wa[l, :, :AO_AT], wa[l, :, AO_AT:], wg[l], wd[l]) for l in range(2)]

    def kept_of(l):
        x, middle = res[2 * l], res[2 * l + 1]
        queries = qkv[l, :, :Q_SLAB].reshape(slots, rows, GROUP, HEAD_DIM)
        keys = qkv[l, :, Q_SLAB:Q_SLAB + HEAD_DIM].reshape(slots, rows, HEAD_DIM)
        values = qkv[l, :, Q_SLAB + HEAD_DIM:].reshape(slots, rows, HEAD_DIM)
        scores = masked_scores(queries, keys, lengths)
        log_total = jax.nn.logsumexp(scores, -1, keepdims=True)
        return (x, rms_scale(x), xn[l], queries, keys, values, log_total, ctx[l], middle,
                rms_scale(middle), hn[l], gu[l, :, :FF_SLAB], gu[l, :, FF_SLAB:], hid[l])

    kept0, kept1 = kept_of(0), kept_of(1)
    dx1, mlp1, attn1, gain1 = backward_layer(kept1, cot * valid, weights[1], gains[1], lengths, tables)
    dx0, mlp0, attn0, gain0 = backward_layer(
        kept0, dx1.astype(BF16).astype(F32), weights[0], gains[0], lengths, tables
    )

    def reduced(pairs):
        (in_rows, in_cols), (out_rows, out_cols) = pairs

        def term(k):
            size = in_rows.shape[1] // 4
            at = jnp.bitwise_xor(shard, k) * size
            cut = lambda v: lax.dynamic_slice_in_dim(v, at, size, 1)
            return jnp.concatenate(
                [mm_rows(cut(in_rows), in_cols), mm_rows(cut(out_rows), out_cols)], 1
            ).astype(BF16)

        total = reduce_rows(term)
        if replicas > 1:
            groups = [[r * LINE + p for r in range(replicas)] for p in range(LINE)]
            total = lax.psum_scatter(total, "dp", scatter_dimension=0, tiled=True, axis_index_groups=groups)
        blocks = total.reshape(LINE, total.shape[0] // LINE, total.shape[1])
        got = line_exchange(blocks, place)
        order = [lax.rem(place - shift + LINE, LINE) for shift in range(LINE)]
        return got

    grads = []
    for pairs in ((mlp1, attn1), (mlp0, attn0)):
        grads.append([jnp.stack(reduced(part)) for part in pairs])
    (m1, a1), (m0, a0) = grads

    def place_order(pieces):
        index = jnp.array([0], jnp.int32)
        index = jnp.remainder(place - jnp.arange(LINE), LINE)
        return jnp.take(pieces, index, axis=0)

    def to_layer_core(zero, one):
        zero, one = place_order(zero), place_order(one)
        mine = jnp.where(first, zero, one)
        others = swap_cores(jnp.where(first, one, zero))
        both = jnp.stack([jnp.where(first, mine, others), jnp.where(first, others, mine)], 1)
        return both.reshape(KV_HEADS, both.shape[2], both.shape[3]).astype(F32)

    grad_attn = to_layer_core(a0, a1)
    grad_mlp = to_layer_core(m0, m1)

    def columns(values, lo, hi):
        part = values[:, :, lo:hi].transpose(1, 0, 2)
        return part.reshape(part.shape[0], -1)

    in_grad = jnp.concatenate(
        [
            columns(grad_attn, 0, Q_SLAB),
            columns(grad_attn, Q_SLAB, Q_SLAB + HEAD_DIM),
            columns(grad_attn, Q_SLAB + HEAD_DIM, QKV_SLAB),
            columns(grad_mlp, 0, FF_SLAB),
            columns(grad_mlp, FF_SLAB, 2 * FF_SLAB),
        ],
        1,
    )
    out_grad = jnp.concatenate(
        [columns(grad_attn, QKV_SLAB, QKV_SLAB + Q_SLAB), columns(grad_mlp, 2 * FF_SLAB, 3 * FF_SLAB)], 1
    )
    own_gains = jnp.where(first, gain0, gain1) + swap_cores(jnp.where(first, gain1, gain0))
    gain_rows = lax.psum_scatter(own_gains, ("shard", "dp"), scatter_dimension=1, tiled=True)
    dx0 = dx0.astype(BF16)
    crossed = swap_cores(jnp.where(first, y1, dx0))
    ends_mine = jnp.where(first, dx0, crossed)
    ends_others = jnp.where(first, crossed, y1)
    ends_out = jnp.concatenate([ends_mine, ends_others], 0)
    return ends_out[None], in_grad[None], out_grad[None], gain_rows[None]


def solution(mesh):
    in_specs = (
        P("section", ("shard", "dp"), None),
        P("section", "shard", None),
        P("section", "shard", None),
        P("section", None, None),
        P(("shard", "dp")),
    )
    out_specs = (
        P("section", ("shard", "dp"), None),
        P("section", ("shard", "dp"), None),
        P("section", ("shard", "dp"), None),
        P("section", None, ("shard", "dp")),
    )
    return jax.shard_map(local, mesh=mesh, in_specs=in_specs, out_specs=out_specs, check_vma=False)
```

```python
import functools

import jax
import jax.numpy as jnp
from jax import lax
from jax.experimental import pallas as pl
from jax.experimental.pallas import tpu as pltpu
from jax.sharding import PartitionSpec as P

HEADS = 32
KV_HEADS = 8
GROUP = HEADS // KV_HEADS
HEAD_DIM = 64
FF = 8192
EPSILON = 1e-05
BF16 = jnp.bfloat16
F32 = jnp.float32
CORES = 2
LINE = KV_HEADS // CORES
SHARDS = 4
SLOT = 64
Q_SLAB = GROUP * HEAD_DIM
QKV_SLAB = Q_SLAB + 2 * HEAD_DIM
FF_SLAB = FF // KV_HEADS
Q_COLS = HEADS * HEAD_DIM
KV_COLS = KV_HEADS * HEAD_DIM


class Here:
    def __init__(self):
        self.core = lax.axis_index("section")
        self.shard = lax.axis_index("shard")
        self.depth = lax.axis_index("dp")
        self.place = lax.rem(self.depth, LINE)
        self.twin = {"section": 1 - self.core}
        self.x_shard = self.shard + 1 - 2 * lax.rem(self.shard, 2)
        self.y_shard = lax.rem(self.shard + 2, SHARDS)
        self.far_shard = SHARDS - 1 - self.shard
        self.x_peer = {"shard": self.x_shard}
        self.y_peer = {"shard": self.y_shard}
        self.above = {"dp": self.depth + 1}
        self.below = {"dp": self.depth - 1}
        self.has_above = self.place < LINE - 1
        self.has_below = self.place > 0

    def greet(self):
        barrier = pltpu.get_barrier_semaphore()
        for peer in (self.twin, self.x_peer, self.y_peer):
            pl.semaphore_signal(barrier, inc=1, device_id=peer)

        @pl.when(self.has_above)
        def _():
            pl.semaphore_signal(barrier, inc=1, device_id=self.above)

        @pl.when(self.has_below)
        def _():
            pl.semaphore_signal(barrier, inc=1, device_id=self.below)

        pl.semaphore_wait(barrier, jnp.where(self.has_above & self.has_below, 5, 4))


def remote(src, dst, send, recv, device):
    return pltpu.make_async_remote_copy(src, dst, send, recv, device_id=device)


def rows_at(ref, start, size):
    return ref.at[pl.ds(pl.multiple_of(start, size), size)]


def line_gather(here, buf, sems, meanwhile=()):
    up_send, dn_send, sib_send, z_recv, sib_recv = sems
    rows = buf.shape[0] // (LINE * CORES)
    core, place = here.core, here.place
    meanwhile = list(meanwhile) + [None] * LINE

    def part(where, whose):
        return rows_at(buf, (whose * LINE + where) * rows, rows)

    def up(where):
        mine = part(where, core)
        return remote(mine, mine, up_send.at[where], z_recv.at[where], here.above)

    def down(where):
        mine = part(where, core)
        return remote(mine, mine, dn_send.at[where], z_recv.at[where], here.below)

    def across(where, whose):
        mine = part(where, whose)
        return remote(mine, mine, sib_send.at[where], sib_recv.at[where], here.twin)

    @pl.when(here.has_above)
    def _():
        up(place).start()

    @pl.when(here.has_below)
    def _():
        down(place).start()

    across(place, core).start()
    for step in range(1, LINE):
        if meanwhile[step - 1] is not None:
            meanwhile[step - 1]()

        @pl.when(place >= step)
        def _():
            up(place - step).wait_recv()

            @pl.when(here.has_above)
            def _():
                up(place - step).start()

            across(place - step, core).start()

        @pl.when(place + step < LINE)
        def _():
            down(place + step).wait_recv()

            @pl.when(here.has_below)
            def _():
                down(place + step).start()

            across(place + step, core).start()

    if meanwhile[LINE - 1] is not None:
        meanwhile[LINE - 1]()
    for where in range(LINE):
        across(where, 1 - core).wait_recv()
        across(where, core).wait_send()

        @pl.when((where <= place) & here.has_above)
        def _():
            up(where).wait_send()

        @pl.when((where >= place) & here.has_below)
        def _():
            down(where).wait_send()


def line_reduce(here, out, ours, theirs, bufs, sems, own_terms=None, meanwhile=()):
    sib_buf, rx_up, rx_dn, tx_up, tx_dn = bufs
    sib_send, sib_recv, up_send, up_recv, dn_send, dn_recv = sems
    rows = out.shape[0]
    place = here.place
    meanwhile = list(meanwhile) + [None] * LINE

    def part(ref, where):
        return rows_at(ref, where * rows, rows)

    def read(ref, where):
        return ref[pl.ds(pl.multiple_of(where * rows, rows), rows), :].astype(F32)

    def across(where):
        return remote(part(theirs, where), part(sib_buf, where), sib_send.at[where], sib_recv.at[where], here.twin)

    def up(where):
        return remote(part(tx_up, where), part(rx_up, where), up_send.at[where], up_recv.at[where], here.above)

    def down(where):
        return remote(part(tx_dn, where), part(rx_dn, where), dn_send.at[where], dn_recv.at[where], here.below)

    def summed(where):
        return read(ours, where) + read(sib_buf, where)

    def put(ref, where, value):
        ref[pl.ds(pl.multiple_of(where * rows, rows), rows), :] = value.astype(BF16)

    for step in range(LINE - 1, 0, -1):
        @pl.when(place + step < LINE)
        def _():
            across(place + step).start()

        @pl.when(place >= step)
        def _():
            across(place - step).start()

    across(place).start()
    if own_terms is not None:
        own_terms()
    for step in range(LINE - 1, 0, -1):
        @pl.when(place + step < LINE)
        def _():
            where = place + step
            across(where).wait_recv()

            @pl.when(here.has_below)
            def _():
                up(where).wait_recv()
                put(tx_up, where, summed(where) + read(rx_up, where))

            @pl.when(place == 0)
            def _():
                put(tx_up, where, summed(where))

            up(where).start()

        @pl.when(place >= step)
        def _():
            where = place - step
            across(where).wait_recv()

            @pl.when(here.has_above)
            def _():
                down(where).wait_recv()
                put(tx_dn, where, summed(where) + read(rx_dn, where))

            @pl.when(place == LINE - 1)
            def _():
                put(tx_dn, where, summed(where))

            down(where).start()

        if meanwhile[LINE - 1 - step] is not None:
            meanwhile[LINE - 1 - step]()

    across(place).wait_recv()
    out[...] = summed(place)

    @pl.when(here.has_below)
    def _():
        up(place).wait_recv()
        out[...] += read(rx_up, place)

    @pl.when(here.has_above)
    def _():
        down(place).wait_recv()
        out[...] += read(rx_dn, place)

    for where in range(LINE):
        across(where).wait_send()

        @pl.when(where > place)
        def _():
            up(where).wait_send()

        @pl.when(where < place)
        def _():
            down(where).wait_send()


def dot(a, b):
    return jnp.dot(a, b, preferred_element_type=F32)


def dot_last(a, b):
    return lax.dot_general(a, b, (((1,), (1,)), ((), ())), preferred_element_type=F32)


def dot_rows(a, b):
    return lax.dot_general(a, b, (((0,), (0,)), ((), ())), preferred_element_type=F32)


def low_lanes(shape, size=HEAD_DIM):
    return lax.rem(lax.broadcasted_iota(jnp.int32, shape, 1), 2 * size) < size


def turn(block, cosine, sine):
    half = HEAD_DIM // 2
    other = jnp.where(low_lanes(block.shape, half), pltpu.roll(block, 128 - half, 1), pltpu.roll(block, half, 1))
    return block * cosine + other * sine


def spread_heads(wide):
    low = low_lanes((wide.shape[0], 128))
    parts = []
    for pair in range(GROUP // 2):
        block = wide[:, pair * 128:(pair + 1) * 128]
        parts.append(jnp.where(low, block, 0.0))
        parts.append(jnp.where(low, pltpu.roll(block, 64, 1), 0.0))
    return jnp.concatenate(parts, 0)


def join_heads(tall, from_high):
    rows = tall.shape[0] // GROUP
    low = low_lanes((rows, 128))
    parts = []
    for pair in range(GROUP // 2):
        one = tall[2 * pair * rows:(2 * pair + 1) * rows]
        two = tall[(2 * pair + 1) * rows:(2 * pair + 2) * rows]
        if from_high:
            parts.append(jnp.where(low, pltpu.roll(one, 64, 1), two))
        else:
            parts.append(jnp.where(low, one, pltpu.roll(two, 64, 1)))
    return jnp.concatenate(parts, 1)


def two_slot_probs(spread, kv, lens, pair):
    rows = 2 * SLOT
    q_at = lax.broadcasted_iota(jnp.int32, (rows, rows), 0)
    k_at = lax.broadcasted_iota(jnp.int32, (rows, rows), 1)
    first = lens[pl.ds(pl.multiple_of(16 * pair, 8), 8), :][:1]
    second = lens[pl.ds(pl.multiple_of(16 * pair + 8, 8), 8), :][:1]
    k_len = jnp.where(lax.broadcasted_iota(jnp.int32, (1, rows), 1) < SLOT, first, second)
    k_pos = jnp.where(k_at < SLOT, k_at, k_at - SLOT).astype(F32)
    allowed = (q_at >= k_at) & ((q_at < SLOT) | (k_at >= SLOT)) & (k_pos < k_len)
    allowed = jnp.concatenate([jnp.where(allowed, 1.0, 0.0)] * GROUP, 0)
    scores = dot_last(spread, kv) * HEAD_DIM**-0.5
    scores = jnp.where(allowed > 0.5, scores, -1e30)
    terms = jnp.exp(scores - jnp.max(scores, -1, keepdims=True))
    return terms / jnp.sum(terms, -1, keepdims=True)


def root(values):
    return lax.rsqrt(jnp.mean(values * values, -1, keepdims=True) + EPSILON)


Q_AT, KV_AT, AO_AT = 0, Q_SLAB, Q_SLAB + 2 * HEAD_DIM
A_COLS = AO_AT + Q_SLAB


def forward_body(
    ends, lens_in, gain_in, tables, w_in, w_out,
    wa_out, wg_out, wd_out, xn_out, hn_out, qkv_out, ctx_out, gu_out, hid_out, res_out, y_out, cot_out, gain_out, lens,
    cross, k_pair, v_pair, kv_mine, kv_twin, wa, wg, wd, seq, hnb, qkv, ctx, gu, hid, theirs, ours, res, total,
    sib_buf, rx_up, rx_dn, tx_up, tx_dn,
    loc_sem, push_send, push_recv, hop_send, hop_recv, misc, misc_send, misc_recv, save, w_save,
    *line_sems,
):
    gather_sems, len_sems, reduce_sems = line_sems[:5], line_sems[5:10], line_sems[10:]
    here = Here()
    core, shard, place = here.core, here.shard, here.place
    width = ends.shape[1]
    part = w_in.shape[0]
    here.greet()

    own_rows = pl.ds(pl.multiple_of(shard * part, part), part)

    def cut(ref, base, size, head):
        return ref.at[:, pl.ds(pl.multiple_of(base + head * size, size), size)]

    ff0 = Q_COLS + 2 * KV_COLS
    slabs = [
        (lambda h: cut(w_in, 0, Q_SLAB, h), lambda l: wa.at[l, own_rows, pl.ds(Q_AT, Q_SLAB)]),
        (lambda h: cut(w_out, 0, Q_SLAB, h), lambda l: wa.at[l, own_rows, pl.ds(AO_AT, Q_SLAB)]),
        (None, lambda l: wa.at[l, own_rows, pl.ds(KV_AT, 2 * HEAD_DIM)]),
        (lambda h: cut(w_in, ff0, FF_SLAB, h), lambda l: wg.at[l, own_rows, pl.ds(0, FF_SLAB)]),
        (lambda h: cut(w_in, ff0 + FF, FF_SLAB, h), lambda l: wg.at[l, own_rows, pl.ds(FF_SLAB, FF_SLAB)]),
        (lambda h: cut(w_out, Q_COLS, FF_SLAB, h), lambda l: wd.at[l, own_rows]),
    ]
    my_head, twin_head = place * CORES + core, place * CORES + 1 - core

    def own_copy(i, layer):
        src, dst = slabs[i]
        return pltpu.make_async_copy(kv_mine if src is None else src(my_head), dst(layer), loc_sem.at[i])

    def twin_copy(i, layer):
        src, dst = slabs[i]
        return remote(kv_twin if src is None else src(twin_head), dst(layer), push_send.at[i], push_recv.at[i], here.twin)

    k_copy = pltpu.make_async_copy(cut(w_in, Q_COLS, 128, place), k_pair, misc.at[0])
    v_copy = pltpu.make_async_copy(cut(w_in, Q_COLS + KV_COLS, 128, place), v_pair, misc.at[1])
    k_copy.start()
    v_copy.start()
    for i in (0, 1):
        twin_copy(i, core).start()
        own_copy(i, core).start()
    other_rows = pl.ds(pl.multiple_of((1 - core) * SLOT, SLOT), SLOT)
    cross_copy = remote(ends.at[other_rows], cross, misc_send.at[0], misc_recv.at[0], here.twin)
    cross_copy.start()
    gain_copy = remote(gain_in, gain_out.at[core], misc_send.at[1], misc_recv.at[1], here.twin)
    gain_copy.start()
    gain_out[core] = gain_in[...]
    k_copy.wait()
    v_copy.wait()
    low = low_lanes(k_pair.shape)
    k, v = k_pair[...].astype(F32), v_pair[...].astype(F32)
    kv0 = jnp.where(low, k, pltpu.roll(v, 64, 1)).astype(BF16)
    kv1 = jnp.where(low, pltpu.roll(k, 64, 1), v).astype(BF16)
    kv_mine[...] = jnp.where(core == 0, kv0, kv1)
    kv_twin[...] = jnp.where(core == 0, kv1, kv0)
    for i in (2, 3, 4, 5):
        twin_copy(i, core).start()
        own_copy(i, core).start()

    PIECES = ((wa, (0, 1, 2)), (wg, (3, 4)), (wd, (5,)))
    half = part // 2

    def own_ready(layer, piece):
        @pl.when(core == layer)
        def _():
            for i in PIECES[piece][1]:
                own_copy(i, layer).wait()

        @pl.when(core != layer)
        def _():
            for i in PIECES[piece][1]:
                twin_copy(i, layer).wait_recv()

    def hop(layer, piece, which, rows, size, peer):
        ref = PIECES[piece][0].at[layer, pl.ds(pl.multiple_of(rows, size), size)]
        return remote(ref, ref, hop_send.at[layer, piece, which], hop_recv.at[layer, piece, which], peer)

    def hops(layer, piece):
        return (
            hop(layer, piece, 0, shard * part, part, here.x_peer),
            hop(layer, piece, 1, shard * part, part, here.y_peer),
            hop(layer, piece, 2, here.x_shard * part, half, here.y_peer),
            hop(layer, piece, 3, here.y_shard * part + half, half, here.x_peer),
        )

    def hop_one(layer, piece):
        own_ready(layer, piece)
        one, two, _, _ = hops(layer, piece)
        one.start()
        two.start()

    def hop_two(layer, piece):
        one, two, three, four = hops(layer, piece)
        one.wait_recv()
        three.start()
        two.wait_recv()
        four.start()

    def all_in(layer, piece):
        _, _, three, four = hops(layer, piece)
        three.wait_recv()
        four.wait_recv()

    hop_one(0, 0)

    rows8 = lens_in.shape[0]
    lens[pl.ds(pl.multiple_of((core * LINE + place) * rows8, rows8), rows8), :] = lens_in[...]
    line_gather(here, lens, len_sems)
    cross_copy.wait()
    gain_copy.wait()
    first = core == 0
    ours0, others0 = ends[:SLOT].astype(F32), ends[SLOT:].astype(F32)
    crossed = cross[...].astype(F32)
    x = jnp.where(first, ours0, crossed)
    cot_out[...] = jnp.where(first, crossed, others0).astype(BF16)
    res[0] = x

    def own_block(ref):
        return ref.at[pl.ds(pl.multiple_of((core * LINE + place) * SLOT, SLOT), SLOT), :]

    def weight_out(layer, piece):
        dst = (wa_out, wg_out, wd_out)[piece].at[layer]
        return pltpu.make_async_copy(PIECES[piece][0].at[layer], dst, w_save.at[layer, piece])

    reduce_bufs = (sib_buf, rx_up, rx_dn, tx_up, tx_dn)
    half_rows = LINE * SLOT

    def layer(index):
        saves = []

        def keep(src, dst):
            copy = pltpu.make_async_copy(src, dst, save.at[index, len(saves)])
            copy.start()
            saves.append(copy)

        if index == 0:
            x = res[0]
        else:
            x = y_out[...].astype(F32)
            res[2] = x
        own_block(seq)[...] = (x * root(x) * gain_out[index, 0:1]).astype(BF16)
        line_gather(here, seq, gather_sems)
        keep(seq, xn_out.at[index])
        hop_two(index, 0)
        hop_one(index, 1 if index == 0 else 2)
        all_in(index, 0)
        weight_out(index, 0).start()

        def attend(pair, _):
            at = pl.ds(pl.multiple_of(pair * 2 * SLOT, 2 * SLOT), 2 * SLOT)
            wide = dot(seq[at, :], wa[index, :, :AO_AT])
            kv = turn(wide[:, KV_AT:AO_AT], tables[2], tables[3])
            q = jnp.concatenate(
                [turn(wide[:, 128 * i:128 * (i + 1)], tables[0], tables[1]) for i in range(GROUP // 2)], 1
            )
            kv_low = kv.astype(BF16)
            qkv[at, :Q_SLAB] = q.astype(BF16)
            qkv[at, KV_AT:AO_AT] = kv_low
            probs = two_slot_probs(spread_heads(q).astype(BF16), kv_low, lens, pair).astype(BF16)
            ctx[at, :] = join_heads(dot(probs, kv_low), True).astype(BF16)
            return 0

        lax.fori_loop(0, LINE, attend, 0)
        keep(qkv, qkv_out.at[index])
        keep(ctx, ctx_out.at[index])
        if index == 0:
            hop_one(0, 2)

        def terms(whose, src, weights, cols, dst):
            rows = pl.ds(pl.multiple_of(whose * half_rows, half_rows), half_rows)

            def tile(n, _):
                at = pl.ds(pl.multiple_of(n * 512, 512), 512)
                dst[:, at] = dot_last(src[rows, :], weights[index, at, cols]).astype(dst.dtype)
                return 0

            lax.fori_loop(0, width // 512, tile, 0)

        def reduce(src, weights, cols):
            terms(1 - core, src, weights, cols, theirs)
            line_reduce(here, total, ours, theirs, reduce_bufs, reduce_sems,
                        lambda: terms(core, src, weights, cols, ours))

        saves[0].wait()
        reduce(ctx, wa, slice(AO_AT, A_COLS))
        middle = x + total[...]
        res[1 + 2 * index] = middle
        own_block(hnb)[...] = (middle * root(middle) * gain_out[index, 1:2]).astype(BF16)
        line_gather(here, hnb, gather_sems)
        keep(hnb, hn_out.at[index])
        hop_two(index, 1)
        if index == 0:
            hop_one(1, 0)
        all_in(index, 1)
        weight_out(index, 1).start()

        def gate_up(n, _):
            at = pl.ds(pl.multiple_of(n * 256, 256), 256)
            at_up = pl.ds(pl.multiple_of(FF_SLAB + n * 256, 256), 256)
            gate = dot(hnb[...], wg[index, :, at])
            up = dot(hnb[...], wg[index, :, at_up])
            gu[:, at] = gate
            gu[:, at_up] = up
            hid[:, at] = (gate * jax.nn.sigmoid(gate) * up).astype(BF16)
            return 0

        lax.fori_loop(0, FF_SLAB // 256, gate_up, 0)
        keep(gu, gu_out.at[index])
        keep(hid, hid_out.at[index])
        hop_two(index, 2)
        if index == 0:
            hop_one(1, 1)
        all_in(index, 2)
        weight_out(index, 2).start()
        saves[3].wait()
        reduce(hid, wd, slice(None))
        y_out[...] = (res[1 + 2 * index] + total[...]).astype(BF16)
        for i in (1, 2, 4, 5):
            saves[i].wait()

    layer(0)
    layer(1)
    for i in range(4):
        pltpu.make_async_copy(res.at[i], res_out.at[i], misc.at[i]).start()
    for i in range(4):
        pltpu.make_async_copy(res.at[i], res_out.at[i], misc.at[i]).wait()
    for i in range(6):
        twin_copy(i, core).wait_send()
    for index in range(2):
        for piece in range(3):
            weight_out(index, piece).wait()
            for move in hops(index, piece):
                move.wait_send()


def forward_call(ends, lens, gain, tables, w_in, w_out):
    width = ends.shape[1]
    rows = LINE * CORES * SLOT
    hbm = pl.BlockSpec(memory_space=pl.ANY)
    vmem = pl.BlockSpec(memory_space=pltpu.VMEM)
    shape = jax.ShapeDtypeStruct
    dma = pltpu.SemaphoreType.DMA
    line = dma((LINE,))
    block = pltpu.VMEM((LINE * SLOT, width), BF16)
    return pl.pallas_call(
        forward_body,
        out_shape=[
            shape((2, width, A_COLS), BF16),
            shape((2, width, 2 * FF_SLAB), BF16),
            shape((2, width, FF_SLAB), BF16),
            shape((2, rows, width), BF16),
            shape((2, rows, width), BF16),
            shape((2, rows, AO_AT), BF16),
            shape((2, rows, Q_SLAB), BF16),
            shape((2, rows, 2 * FF_SLAB), F32),
            shape((2, rows, FF_SLAB), BF16),
            shape((4, SLOT, width), F32),
            shape((SLOT, width), BF16),
            shape((SLOT, width), BF16),
            shape((2, 2, width), F32),
            shape((LINE * CORES * 8, 128), F32),
        ],
        in_specs=[vmem, vmem, vmem, vmem, hbm, hbm],
        out_specs=[hbm] * 10 + [vmem] * 4,
        scratch_shapes=[
            pltpu.VMEM((SLOT, width), BF16),
            pltpu.VMEM((w_in.shape[0], 128), BF16),
            pltpu.VMEM((w_in.shape[0], 128), BF16),
            pltpu.VMEM((w_in.shape[0], 128), BF16),
            pltpu.VMEM((w_in.shape[0], 128), BF16),
            pltpu.VMEM((2, width, A_COLS), BF16),
            pltpu.VMEM((2, width, 2 * FF_SLAB), BF16),
            pltpu.VMEM((2, width, FF_SLAB), BF16),
            pltpu.VMEM((rows, width), BF16),
            pltpu.VMEM((rows, width), BF16),
            pltpu.VMEM((rows, AO_AT), BF16),
            pltpu.VMEM((rows, Q_SLAB), BF16),
            pltpu.VMEM((rows, 2 * FF_SLAB), F32),
            pltpu.VMEM((rows, FF_SLAB), BF16),
            block,
            pltpu.VMEM((LINE * SLOT, width), F32),
            pltpu.VMEM((4, SLOT, width), F32),
            pltpu.VMEM((SLOT, width), F32),
            block, block, block, block, block,
            dma((6,)), dma((6,)), dma((6,)), dma((2, 3, 4)), dma((2, 3, 4)),
            dma((4,)), dma((2,)), dma((2,)), dma((2, 6)), dma((2, 3)),
        ] + [line] * 16,
        compiler_params=pltpu.CompilerParams(
            collective_id=0, has_side_effects=True, vmem_limit_bytes=60 * 2**20
        ),
        name="forward_two_layers",
        cost_estimate=pl.CostEstimate(flops=16_000_000_000, bytes_accessed=600_000_000, transcendentals=0),
    )(ends, lens, gain, tables, w_in, w_out)


def spread_heads_high(wide):
    low = low_lanes((wide.shape[0], 128))
    parts = []
    for pair in range(GROUP // 2):
        block = wide[:, pair * 128:(pair + 1) * 128]
        parts.append(jnp.where(low, 0.0, pltpu.roll(block, 64, 1)))
        parts.append(jnp.where(low, 0.0, block))
    return jnp.concatenate(parts, 0)


CHUNKS = ((0, FF_SLAB), (FF_SLAB, FF_SLAB), (2 * FF_SLAB, FF_SLAB), (3 * FF_SLAB, A_COLS))
SLAB = 3 * FF_SLAB + A_COLS


def backward_body(
    replicas,
    cot_in, y_in, gain, lens, tables, res_in, wa_in, wg_in, wd_in, xn_in, hn_in, qkv_in, ctx_in, gu_in, hid_in,
    fin, ends_out, gain_out, far_rx, near_rx,
    wa, wg, wd, xn, hn, qkv, ctx, gu, hid, dm, da, dgu, dqkv, theirs, ours, total, res,
    sib_buf, rx_up, rx_dn, tx_up, tx_dn, tx_far, tx_x, tx_y, tx_fin, stage, gain_loc, gain_x, gain_y, gain_line,
    end_tx, end_rx,
    load_sem, gu_sem, res_sem, far_send, far_recv, near_send, near_recv, fin_send, fin_recv, stage_sem, misc_send, misc_recv,
    *line_sems,
):
    gather_sems, gain_sems, reduce_sems = line_sems[:5], line_sems[5:10], line_sems[10:]
    here = Here()
    core, shard, place = here.core, here.shard, here.place
    width = cot_in.shape[1]
    part = width // SHARDS
    half = part // 2
    half_rows = LINE * SLOT
    base = here.depth - place

    barrier = pltpu.get_barrier_semaphore()
    for peer in (here.x_peer, here.y_peer):
        pl.semaphore_signal(barrier, inc=1, device_id=peer)
    for other in range(CORES):
        for where in range(LINE):
            @pl.when((core != other) | (place != where))
            def _():
                pl.semaphore_signal(barrier, inc=1, device_id={"section": other, "dp": base + where})

    pl.semaphore_wait(barrier, 2 + CORES * LINE - 1)

    NAMES = ("wd", "wg", "wa", "hid", "qkv", "ctx", "hn", "xn")
    VIEWS = {
        "wd": (wd_in, lambda l: wd), "wg": (wg_in, lambda l: wg), "wa": (wa_in, lambda l: wa),
        "hid": (hid_in, lambda l: hid), "qkv": (qkv_in, lambda l: qkv.at[l]), "ctx": (ctx_in, lambda l: ctx.at[l]),
        "hn": (hn_in, lambda l: hn), "xn": (xn_in, lambda l: xn),
    }

    def load(name, layer):
        src, dst = VIEWS[name]
        return pltpu.make_async_copy(src.at[layer], dst(layer), load_sem.at[layer, NAMES.index(name)])

    def gu_loads(layer, tile):
        return [
            pltpu.make_async_copy(
                gu_in.at[layer, :, pl.ds(i * FF_SLAB + tile * 256, 256)],
                gu.at[tile % 2, :, pl.ds(i * 256, 256)], gu_sem.at[tile % 2, i])
            for i in range(2)
        ]

    for tile in range(2):
        for copy in gu_loads(1, tile):
            copy.start()
    for name in NAMES:
        load(name, 1).start()

    ready = set()

    def need(name, layer):
        if (name, layer) not in ready:
            ready.add((name, layer))
            load(name, layer).wait()

    gain_loc[...] = jnp.zeros_like(gain_loc)

    pending = {}

    def claim(key):
        for move in pending.pop(key, ()):
            move.wait_send()

    def products(layer, chunk, block, put):
        at = pl.ds(pl.multiple_of(block * part, part), part)
        need("hn" if chunk < 2 else "hid" if chunk == 2 else "xn", layer)

        def tiles(lhs, rhs, size, to):
            for lo in range(0, size, 512):
                hi = min(lo + 512, size)
                put(slice(to + lo, to + hi), dot_rows(lhs[:, at], rhs[:, lo:hi]))

        if chunk < 2:
            tiles(hn, dgu.at[layer, :, pl.ds(chunk * FF_SLAB, FF_SLAB)], FF_SLAB, 0)
        elif chunk == 2:
            tiles(dm.at[layer], hid, FF_SLAB, 0)
        else:
            tiles(xn, dqkv.at[layer], AO_AT, 0)
            tiles(da.at[layer], ctx.at[layer], Q_SLAB, AO_AT)

    def far_moves(layer, chunk):
        lo, size = CHUNKS[chunk]
        src = tx_far.at[chunk % 2]
        cols = pl.ds(0, size)
        return [
            remote(src.at[pl.ds(i * half, half), cols], far_rx.at[layer, i, :, pl.ds(lo, size)],
                   far_send.at[layer, chunk, i], far_recv.at[layer, chunk, i], peer)
            for i, peer in ((0, here.x_peer), (1, here.y_peer))
        ]

    def near_moves(layer, chunk):
        lo, size = CHUNKS[chunk]
        cols = pl.ds(0, size)
        return [
            remote(src.at[chunk % 2, :, cols], near_rx.at[layer, i, :, pl.ds(lo, size)],
                   near_send.at[layer, chunk, i], near_recv.at[layer, chunk, i], peer)
            for i, (src, peer) in enumerate(((tx_x, here.x_peer), (tx_y, here.y_peer)))
        ]

    def stage_far(layer, chunk, i):
        lo, size = CHUNKS[chunk]
        return pltpu.make_async_copy(
            far_rx.at[layer, i, :, pl.ds(lo, size)], stage.at[i, pl.ds(0, half), pl.ds(0, size)], stage_sem.at[i])

    def stage_near(layer, chunk, i):
        lo, size = CHUNKS[chunk]
        return pltpu.make_async_copy(
            near_rx.at[layer, i, :, pl.ds(lo, size)], stage.at[i, :, pl.ds(0, size)], stage_sem.at[i])

    def step_one(layer, chunk):
        claim(("far", chunk % 2))

        def put(cols, value):
            tx_far[chunk % 2, :, cols] = value.astype(BF16)

        products(layer, chunk, here.far_shard, put)
        moves = far_moves(layer, chunk)
        for move in moves:
            move.start()
        pending["far", chunk % 2] = moves

    def step_two(layer, chunk):
        arrivals = far_moves(layer, chunk)
        for i in (1, 0):
            arrivals[i].wait_recv()
            stage_far(layer, chunk, i).start()
        claim(("near", chunk % 2))
        moves = near_moves(layer, chunk)

        def put_x(cols, value):
            tx_x[chunk % 2, :half, cols] = value[:half].astype(BF16)
            tx_x[chunk % 2, half:, cols] = (value[half:] + stage[1, :half, cols].astype(F32)).astype(BF16)

        def put_y(cols, value):
            tx_y[chunk % 2, :half, cols] = (value[:half] + stage[0, :half, cols].astype(F32)).astype(BF16)
            tx_y[chunk % 2, half:, cols] = value[half:].astype(BF16)

        stage_far(layer, chunk, 1).wait()
        products(layer, chunk, here.x_shard, put_x)
        moves[0].start()
        stage_far(layer, chunk, 0).wait()
        products(layer, chunk, here.y_shard, put_y)
        moves[1].start()
        pending["near", chunk % 2] = moves

    piece = part // (replicas * LINE)

    def fin_moves(layer, chunk):
        lo, size = CHUNKS[chunk]
        head = place * CORES + core
        moves = []
        for rep in range(replicas):
            for where in range(LINE):
                src = tx_fin.at[chunk % 2, pl.ds((rep * LINE + where) * piece, piece), pl.ds(0, size)]
                dst = fin.at[head, pl.ds(rep * piece, piece), pl.ds(lo, size)]
                same = (core == layer) & (place == where)
                move = remote(src, dst, fin_send.at[layer, chunk, rep, where], fin_recv.at[rep, head, chunk],
                              {"section": layer, "dp": base + where})
                stay = pltpu.make_async_copy(src, dst, fin_send.at[layer, chunk, rep, where])
                moves.append((same, move, stay))
        return moves

    class Leave:
        def __init__(self, entry):
            self.same, self.move, self.stay = entry

        def start(self):
            @pl.when(self.same)
            def _():
                self.stay.start()

            @pl.when(jnp.logical_not(self.same))
            def _():
                self.move.start()

        def wait_send(self):
            @pl.when(self.same)
            def _():
                self.stay.wait()

            @pl.when(jnp.logical_not(self.same))
            def _():
                self.move.wait_send()

    def step_three(layer, chunk):
        arrivals = near_moves(layer, chunk)
        for i in range(2):
            arrivals[i].wait_recv()
            stage_near(layer, chunk, i).start()
        claim(("fin", chunk % 2))
        stage_near(layer, chunk, 0).wait()
        stage_near(layer, chunk, 1).wait()

        def put(cols, value):
            tx_fin[chunk % 2, :, cols] = (
                value + stage[0, :, cols].astype(F32) + stage[1, :, cols].astype(F32)
            ).astype(BF16)

        products(layer, chunk, shard, put)
        moves = [Leave(entry) for entry in fin_moves(layer, chunk)]
        for move in moves:
            move.start()
        pending["fin", chunk % 2] = moves

    def steps(*todo):
        def run():
            for kind, layer, chunk in todo:
                (step_one, step_two, step_three)[kind - 1](layer, chunk)
                if layer == 1 and kind == 3 and chunk == 1:
                    load("hn", 0).start()
                if layer == 1 and kind == 3 and chunk == 2:
                    load("hid", 0).start()
                if layer == 1 and kind == 3 and chunk == 3:
                    load("xn", 0).start()
        return run

    reduce_bufs = (sib_buf, rx_up, rx_dn, tx_up, tx_dn)

    def own_block(ref, layer):
        return ref.at[layer, pl.ds(pl.multiple_of((core * LINE + place) * SLOT, SLOT), SLOT), :]

    def terms(whose, src, weights, cols, dst):
        rows = pl.ds(pl.multiple_of(whose * half_rows, half_rows), half_rows)

        def tile(n, _):
            at = pl.ds(pl.multiple_of(n * 512, 512), 512)
            dst[:, at] = dot_last(src[rows, :], weights[at, cols]).astype(dst.dtype)
            return 0

        lax.fori_loop(0, width // 512, tile, 0)

    def reduce(slot, src, weights, cols, meanwhile):
        res_load(slot).start()
        terms(1 - core, src, weights, cols, theirs)
        line_reduce(here, total, ours, theirs, reduce_bufs, reduce_sems,
                    lambda: terms(core, src, weights, cols, ours), meanwhile)

    def res_load(slot):
        return pltpu.make_async_copy(res_in.at[slot], res, res_sem.at[slot])

    def norm_back(gain_row, slot):
        res_load(slot).wait()
        values = res[...]
        scale = root(values)
        grad = total[...]
        hat = grad * gain_row
        gain_loc[slot:slot + 1, :] = jnp.sum(grad * values * scale, 0, keepdims=True)
        inner = jnp.mean(hat * values, -1, keepdims=True)
        return scale * hat - values * (scale * scale * scale * inner)

    def layer_back(layer, grad_out, jobs):
        own_block(dm, layer)[...] = grad_out.astype(BF16)
        line_gather(here, dm.at[layer], gather_sems, jobs[0])
        need("wd", layer)
        tiles = FF_SLAB // 256
        for tile in range(tiles):
            at = slice(tile * 256, tile * 256 + 256)
            at_up = slice(FF_SLAB + tile * 256, FF_SLAB + tile * 256 + 256)
            grad = dot(dm[layer], wd[:, at])
            for copy in gu_loads(layer, tile):
                copy.wait()
            gate, up = gu[tile % 2, :, :256], gu[tile % 2, :, 256:]
            sig = jax.nn.sigmoid(gate)
            dgu[layer, :, at] = (grad * up * sig * (1.0 + gate * (1.0 - sig))).astype(BF16)
            dgu[layer, :, at_up] = (grad * gate * sig).astype(BF16)
            ahead = (layer, tile + 2) if tile + 2 < tiles else (layer - 1, tile + 2 - tiles)
            if ahead[0] >= 0:
                for copy in gu_loads(*ahead):
                    copy.start()
        need("wg", layer)
        if layer == 1:
            load("wd", 0).start()
        reduce(2 * layer + 1, dgu.at[layer], wg, slice(None), jobs[1])
        if layer == 1:
            load("wg", 0).start()
        grad_mid = grad_out + norm_back(gain[layer, 1:2], 2 * layer + 1)
        own_block(da, layer)[...] = grad_mid.astype(BF16)
        line_gather(here, da.at[layer], gather_sems, jobs[2])
        need("wa", layer)
        need("qkv", layer)
        need("ctx", layer)

        def attend(pair, _):
            at = pl.ds(pl.multiple_of(pair * 2 * SLOT, 2 * SLOT), 2 * SLOT)
            grad_ctx = dot(da[layer, at, :], wa[:, AO_AT:A_COLS]).astype(BF16).astype(F32)
            kv = qkv[layer, at, KV_AT:AO_AT]
            q = spread_heads(qkv[layer, at, :Q_SLAB].astype(F32)).astype(BF16)
            probs = two_slot_probs(q, kv, lens, pair)
            grad_high = spread_heads_high(grad_ctx).astype(BF16)
            grad_probs = dot_last(grad_high, kv)
            inner = jnp.sum(grad_probs * probs, -1, keepdims=True)
            grad_scores = (probs * (grad_probs - inner)).astype(BF16)
            grad_q = join_heads(dot(grad_scores, kv), False) * HEAD_DIM**-0.5
            grad_kv = dot_rows(grad_scores, q) * HEAD_DIM**-0.5 + dot_rows(probs.astype(BF16), grad_high)
            for i in range(GROUP // 2):
                cols = slice(128 * i, 128 * (i + 1))
                dqkv[layer, at, cols] = turn(grad_q[:, cols], tables[0], -tables[1]).astype(BF16)
            dqkv[layer, at, KV_AT:AO_AT] = turn(grad_kv, tables[2], -tables[3]).astype(BF16)
            return 0

        lax.fori_loop(0, LINE, attend, 0)
        reduce(2 * layer, dqkv.at[layer], wa, slice(0, AO_AT), jobs[3])
        if layer == 1:
            load("wa", 0).start()
            load("qkv", 0).start()
            load("ctx", 0).start()
        return grad_mid + norm_back(gain[layer, 0:1], 2 * layer)

    own_len = lens[pl.ds(pl.multiple_of((core * LINE + place) * 8, 8), 8), :][:1]
    live = lax.broadcasted_iota(jnp.int32, (SLOT, 128), 0).astype(F32) < own_len
    valid = jnp.where(live, 1.0, 0.0)[:, :1]
    dx1 = layer_back(1, cot_in[...].astype(F32) * valid, (
        (),
        (steps((1, 1, 0)), steps((1, 1, 1)), steps((1, 1, 2))),
        (steps((2, 1, 0)), None, steps((2, 1, 1))),
        (steps((2, 1, 2)), steps((1, 1, 3)), steps((3, 1, 0))),
    ))
    dx0 = layer_back(0, dx1.astype(BF16).astype(F32), (
        (steps((2, 1, 3)), steps((3, 1, 1)), None),
        (steps((1, 0, 0)), steps((3, 1, 2)), steps((1, 0, 1))),
        (steps((1, 0, 2)), steps((2, 0, 0), (3, 1, 3)), steps((2, 0, 1))),
        (steps((2, 0, 2)), steps((1, 0, 3)), steps((3, 0, 0))),
    ))

    first = core == 0
    dx0 = dx0.astype(BF16).astype(F32)
    y1 = y_in[...].astype(F32)
    end_tx[...] = jnp.where(first, y1, dx0).astype(BF16)
    end_move = remote(end_tx, end_rx, misc_send.at[0], misc_recv.at[0], here.twin)
    end_move.start()

    gain_x_move = remote(gain_loc, gain_x, misc_send.at[1], misc_recv.at[1], here.x_peer)
    gain_x_move.start()
    steps((2, 0, 3))()
    gain_x_move.wait()
    gain_loc[...] += gain_x[...]
    gain_y_move = remote(gain_loc, gain_y, misc_send.at[2], misc_recv.at[2], here.y_peer)
    gain_y_move.start()
    steps((3, 0, 1))()
    gain_y_move.wait()
    cols = pl.ds(pl.multiple_of(shard * part, part), part)
    own_gains = pl.ds(pl.multiple_of((core * LINE + place) * 8, 8), 8)
    gain_line[own_gains, :] = gain_loc[:, cols] + gain_y[:, cols]
    line_gather(here, gain_line, gain_sems)
    gain_sum = gain_line[0:8, :]
    for i in range(1, LINE * CORES):
        gain_sum += gain_line[8 * i:8 * i + 8, :]
    gain_out[...] = gain_sum
    end_move.wait()
    crossed = end_rx[...].astype(F32)
    ends_out[:SLOT] = jnp.where(first, dx0, crossed).astype(BF16)
    ends_out[SLOT:] = jnp.where(first, crossed, y1).astype(BF16)
    steps((3, 0, 2))()
    steps((3, 0, 3))()
    for key in list(pending):
        claim(key)
    for rep in range(replicas):
        for where in range(LINE):
            for other in range(CORES):
                head = where * CORES + other

                @pl.when((core != other) | (place != where))
                def _():
                    for chunk, (lo, size) in enumerate(CHUNKS):
                        src = tx_fin.at[0, pl.ds(0, piece), pl.ds(0, size)]
                        dst = fin.at[head, pl.ds(rep * piece, piece), pl.ds(lo, size)]
                        remote(src, dst, fin_send.at[0, 0, 0, 0], fin_recv.at[rep, head, chunk], here.twin).wait_recv()


def backward_call(replicas, cot, y, gain, lens, tables, res, wa, wg, wd, xn, hn, qkv, ctx, gu, hid):
    width = cot.shape[1]
    rows = LINE * CORES * SLOT
    part = width // SHARDS
    hbm = pl.BlockSpec(memory_space=pl.ANY)
    vmem = pl.BlockSpec(memory_space=pltpu.VMEM)
    shape = jax.ShapeDtypeStruct
    dma = pltpu.SemaphoreType.DMA
    line = dma((LINE,))
    vm = pltpu.VMEM
    block = vm((LINE * SLOT, width), BF16)
    move = vm((2, part, FF_SLAB), BF16)
    return pl.pallas_call(
        functools.partial(backward_body, replicas),
        out_shape=[
            shape((KV_HEADS, part // LINE, SLAB), BF16),
            shape((CORES * SLOT, width), BF16),
            shape((8, part), F32),
            shape((2, 2, part // 2, SLAB), BF16),
            shape((2, 2, part, SLAB), BF16),
        ],
        in_specs=[vmem] * 5 + [hbm] * 10,
        out_specs=[hbm, vmem, vmem, hbm, hbm],
        scratch_shapes=[
            vm((width, A_COLS), BF16), vm((width, 2 * FF_SLAB), BF16), vm((width, FF_SLAB), BF16),
            vm((rows, width), BF16), vm((rows, width), BF16), vm((2, rows, AO_AT), BF16), vm((2, rows, Q_SLAB), BF16),
            vm((2, rows, 512), F32), vm((rows, FF_SLAB), BF16),
            vm((2, rows, width), BF16), vm((2, rows, width), BF16),
            vm((2, rows, 2 * FF_SLAB), BF16), vm((2, rows, AO_AT), BF16),
            block, vm((LINE * SLOT, width), F32), vm((SLOT, width), F32), vm((SLOT, width), F32),
            block, block, block, block, block,
            move, move, move, move, move,
            vm((8, width), F32), vm((8, width), F32), vm((8, width), F32), vm((8 * LINE * CORES, part), F32),
            vm((SLOT, width), BF16), vm((SLOT, width), BF16),
            dma((2, 8)), dma((2, 2)), dma((4,)), dma((2, 4, 2)), dma((2, 4, 2)), dma((2, 4, 2)), dma((2, 4, 2)),
            dma((2, 4, replicas, LINE)), dma((replicas, KV_HEADS, 4)), dma((2,)), dma((3,)), dma((3,)),
        ] + [line] * 16,
        compiler_params=pltpu.CompilerParams(
            collective_id=1, has_side_effects=True, vmem_limit_bytes=61 * 2**20
        ),
        name="backward_two_layers",
        cost_estimate=pl.CostEstimate(flops=32_000_000_000, bytes_accessed=600_000_000, transcendentals=0),
    )(cot, y, gain, lens, tables, res, wa, wg, wd, xn, hn, qkv, ctx, gu, hid)


def place_body(fin, in_out, out_out, held, wide_in, wide_out, load_sem, save_sem):
    steps = KV_HEADS // 2
    q_two, ff_two = 2 * Q_SLAB, 2 * FF_SLAB
    ff0 = Q_COLS + 2 * KV_COLS

    def fetch(step):
        return pltpu.make_async_copy(fin.at[pl.ds(2 * step, 2)], held.at[step % 2], load_sem.at[step % 2])

    def saves(step):
        slot = step % 2
        moves = []
        for i, (src, lo, dst, to, size) in enumerate((
            (wide_in, 0, in_out, step * q_two, q_two),
            (wide_in, q_two, in_out, Q_COLS + step * 128, 128),
            (wide_in, q_two + 128, in_out, Q_COLS + KV_COLS + step * 128, 128),
            (wide_in, q_two + 256, in_out, ff0 + step * ff_two, ff_two),
            (wide_in, q_two + 256 + ff_two, in_out, ff0 + FF + step * ff_two, ff_two),
            (wide_out, 0, out_out, step * q_two, q_two),
            (wide_out, q_two, out_out, Q_COLS + step * ff_two, ff_two),
        )):
            moves.append(pltpu.make_async_copy(
                src.at[slot, :, pl.ds(lo, size)], dst.at[:, pl.ds(to, size)], save_sem.at[slot, i]))
        return moves

    fetch(0).start()
    a_at = 3 * FF_SLAB
    for step in range(steps):
        slot = step % 2
        if step + 1 < steps:
            fetch(step + 1).start()
        fetch(step).wait()
        if step >= 2:
            for move in saves(step - 2):
                move.wait()
        for i in range(2):
            q_to = i * Q_SLAB
            wide_in[slot, :, q_to:q_to + Q_SLAB] = held[slot, i, :, a_at:a_at + Q_SLAB].astype(F32)
            wide_out[slot, :, q_to:q_to + Q_SLAB] = held[slot, i, :, a_at + AO_AT:a_at + A_COLS].astype(F32)
            for k, (src_ref, to) in enumerate(((wide_in, q_two + 256), (wide_in, q_two + 256 + ff_two), (wide_out, q_two))):
                at = to + i * FF_SLAB
                src_ref[slot, :, at:at + FF_SLAB] = held[slot, i, :, k * FF_SLAB:(k + 1) * FF_SLAB].astype(F32)
        one = held[slot, 0, :, a_at + KV_AT:a_at + AO_AT].astype(F32)
        two = held[slot, 1, :, a_at + KV_AT:a_at + AO_AT].astype(F32)
        low = low_lanes(one.shape)
        wide_in[slot, :, q_two:q_two + 128] = jnp.where(low, one, pltpu.roll(two, 64, 1))
        wide_in[slot, :, q_two + 128:q_two + 256] = jnp.where(low, pltpu.roll(one, 64, 1), two)
        for move in saves(step):
            move.start()
    for step in range(max(steps - 2, 0), steps):
        for move in saves(step):
            move.wait()


def place_call(fin, in_cols, out_cols):
    rows = fin.shape[1]
    hbm = pl.BlockSpec(memory_space=pl.ANY)
    q_two, ff_two = 2 * Q_SLAB, 2 * FF_SLAB
    return pl.pallas_call(
        place_body,
        out_shape=[jax.ShapeDtypeStruct((rows, in_cols), F32), jax.ShapeDtypeStruct((rows, out_cols), F32)],
        in_specs=[hbm],
        out_specs=[hbm, hbm],
        scratch_shapes=[
            pltpu.VMEM((2, 2, rows, SLAB), BF16),
            pltpu.VMEM((2, rows, q_two + 256 + 2 * ff_two), F32),
            pltpu.VMEM((2, rows, q_two + ff_two), F32),
            pltpu.SemaphoreType.DMA((2,)),
            pltpu.SemaphoreType.DMA((2, 7)),
        ],
        compiler_params=pltpu.CompilerParams(vmem_limit_bytes=32 * 2**20),
        name="place_columns",
    )(fin)


def rope_blocks():
    half_dim = HEAD_DIM // 2
    inverse = 500000.0 ** (-(jnp.arange(half_dim, dtype=F32) * 2.0 / HEAD_DIM))
    angles = jnp.arange(SLOT, dtype=F32)[:, None] * inverse[None, :]
    cos, sin = jnp.cos(angles), jnp.sin(angles)
    one, zero = jnp.ones((SLOT, HEAD_DIM), F32), jnp.zeros((SLOT, HEAD_DIM), F32)
    rows = [
        jnp.concatenate([cos] * 4, 1),
        jnp.concatenate([-sin, sin] * 2, 1),
        jnp.concatenate([cos, cos, one], 1),
        jnp.concatenate([-sin, sin, zero], 1),
    ]
    return jnp.stack([jnp.tile(block, (2, 1)) for block in rows])


def local(ends_in, in_weight, out_weight, norm_gain, seq_len):
    core = lax.axis_index("section")
    replicas = lax.axis_size("dp") // LINE
    own_length = jnp.where(core == 0, seq_len[0], seq_len[1])
    lens_block = jnp.full((8, 128), own_length.astype(F32))
    rope = rope_blocks()
    (wa, wg, wd, xn, hn, qkv, ctx, gu, hid, res, y1, cot, gains, lens) = forward_call(
        ends_in[0], lens_block, norm_gain[0], rope, in_weight[0], out_weight[0]
    )
    fin, ends_out, gain_sum, _, _ = backward_call(
        replicas, cot, y1, gains, lens, rope, res, wa, wg, wd, xn, hn, qkv, ctx, gu, hid
    )
    own_gain = lax.dynamic_slice_in_dim(gain_sum, 2 * core, 2, 0)
    if replicas > 1:
        groups = [[r * LINE + p for r in range(replicas)] for p in range(LINE)]
        fin = lax.psum_scatter(fin, "dp", scatter_dimension=1, tiled=True, axis_index_groups=groups)
        own_gain = lax.psum(own_gain, "dp", axis_index_groups=groups)
    in_grad, out_grad = place_call(fin, in_weight.shape[2], out_weight.shape[2])
    size = own_gain.shape[1] // lax.axis_size("dp")
    own_gain = lax.dynamic_slice_in_dim(own_gain, lax.axis_index("dp") * size, size, 1)
    return ends_out[None], in_grad[None], out_grad[None], own_gain[None]


def solution(mesh):
    in_specs = (
        P("section", ("shard", "dp"), None),
        P("section", "shard", None),
        P("section", "shard", None),
        P("section", None, None),
        P(("shard", "dp")),
    )
    out_specs = (
        P("section", ("shard", "dp"), None),
        P("section", ("shard", "dp"), None),
        P("section", ("shard", "dp"), None),
        P("section", None, ("shard", "dp")),
    )
    return jax.shard_map(local, mesh=mesh, in_specs=in_specs, out_specs=out_specs, check_vma=False)
```

```python
import functools

import jax
import jax.numpy as jnp
from jax import lax
from jax.experimental import pallas as pl
from jax.experimental.pallas import tpu as pltpu
from jax.sharding import PartitionSpec as P

HEADS = 32
KV_HEADS = 8
GROUP = HEADS // KV_HEADS
HEAD_DIM = 64
FF = 8192
EPSILON = 1e-05
BF16 = jnp.bfloat16
F32 = jnp.float32
CORES = 2
LINE = KV_HEADS // CORES
SHARDS = 4
SLOT = 64
SUBS = 2
Q_SLAB = GROUP * HEAD_DIM
QKV_SLAB = Q_SLAB + 2 * HEAD_DIM
FF_SLAB = FF // KV_HEADS
Q_COLS = HEADS * HEAD_DIM
KV_COLS = KV_HEADS * HEAD_DIM


class Here:
    def __init__(self):
        self.core = lax.axis_index("section")
        self.shard = lax.axis_index("shard")
        self.depth = lax.axis_index("dp")
        self.place = lax.rem(self.depth, LINE)
        self.twin = {"section": 1 - self.core}
        self.x_shard = self.shard + 1 - 2 * lax.rem(self.shard, 2)
        self.y_shard = lax.rem(self.shard + 2, SHARDS)
        self.far_shard = SHARDS - 1 - self.shard
        self.x_peer = {"shard": self.x_shard}
        self.y_peer = {"shard": self.y_shard}
        self.above = {"dp": self.depth + 1}
        self.below = {"dp": self.depth - 1}
        self.has_above = self.place < LINE - 1
        self.has_below = self.place > 0

    def greet(self):
        barrier = pltpu.get_barrier_semaphore()
        for peer in (self.twin, self.x_peer, self.y_peer):
            pl.semaphore_signal(barrier, inc=1, device_id=peer)

        @pl.when(self.has_above)
        def _():
            pl.semaphore_signal(barrier, inc=1, device_id=self.above)

        @pl.when(self.has_below)
        def _():
            pl.semaphore_signal(barrier, inc=1, device_id=self.below)

        pl.semaphore_wait(barrier, jnp.where(self.has_above & self.has_below, 5, 4))


def remote(src, dst, send, recv, device):
    return pltpu.make_async_remote_copy(src, dst, send, recv, device_id=device)


def rows_at(ref, start, size):
    return ref.at[pl.ds(pl.multiple_of(start, size), size)]


def line_gather(here, buf, sems, meanwhile=(), subs=SUBS):
    up_send, dn_send, sib_send, z_recv, sib_recv = sems
    rows = buf.shape[0] // (LINE * CORES)
    size = rows // subs
    core, place = here.core, here.place
    meanwhile = list(meanwhile) + [None] * (LINE + 1)

    def part(where, whose, sub):
        return rows_at(buf, (whose * LINE + where) * rows + sub * size, size)

    def up(where, sub):
        mine = part(where, core, sub)
        return remote(mine, mine, up_send.at[where, sub], z_recv.at[where, sub], here.above)

    def down(where, sub):
        mine = part(where, core, sub)
        return remote(mine, mine, dn_send.at[where, sub], z_recv.at[where, sub], here.below)

    def across(where, whose, sub):
        mine = part(where, whose, sub)
        return remote(mine, mine, sib_send.at[where, sub], sib_recv.at[where, sub], here.twin)

    for sub in range(subs):
        @pl.when(here.has_above)
        def _():
            up(place, sub).start()

        @pl.when(here.has_below)
        def _():
            down(place, sub).start()

    for sub in range(subs):
        across(place, core, sub).start()
    for step in range(1, LINE):
        if meanwhile[step - 1] is not None:
            meanwhile[step - 1]()
        for sub in range(subs):
            @pl.when(place >= step)
            def _():
                up(place - step, sub).wait_recv()

                @pl.when(here.has_above)
                def _():
                    up(place - step, sub).start()

                across(place - step, core, sub).start()

            @pl.when(place + step < LINE)
            def _():
                down(place + step, sub).wait_recv()

                @pl.when(here.has_below)
                def _():
                    down(place + step, sub).start()

                across(place + step, core, sub).start()

    if meanwhile[LINE - 1] is not None:
        meanwhile[LINE - 1]()
    for where in range(LINE):
        for sub in range(subs):
            across(where, 1 - core, sub).wait_recv()

    for where in range(LINE):
        for sub in range(subs):
            across(where, core, sub).wait_send()

            @pl.when((where <= place) & here.has_above)
            def _():
                up(where, sub).wait_send()

            @pl.when((where >= place) & here.has_below)
            def _():
                down(where, sub).wait_send()


def line_reduce(here, out, ours, theirs, bufs, sems, terms, meanwhile=()):
    sib_buf, rx_up, rx_dn, tx_up, tx_dn = bufs
    sib_send, sib_recv, up_send, up_recv, dn_send, dn_recv = sems
    rows, width = out.shape
    size = width // SUBS
    place, core = here.place, here.core
    meanwhile = list(meanwhile) + [None] * (LINE + 1)

    def cols(sub):
        return slice(sub * size, (sub + 1) * size)

    def part(ref, where, sub):
        return ref.at[pl.ds(pl.multiple_of(where * rows, rows), rows), pl.ds(sub * size, size)]

    def read(ref, where, sub):
        return ref[pl.ds(pl.multiple_of(where * rows, rows), rows), cols(sub)].astype(F32)

    def across(where, sub):
        return remote(part(theirs, where, sub), part(sib_buf, where, sub),
                      sib_send.at[where, sub], sib_recv.at[where, sub], here.twin)

    def up(where, sub):
        return remote(part(tx_up, where, sub), part(rx_up, where, sub),
                      up_send.at[where, sub], up_recv.at[where, sub], here.above)

    def down(where, sub):
        return remote(part(tx_dn, where, sub), part(rx_dn, where, sub),
                      dn_send.at[where, sub], dn_recv.at[where, sub], here.below)

    def summed(where, sub):
        return read(ours, where, sub) + read(sib_buf, where, sub)

    def put(ref, where, sub, value):
        ref[pl.ds(pl.multiple_of(where * rows, rows), rows), cols(sub)] = value.astype(BF16)

    def begin(sub):
        terms(1 - core, theirs, sub)
        for step in range(LINE - 1, 0, -1):
            @pl.when(place + step < LINE)
            def _():
                across(place + step, sub).start()

            @pl.when(place >= step)
            def _():
                across(place - step, sub).start()

        across(place, sub).start()
        terms(core, ours, sub)

    def turn_on(step, sub):
        @pl.when(place + step < LINE)
        def _():
            where = place + step
            across(where, sub).wait_recv()

            @pl.when(here.has_below)
            def _():
                up(where, sub).wait_recv()
                put(tx_up, where, sub, summed(where, sub) + read(rx_up, where, sub))

            @pl.when(place == 0)
            def _():
                put(tx_up, where, sub, summed(where, sub))

            up(where, sub).start()

        @pl.when(place >= step)
        def _():
            where = place - step
            across(where, sub).wait_recv()

            @pl.when(here.has_above)
            def _():
                down(where, sub).wait_recv()
                put(tx_dn, where, sub, summed(where, sub) + read(rx_dn, where, sub))

            @pl.when(place == LINE - 1)
            def _():
                put(tx_dn, where, sub, summed(where, sub))

            down(where, sub).start()

    for sub in range(SUBS):
        begin(sub)
        turn_on(LINE - 1, sub)
    for step in range(LINE - 2, -1, -1):
        if meanwhile[LINE - 2 - step] is not None:
            meanwhile[LINE - 2 - step]()
        if step > 0:
            for sub in range(SUBS):
                turn_on(step, sub)

    for sub in range(SUBS):
        across(place, sub).wait_recv()
        out[:, cols(sub)] = summed(place, sub)

        @pl.when(here.has_below)
        def _():
            up(place, sub).wait_recv()
            out[:, cols(sub)] += read(rx_up, place, sub)

        @pl.when(here.has_above)
        def _():
            down(place, sub).wait_recv()
            out[:, cols(sub)] += read(rx_dn, place, sub)

    for where in range(LINE):
        for sub in range(SUBS):
            across(where, sub).wait_send()

            @pl.when(where > place)
            def _():
                up(where, sub).wait_send()

            @pl.when(where < place)
            def _():
                down(where, sub).wait_send()


def dot(a, b):
    return jnp.dot(a, b, preferred_element_type=F32)


def dot_last(a, b):
    return lax.dot_general(a, b, (((1,), (1,)), ((), ())), preferred_element_type=F32)


def dot_rows(a, b):
    return lax.dot_general(a, b, (((0,), (0,)), ((), ())), preferred_element_type=F32)


def low_lanes(shape, size=HEAD_DIM):
    return lax.rem(lax.broadcasted_iota(jnp.int32, shape, 1), 2 * size) < size


def turn(block, cosine, sine):
    half = HEAD_DIM // 2
    other = jnp.where(low_lanes(block.shape, half), pltpu.roll(block, 128 - half, 1), pltpu.roll(block, half, 1))
    return block * cosine + other * sine


def spread_heads(wide):
    low = low_lanes((wide.shape[0], 128))
    parts = []
    for pair in range(GROUP // 2):
        block = wide[:, pair * 128:(pair + 1) * 128]
        parts.append(jnp.where(low, block, 0.0))
        parts.append(jnp.where(low, pltpu.roll(block, 64, 1), 0.0))
    return jnp.concatenate(parts, 0)


def join_heads(tall, from_high):
    rows = tall.shape[0] // GROUP
    low = low_lanes((rows, 128))
    parts = []
    for pair in range(GROUP // 2):
        one = tall[2 * pair * rows:(2 * pair + 1) * rows]
        two = tall[(2 * pair + 1) * rows:(2 * pair + 2) * rows]
        if from_high:
            parts.append(jnp.where(low, pltpu.roll(one, 64, 1), two))
        else:
            parts.append(jnp.where(low, one, pltpu.roll(two, 64, 1)))
    return jnp.concatenate(parts, 1)


def two_slot_probs(spread, kv, lens, pair):
    rows = 2 * SLOT
    q_at = lax.broadcasted_iota(jnp.int32, (rows, rows), 0)
    k_at = lax.broadcasted_iota(jnp.int32, (rows, rows), 1)
    first = lens[pl.ds(pl.multiple_of(16 * pair, 8), 8), :][:1]
    second = lens[pl.ds(pl.multiple_of(16 * pair + 8, 8), 8), :][:1]
    k_len = jnp.where(lax.broadcasted_iota(jnp.int32, (1, rows), 1) < SLOT, first, second)
    k_pos = jnp.where(k_at < SLOT, k_at, k_at - SLOT).astype(F32)
    allowed = (q_at >= k_at) & ((q_at < SLOT) | (k_at >= SLOT)) & (k_pos < k_len)
    allowed = jnp.concatenate([jnp.where(allowed, 1.0, 0.0)] * GROUP, 0)
    scores = dot_last(spread, kv) * HEAD_DIM**-0.5
    scores = jnp.where(allowed > 0.5, scores, -1e30)
    terms = jnp.exp(scores - jnp.max(scores, -1, keepdims=True))
    return terms / jnp.sum(terms, -1, keepdims=True)


def root(values):
    return lax.rsqrt(jnp.mean(values * values, -1, keepdims=True) + EPSILON)


Q_AT, KV_AT, AO_AT = 0, Q_SLAB, Q_SLAB + 2 * HEAD_DIM
A_COLS = AO_AT + Q_SLAB


def forward_body(
    ends, lens_in, gain_in, tables, w_in, w_out,
    wa_out, wg_out, wd_out, xn_out, hn_out, qkv_out, ctx_out, gu_out, hid_out, res_out, y_out, cot_out, gain_out, lens,
    cross, k_pair, v_pair, kv_mine, kv_twin, wa, wg, wd, seq, hnb, qkv, ctx, gu, hid, theirs, ours, res, total,
    sib_buf, rx_up, rx_dn, tx_up, tx_dn,
    loc_sem, push_send, push_recv, hop_send, hop_recv, misc, misc_send, misc_recv, save, w_save,
    *line_sems,
):
    gather_sems, len_sems, reduce_sems = line_sems[:5], line_sems[5:10], line_sems[10:]
    here = Here()
    core, shard, place = here.core, here.shard, here.place
    width = ends.shape[1]
    part = w_in.shape[0]
    here.greet()

    own_rows = pl.ds(pl.multiple_of(shard * part, part), part)

    def cut(ref, base, size, head):
        return ref.at[:, pl.ds(pl.multiple_of(base + head * size, size), size)]

    ff0 = Q_COLS + 2 * KV_COLS
    slabs = [
        (lambda h: cut(w_in, 0, Q_SLAB, h), lambda l: wa.at[l, own_rows, pl.ds(Q_AT, Q_SLAB)]),
        (lambda h: cut(w_out, 0, Q_SLAB, h), lambda l: wa.at[l, own_rows, pl.ds(AO_AT, Q_SLAB)]),
        (None, lambda l: wa.at[l, own_rows, pl.ds(KV_AT, 2 * HEAD_DIM)]),
        (lambda h: cut(w_in, ff0, FF_SLAB, h), lambda l: wg.at[l, own_rows, pl.ds(0, FF_SLAB)]),
        (lambda h: cut(w_in, ff0 + FF, FF_SLAB, h), lambda l: wg.at[l, own_rows, pl.ds(FF_SLAB, FF_SLAB)]),
        (lambda h: cut(w_out, Q_COLS, FF_SLAB, h), lambda l: wd.at[l, own_rows]),
    ]
    my_head, twin_head = place * CORES + core, place * CORES + 1 - core

    def own_copy(i, layer):
        src, dst = slabs[i]
        return pltpu.make_async_copy(kv_mine if src is None else src(my_head), dst(layer), loc_sem.at[i])

    def twin_copy(i, layer):
        src, dst = slabs[i]
        return remote(kv_twin if src is None else src(twin_head), dst(layer), push_send.at[i], push_recv.at[i], here.twin)

    k_copy = pltpu.make_async_copy(cut(w_in, Q_COLS, 128, place), k_pair, misc.at[0])
    v_copy = pltpu.make_async_copy(cut(w_in, Q_COLS + KV_COLS, 128, place), v_pair, misc.at[1])
    k_copy.start()
    v_copy.start()
    for i in (0, 1):
        twin_copy(i, core).start()
        own_copy(i, core).start()
    other_rows = pl.ds(pl.multiple_of((1 - core) * SLOT, SLOT), SLOT)
    cross_copy = remote(ends.at[other_rows], cross, misc_send.at[0], misc_recv.at[0], here.twin)
    cross_copy.start()
    gain_copy = remote(gain_in, gain_out.at[core], misc_send.at[1], misc_recv.at[1], here.twin)
    gain_copy.start()
    gain_out[core] = gain_in[...]
    k_copy.wait()
    v_copy.wait()
    low = low_lanes(k_pair.shape)
    k, v = k_pair[...].astype(F32), v_pair[...].astype(F32)
    kv0 = jnp.where(low, k, pltpu.roll(v, 64, 1)).astype(BF16)
    kv1 = jnp.where(low, pltpu.roll(k, 64, 1), v).astype(BF16)
    kv_mine[...] = jnp.where(core == 0, kv0, kv1)
    kv_twin[...] = jnp.where(core == 0, kv1, kv0)
    for i in (2, 3, 4, 5):
        twin_copy(i, core).start()
        own_copy(i, core).start()

    PIECES = ((wa, (0, 1, 2)), (wg, (3, 4)), (wd, (5,)))
    half = part // 2

    def own_ready(layer, piece):
        @pl.when(core == layer)
        def _():
            for i in PIECES[piece][1]:
                own_copy(i, layer).wait()

        @pl.when(core != layer)
        def _():
            for i in PIECES[piece][1]:
                twin_copy(i, layer).wait_recv()

    def hop(layer, piece, which, rows, size, peer):
        ref = PIECES[piece][0].at[layer, pl.ds(pl.multiple_of(rows, size), size)]
        return remote(ref, ref, hop_send.at[layer, piece, which], hop_recv.at[layer, piece, which], peer)

    def hops(layer, piece):
        return (
            hop(layer, piece, 0, shard * part, part, here.x_peer),
            hop(layer, piece, 1, shard * part, part, here.y_peer),
            hop(layer, piece, 2, here.x_shard * part, half, here.y_peer),
            hop(layer, piece, 3, here.y_shard * part + half, half, here.x_peer),
        )

    def hop_one(layer, piece):
        own_ready(layer, piece)
        one, two, _, _ = hops(layer, piece)
        one.start()
        two.start()

    def hop_two(layer, piece):
        one, two, three, four = hops(layer, piece)
        one.wait_recv()
        three.start()
        two.wait_recv()
        four.start()

    def all_in(layer, piece):
        _, _, three, four = hops(layer, piece)
        three.wait_recv()
        four.wait_recv()

    hop_one(0, 0)

    rows8 = lens_in.shape[0]
    lens[pl.ds(pl.multiple_of((core * LINE + place) * rows8, rows8), rows8), :] = lens_in[...]
    line_gather(here, lens, len_sems, (), 1)
    cross_copy.wait()
    gain_copy.wait()
    first = core == 0
    ours0, others0 = ends[:SLOT].astype(F32), ends[SLOT:].astype(F32)
    crossed = cross[...].astype(F32)
    x = jnp.where(first, ours0, crossed)
    cot_out[...] = jnp.where(first, crossed, others0).astype(BF16)
    res[0] = x

    def own_block(ref):
        return ref.at[pl.ds(pl.multiple_of((core * LINE + place) * SLOT, SLOT), SLOT), :]

    def weight_out(layer, piece):
        dst = (wa_out, wg_out, wd_out)[piece].at[layer]
        return pltpu.make_async_copy(PIECES[piece][0].at[layer], dst, w_save.at[layer, piece])

    reduce_bufs = (sib_buf, rx_up, rx_dn, tx_up, tx_dn)
    half_rows = LINE * SLOT

    def layer(index):
        saves = []

        def keep(src, dst):
            copy = pltpu.make_async_copy(src, dst, save.at[index, len(saves)])
            copy.start()
            saves.append(copy)

        if index == 0:
            x = res[0]
        else:
            x = y_out[...].astype(F32)
            res[2] = x
        own_block(seq)[...] = (x * root(x) * gain_out[index, 0:1]).astype(BF16)
        if index == 0:
            line_gather(here, seq, gather_sems, (None, None, lambda: (hop_two(0, 0), hop_one(0, 1))))
        else:
            line_gather(here, seq, gather_sems, (None, lambda: hop_one(1, 2)))
        keep(seq, xn_out.at[index])
        all_in(index, 0)
        weight_out(index, 0).start()

        def attend(pair, _):
            at = pl.ds(pl.multiple_of(pair * 2 * SLOT, 2 * SLOT), 2 * SLOT)
            wide = dot(seq[at, :], wa[index, :, :AO_AT])
            kv = turn(wide[:, KV_AT:AO_AT], tables[2], tables[3])
            q = jnp.concatenate(
                [turn(wide[:, 128 * i:128 * (i + 1)], tables[0], tables[1]) for i in range(GROUP // 2)], 1
            )
            kv_low = kv.astype(BF16)
            qkv[at, :Q_SLAB] = q.astype(BF16)
            qkv[at, KV_AT:AO_AT] = kv_low
            probs = two_slot_probs(spread_heads(q).astype(BF16), kv_low, lens, pair).astype(BF16)
            ctx[at, :] = join_heads(dot(probs, kv_low), True).astype(BF16)
            return 0

        lax.fori_loop(0, LINE, attend, 0)
        keep(qkv, qkv_out.at[index])
        keep(ctx, ctx_out.at[index])

        def reduce(src, weights, cols, meanwhile):
            def terms(whose, dst, sub):
                rows = pl.ds(pl.multiple_of(whose * half_rows, half_rows), half_rows)
                size = width // SUBS
                for lo in range(sub * size, (sub + 1) * size, 512):
                    at = slice(lo, lo + 512)
                    dst[:, at] = dot_last(src[rows, :], weights[index, at, cols]).astype(dst.dtype)

            line_reduce(here, total, ours, theirs, reduce_bufs, reduce_sems, terms, meanwhile)

        saves[0].wait()
        reduce(ctx, wa, slice(AO_AT, A_COLS), () if index == 0 else (None, None, lambda: hop_two(1, 1)))
        middle = x + total[...]
        res[1 + 2 * index] = middle
        own_block(hnb)[...] = (middle * root(middle) * gain_out[index, 1:2]).astype(BF16)
        if index == 0:
            line_gather(here, hnb, gather_sems, (None, lambda: hop_one(0, 2), None, lambda: hop_two(0, 1)))
        else:
            line_gather(here, hnb, gather_sems, (None, None, lambda: hop_two(1, 2)))
        keep(hnb, hn_out.at[index])
        all_in(index, 1)
        weight_out(index, 1).start()

        def gate_up(n, _):
            at = pl.ds(pl.multiple_of(n * 256, 256), 256)
            at_up = pl.ds(pl.multiple_of(FF_SLAB + n * 256, 256), 256)
            gate = dot(hnb[...], wg[index, :, at])
            up = dot(hnb[...], wg[index, :, at_up])
            gu[:, at] = gate
            gu[:, at_up] = up
            hid[:, at] = (gate * jax.nn.sigmoid(gate) * up).astype(BF16)
            return 0

        lax.fori_loop(0, FF_SLAB // 256, gate_up, 0)
        keep(gu, gu_out.at[index])
        keep(hid, hid_out.at[index])
        if index == 0:
            hop_one(1, 0)
            hop_two(0, 2)
            hop_one(1, 1)
        all_in(index, 2)
        weight_out(index, 2).start()
        saves[3].wait()
        reduce(hid, wd, slice(None), (None, lambda: hop_two(1, 0)) if index == 0 else ())
        y_out[...] = (res[1 + 2 * index] + total[...]).astype(BF16)
        for i in (1, 2, 4, 5):
            saves[i].wait()

    layer(0)
    layer(1)
    for i in range(4):
        pltpu.make_async_copy(res.at[i], res_out.at[i], misc.at[i]).start()
    for i in range(4):
        pltpu.make_async_copy(res.at[i], res_out.at[i], misc.at[i]).wait()
    for i in range(6):
        twin_copy(i, core).wait_send()
    for index in range(2):
        for piece in range(3):
            weight_out(index, piece).wait()
            for move in hops(index, piece):
                move.wait_send()


def forward_call(ends, lens, gain, tables, w_in, w_out):
    width = ends.shape[1]
    rows = LINE * CORES * SLOT
    hbm = pl.BlockSpec(memory_space=pl.ANY)
    vmem = pl.BlockSpec(memory_space=pltpu.VMEM)
    shape = jax.ShapeDtypeStruct
    dma = pltpu.SemaphoreType.DMA
    line = dma((LINE, SUBS))
    block = pltpu.VMEM((LINE * SLOT, width), BF16)
    return pl.pallas_call(
        forward_body,
        out_shape=[
            shape((2, width, A_COLS), BF16),
            shape((2, width, 2 * FF_SLAB), BF16),
            shape((2, width, FF_SLAB), BF16),
            shape((2, rows, width), BF16),
            shape((2, rows, width), BF16),
            shape((2, rows, AO_AT), BF16),
            shape((2, rows, Q_SLAB), BF16),
            shape((2, rows, 2 * FF_SLAB), F32),
            shape((2, rows, FF_SLAB), BF16),
            shape((4, SLOT, width), F32),
            shape((SLOT, width), BF16),
            shape((SLOT, width), BF16),
            shape((2, 2, width), F32),
            shape((LINE * CORES * 8, 128), F32),
        ],
        in_specs=[vmem, vmem, vmem, vmem, hbm, hbm],
        out_specs=[hbm] * 10 + [vmem] * 4,
        scratch_shapes=[
            pltpu.VMEM((SLOT, width), BF16),
            pltpu.VMEM((w_in.shape[0], 128), BF16),
            pltpu.VMEM((w_in.shape[0], 128), BF16),
            pltpu.VMEM((w_in.shape[0], 128), BF16),
            pltpu.VMEM((w_in.shape[0], 128), BF16),
            pltpu.VMEM((2, width, A_COLS), BF16),
            pltpu.VMEM((2, width, 2 * FF_SLAB), BF16),
            pltpu.VMEM((2, width, FF_SLAB), BF16),
            pltpu.VMEM((rows, width), BF16),
            pltpu.VMEM((rows, width), BF16),
            pltpu.VMEM((rows, AO_AT), BF16),
            pltpu.VMEM((rows, Q_SLAB), BF16),
            pltpu.VMEM((rows, 2 * FF_SLAB), F32),
            pltpu.VMEM((rows, FF_SLAB), BF16),
            block,
            pltpu.VMEM((LINE * SLOT, width), F32),
            pltpu.VMEM((4, SLOT, width), F32),
            pltpu.VMEM((SLOT, width), F32),
            block, block, block, block, block,
            dma((6,)), dma((6,)), dma((6,)), dma((2, 3, 4)), dma((2, 3, 4)),
            dma((4,)), dma((2,)), dma((2,)), dma((2, 6)), dma((2, 3)),
        ] + [line] * 16,
        compiler_params=pltpu.CompilerParams(
            collective_id=0, has_side_effects=True, vmem_limit_bytes=60 * 2**20
        ),
        name="forward_two_layers",
        cost_estimate=pl.CostEstimate(flops=16_000_000_000, bytes_accessed=600_000_000, transcendentals=0),
    )(ends, lens, gain, tables, w_in, w_out)


def spread_heads_high(wide):
    low = low_lanes((wide.shape[0], 128))
    parts = []
    for pair in range(GROUP // 2):
        block = wide[:, pair * 128:(pair + 1) * 128]
        parts.append(jnp.where(low, 0.0, pltpu.roll(block, 64, 1)))
        parts.append(jnp.where(low, 0.0, block))
    return jnp.concatenate(parts, 0)


CHUNKS = ((0, FF_SLAB), (FF_SLAB, FF_SLAB), (2 * FF_SLAB, FF_SLAB), (3 * FF_SLAB, A_COLS))
SLAB = 3 * FF_SLAB + A_COLS


def backward_body(
    replicas,
    cot_in, y_in, gain, lens, tables, res_in, wa_in, wg_in, wd_in, xn_in, hn_in, qkv_in, ctx_in, gu_in, hid_in,
    fin, ends_out, gain_out, far_rx, near_rx,
    wa, wg, wd, xn, hn, qkv, ctx, gu, hid, dm, da, dgu, dqkv, theirs, ours, total, res,
    sib_buf, rx_up, rx_dn, tx_up, tx_dn, tx_far, tx_x, tx_y, tx_fin, stage, gain_loc, gain_x, gain_y, gain_line,
    end_tx, end_rx,
    load_sem, gu_sem, res_sem, far_send, far_recv, near_send, near_recv, fin_send, fin_recv, stage_sem, misc_send, misc_recv,
    *line_sems,
):
    gather_sems, gain_sems, reduce_sems = line_sems[:5], line_sems[5:10], line_sems[10:]
    here = Here()
    core, shard, place = here.core, here.shard, here.place
    width = cot_in.shape[1]
    part = width // SHARDS
    half = part // 2
    half_rows = LINE * SLOT
    base = here.depth - place

    barrier = pltpu.get_barrier_semaphore()
    for peer in (here.x_peer, here.y_peer):
        pl.semaphore_signal(barrier, inc=1, device_id=peer)
    for other in range(CORES):
        for where in range(LINE):
            @pl.when((core != other) | (place != where))
            def _():
                pl.semaphore_signal(barrier, inc=1, device_id={"section": other, "dp": base + where})

    pl.semaphore_wait(barrier, 2 + CORES * LINE - 1)

    NAMES = ("wd", "wg", "wa", "hid", "qkv", "ctx", "hn", "xn")
    VIEWS = {
        "wd": (wd_in, lambda l: wd), "wg": (wg_in, lambda l: wg), "wa": (wa_in, lambda l: wa),
        "hid": (hid_in, lambda l: hid), "qkv": (qkv_in, lambda l: qkv.at[l]), "ctx": (ctx_in, lambda l: ctx.at[l]),
        "hn": (hn_in, lambda l: hn), "xn": (xn_in, lambda l: xn),
    }

    def load(name, layer):
        src, dst = VIEWS[name]
        return pltpu.make_async_copy(src.at[layer], dst(layer), load_sem.at[layer, NAMES.index(name)])

    def gu_loads(layer, tile):
        return [
            pltpu.make_async_copy(
                gu_in.at[layer, :, pl.ds(i * FF_SLAB + tile * 256, 256)],
                gu.at[tile % 2, :, pl.ds(i * 256, 256)], gu_sem.at[tile % 2, i])
            for i in range(2)
        ]

    for tile in range(2):
        for copy in gu_loads(1, tile):
            copy.start()
    for name in NAMES:
        load(name, 1).start()

    ready = set()

    def need(name, layer):
        if (name, layer) not in ready:
            ready.add((name, layer))
            load(name, layer).wait()

    gain_loc[...] = jnp.zeros_like(gain_loc)

    pending = {}

    def claim(key):
        for move in pending.pop(key, ()):
            move.wait_send()

    def products(layer, chunk, block, put):
        at = pl.ds(pl.multiple_of(block * part, part), part)
        need("hn" if chunk < 2 else "hid" if chunk == 2 else "xn", layer)

        def tiles(lhs, rhs, size, to):
            for lo in range(0, size, 512):
                hi = min(lo + 512, size)
                put(slice(to + lo, to + hi), dot_rows(lhs[:, at], rhs[:, lo:hi]))

        if chunk < 2:
            tiles(hn, dgu.at[layer, :, pl.ds(chunk * FF_SLAB, FF_SLAB)], FF_SLAB, 0)
        elif chunk == 2:
            tiles(dm.at[layer], hid, FF_SLAB, 0)
        else:
            tiles(xn, dqkv.at[layer], AO_AT, 0)
            tiles(da.at[layer], ctx.at[layer], Q_SLAB, AO_AT)

    def far_moves(layer, chunk):
        lo, size = CHUNKS[chunk]
        src = tx_far.at[chunk % 2]
        cols = pl.ds(0, size)
        return [
            remote(src.at[pl.ds(i * half, half), cols], far_rx.at[layer, i, :, pl.ds(lo, size)],
                   far_send.at[layer, chunk, i], far_recv.at[layer, chunk, i], peer)
            for i, peer in ((0, here.x_peer), (1, here.y_peer))
        ]

    def near_moves(layer, chunk):
        lo, size = CHUNKS[chunk]
        cols = pl.ds(0, size)
        return [
            remote(src.at[chunk % 2, :, cols], near_rx.at[layer, i, :, pl.ds(lo, size)],
                   near_send.at[layer, chunk, i], near_recv.at[layer, chunk, i], peer)
            for i, (src, peer) in enumerate(((tx_x, here.x_peer), (tx_y, here.y_peer)))
        ]

    def stage_far(layer, chunk, i):
        lo, size = CHUNKS[chunk]
        return pltpu.make_async_copy(
            far_rx.at[layer, i, :, pl.ds(lo, size)], stage.at[i, pl.ds(0, half), pl.ds(0, size)], stage_sem.at[i])

    def stage_near(layer, chunk, i):
        lo, size = CHUNKS[chunk]
        return pltpu.make_async_copy(
            near_rx.at[layer, i, :, pl.ds(lo, size)], stage.at[i, :, pl.ds(0, size)], stage_sem.at[i])

    def step_one(layer, chunk):
        claim(("far", chunk % 2))

        def put(cols, value):
            tx_far[chunk % 2, :, cols] = value.astype(BF16)

        products(layer, chunk, here.far_shard, put)
        moves = far_moves(layer, chunk)
        for move in moves:
            move.start()
        pending["far", chunk % 2] = moves

    def step_two(layer, chunk):
        arrivals = far_moves(layer, chunk)
        for i in (1, 0):
            arrivals[i].wait_recv()
            stage_far(layer, chunk, i).start()
        claim(("near", chunk % 2))
        moves = near_moves(layer, chunk)

        def put_x(cols, value):
            tx_x[chunk % 2, :half, cols] = value[:half].astype(BF16)
            tx_x[chunk % 2, half:, cols] = (value[half:] + stage[1, :half, cols].astype(F32)).astype(BF16)

        def put_y(cols, value):
            tx_y[chunk % 2, :half, cols] = (value[:half] + stage[0, :half, cols].astype(F32)).astype(BF16)
            tx_y[chunk % 2, half:, cols] = value[half:].astype(BF16)

        stage_far(layer, chunk, 1).wait()
        products(layer, chunk, here.x_shard, put_x)
        moves[0].start()
        stage_far(layer, chunk, 0).wait()
        products(layer, chunk, here.y_shard, put_y)
        moves[1].start()
        pending["near", chunk % 2] = moves

    piece = part // (replicas * LINE)

    def fin_moves(layer, chunk):
        lo, size = CHUNKS[chunk]
        head = place * CORES + core
        moves = []
        for rep in range(replicas):
            for where in range(LINE):
                src = tx_fin.at[chunk % 2, pl.ds((rep * LINE + where) * piece, piece), pl.ds(0, size)]
                dst = fin.at[head, pl.ds(rep * piece, piece), pl.ds(lo, size)]
                same = (core == layer) & (place == where)
                move = remote(src, dst, fin_send.at[layer, chunk, rep, where], fin_recv.at[rep, head, chunk],
                              {"section": layer, "dp": base + where})
                stay = pltpu.make_async_copy(src, dst, fin_send.at[layer, chunk, rep, where])
                moves.append((same, move, stay))
        return moves

    class Leave:
        def __init__(self, entry):
            self.same, self.move, self.stay = entry

        def start(self):
            @pl.when(self.same)
            def _():
                self.stay.start()

            @pl.when(jnp.logical_not(self.same))
            def _():
                self.move.start()

        def wait_send(self):
            @pl.when(self.same)
            def _():
                self.stay.wait()

            @pl.when(jnp.logical_not(self.same))
            def _():
                self.move.wait_send()

    def step_three(layer, chunk):
        arrivals = near_moves(layer, chunk)
        for i in range(2):
            arrivals[i].wait_recv()
            stage_near(layer, chunk, i).start()
        claim(("fin", chunk % 2))
        stage_near(layer, chunk, 0).wait()
        stage_near(layer, chunk, 1).wait()

        def put(cols, value):
            tx_fin[chunk % 2, :, cols] = (
                value + stage[0, :, cols].astype(F32) + stage[1, :, cols].astype(F32)
            ).astype(BF16)

        products(layer, chunk, shard, put)
        moves = [Leave(entry) for entry in fin_moves(layer, chunk)]
        for move in moves:
            move.start()
        pending["fin", chunk % 2] = moves

    def steps(*todo):
        def run():
            for kind, layer, chunk in todo:
                (step_one, step_two, step_three)[kind - 1](layer, chunk)
                if layer == 1 and kind == 3 and chunk == 1:
                    load("hn", 0).start()
                if layer == 1 and kind == 3 and chunk == 2:
                    load("hid", 0).start()
                if layer == 1 and kind == 3 and chunk == 3:
                    load("xn", 0).start()
        return run

    reduce_bufs = (sib_buf, rx_up, rx_dn, tx_up, tx_dn)

    def own_block(ref, layer):
        return ref.at[layer, pl.ds(pl.multiple_of((core * LINE + place) * SLOT, SLOT), SLOT), :]

    def reduce(slot, src, weights, cols, meanwhile):
        res_load(slot).start()

        def terms(whose, dst, sub):
            rows = pl.ds(pl.multiple_of(whose * half_rows, half_rows), half_rows)
            size = width // SUBS
            for lo in range(sub * size, (sub + 1) * size, 512):
                at = slice(lo, lo + 512)
                dst[:, at] = dot_last(src[rows, :], weights[at, cols]).astype(dst.dtype)

        line_reduce(here, total, ours, theirs, reduce_bufs, reduce_sems, terms, meanwhile)

    def res_load(slot):
        return pltpu.make_async_copy(res_in.at[slot], res, res_sem.at[slot])

    def norm_back(gain_row, slot):
        res_load(slot).wait()
        values = res[...]
        scale = root(values)
        grad = total[...]
        hat = grad * gain_row
        gain_loc[slot:slot + 1, :] = jnp.sum(grad * values * scale, 0, keepdims=True)
        inner = jnp.mean(hat * values, -1, keepdims=True)
        return scale * hat - values * (scale * scale * scale * inner)

    def layer_back(layer, grad_out, jobs):
        own_block(dm, layer)[...] = grad_out.astype(BF16)
        line_gather(here, dm.at[layer], gather_sems, jobs[0])
        need("wd", layer)
        tiles = FF_SLAB // 256
        for tile in range(tiles):
            at = slice(tile * 256, tile * 256 + 256)
            at_up = slice(FF_SLAB + tile * 256, FF_SLAB + tile * 256 + 256)
            grad = dot(dm[layer], wd[:, at])
            for copy in gu_loads(layer, tile):
                copy.wait()
            gate, up = gu[tile % 2, :, :256], gu[tile % 2, :, 256:]
            sig = jax.nn.sigmoid(gate)
            dgu[layer, :, at] = (grad * up * sig * (1.0 + gate * (1.0 - sig))).astype(BF16)
            dgu[layer, :, at_up] = (grad * gate * sig).astype(BF16)
            ahead = (layer, tile + 2) if tile + 2 < tiles else (layer - 1, tile + 2 - tiles)
            if ahead[0] >= 0:
                for copy in gu_loads(*ahead):
                    copy.start()
        need("wg", layer)
        if layer == 1:
            load("wd", 0).start()
        reduce(2 * layer + 1, dgu.at[layer], wg, slice(None), jobs[1])
        if layer == 1:
            load("wg", 0).start()
        grad_mid = grad_out + norm_back(gain[layer, 1:2], 2 * layer + 1)
        own_block(da, layer)[...] = grad_mid.astype(BF16)
        line_gather(here, da.at[layer], gather_sems, jobs[2])
        need("wa", layer)
        need("qkv", layer)
        need("ctx", layer)

        def attend(pair, _):
            at = pl.ds(pl.multiple_of(pair * 2 * SLOT, 2 * SLOT), 2 * SLOT)
            grad_ctx = dot(da[layer, at, :], wa[:, AO_AT:A_COLS]).astype(BF16).astype(F32)
            kv = qkv[layer, at, KV_AT:AO_AT]
            q = spread_heads(qkv[layer, at, :Q_SLAB].astype(F32)).astype(BF16)
            probs = two_slot_probs(q, kv, lens, pair)
            grad_high = spread_heads_high(grad_ctx).astype(BF16)
            grad_probs = dot_last(grad_high, kv)
            inner = jnp.sum(grad_probs * probs, -1, keepdims=True)
            grad_scores = (probs * (grad_probs - inner)).astype(BF16)
            grad_q = join_heads(dot(grad_scores, kv), False) * HEAD_DIM**-0.5
            grad_kv = dot_rows(grad_scores, q) * HEAD_DIM**-0.5 + dot_rows(probs.astype(BF16), grad_high)
            for i in range(GROUP // 2):
                cols = slice(128 * i, 128 * (i + 1))
                dqkv[layer, at, cols] = turn(grad_q[:, cols], tables[0], -tables[1]).astype(BF16)
            dqkv[layer, at, KV_AT:AO_AT] = turn(grad_kv, tables[2], -tables[3]).astype(BF16)
            return 0

        lax.fori_loop(0, LINE, attend, 0)
        reduce(2 * layer, dqkv.at[layer], wa, slice(0, AO_AT), jobs[3])
        if layer == 1:
            load("wa", 0).start()
            load("qkv", 0).start()
            load("ctx", 0).start()
        return grad_mid + norm_back(gain[layer, 0:1], 2 * layer)

    own_len = lens[pl.ds(pl.multiple_of((core * LINE + place) * 8, 8), 8), :][:1]
    live = lax.broadcasted_iota(jnp.int32, (SLOT, 128), 0).astype(F32) < own_len
    valid = jnp.where(live, 1.0, 0.0)[:, :1]
    dx1 = layer_back(1, cot_in[...].astype(F32) * valid, (
        (),
        (steps((1, 1, 0)), steps((1, 1, 1)), steps((1, 1, 2))),
        (steps((2, 1, 0)), None, steps((2, 1, 1))),
        (steps((1, 1, 3)), steps((2, 1, 2)), steps((3, 1, 0))),
    ))
    dx0 = layer_back(0, dx1.astype(BF16).astype(F32), (
        (None, None, None, steps((3, 1, 1))),
        (steps((1, 0, 0)), steps((1, 0, 1))),
        (steps((2, 1, 3), (3, 1, 2)), None, steps((1, 0, 2), (2, 0, 0))),
        (steps((2, 0, 1)), steps((3, 1, 3)), steps((1, 0, 3))),
    ))

    first = core == 0
    dx0 = dx0.astype(BF16).astype(F32)
    y1 = y_in[...].astype(F32)
    end_tx[...] = jnp.where(first, y1, dx0).astype(BF16)
    end_move = remote(end_tx, end_rx, misc_send.at[0], misc_recv.at[0], here.twin)
    end_move.start()

    gain_x_move = remote(gain_loc, gain_x, misc_send.at[1], misc_recv.at[1], here.x_peer)
    gain_x_move.start()
    steps((2, 0, 2), (3, 0, 0))()
    gain_x_move.wait()
    gain_loc[...] += gain_x[...]
    gain_y_move = remote(gain_loc, gain_y, misc_send.at[2], misc_recv.at[2], here.y_peer)
    gain_y_move.start()
    steps((3, 0, 1))()
    gain_y_move.wait()
    cols = pl.ds(pl.multiple_of(shard * part, part), part)
    own_gains = pl.ds(pl.multiple_of((core * LINE + place) * 8, 8), 8)
    gain_line[own_gains, :] = gain_loc[:, cols] + gain_y[:, cols]
    line_gather(here, gain_line, gain_sems, (), 1)
    gain_sum = gain_line[0:8, :]
    for i in range(1, LINE * CORES):
        gain_sum += gain_line[8 * i:8 * i + 8, :]
    gain_out[...] = gain_sum
    end_move.wait()
    crossed = end_rx[...].astype(F32)
    ends_out[:SLOT] = jnp.where(first, dx0, crossed).astype(BF16)
    ends_out[SLOT:] = jnp.where(first, crossed, y1).astype(BF16)
    steps((2, 0, 3), (3, 0, 2), (3, 0, 3))()
    for key in list(pending):
        claim(key)
    for rep in range(replicas):
        for where in range(LINE):
            for other in range(CORES):
                head = where * CORES + other

                @pl.when((core != other) | (place != where))
                def _():
                    for chunk, (lo, size) in enumerate(CHUNKS):
                        src = tx_fin.at[0, pl.ds(0, piece), pl.ds(0, size)]
                        dst = fin.at[head, pl.ds(rep * piece, piece), pl.ds(lo, size)]
                        remote(src, dst, fin_send.at[0, 0, 0, 0], fin_recv.at[rep, head, chunk],
                               {"section": 1 - core, "dp": base + where}).wait_recv()


def backward_call(replicas, cot, y, gain, lens, tables, res, wa, wg, wd, xn, hn, qkv, ctx, gu, hid):
    width = cot.shape[1]
    rows = LINE * CORES * SLOT
    part = width // SHARDS
    hbm = pl.BlockSpec(memory_space=pl.ANY)
    vmem = pl.BlockSpec(memory_space=pltpu.VMEM)
    shape = jax.ShapeDtypeStruct
    dma = pltpu.SemaphoreType.DMA
    line = dma((LINE, SUBS))
    vm = pltpu.VMEM
    block = vm((LINE * SLOT, width), BF16)
    move = vm((2, part, FF_SLAB), BF16)
    return pl.pallas_call(
        functools.partial(backward_body, replicas),
        out_shape=[
            shape((KV_HEADS, part // LINE, SLAB), BF16),
            shape((CORES * SLOT, width), BF16),
            shape((8, part), F32),
            shape((2, 2, part // 2, SLAB), BF16),
            shape((2, 2, part, SLAB), BF16),
        ],
        in_specs=[vmem] * 5 + [hbm] * 10,
        out_specs=[hbm, vmem, vmem, hbm, hbm],
        scratch_shapes=[
            vm((width, A_COLS), BF16), vm((width, 2 * FF_SLAB), BF16), vm((width, FF_SLAB), BF16),
            vm((rows, width), BF16), vm((rows, width), BF16), vm((2, rows, AO_AT), BF16), vm((2, rows, Q_SLAB), BF16),
            vm((2, rows, 512), F32), vm((rows, FF_SLAB), BF16),
            vm((2, rows, width), BF16), vm((2, rows, width), BF16),
            vm((2, rows, 2 * FF_SLAB), BF16), vm((2, rows, AO_AT), BF16),
            block, vm((LINE * SLOT, width), F32), vm((SLOT, width), F32), vm((SLOT, width), F32),
            block, block, block, block, block,
            move, move, move, move, move,
            vm((8, width), F32), vm((8, width), F32), vm((8, width), F32), vm((8 * LINE * CORES, part), F32),
            vm((SLOT, width), BF16), vm((SLOT, width), BF16),
            dma((2, 8)), dma((2, 2)), dma((4,)), dma((2, 4, 2)), dma((2, 4, 2)), dma((2, 4, 2)), dma((2, 4, 2)),
            dma((2, 4, replicas, LINE)), dma((replicas, KV_HEADS, 4)), dma((2,)), dma((3,)), dma((3,)),
        ] + [line] * 16,
        compiler_params=pltpu.CompilerParams(
            collective_id=1, has_side_effects=True, vmem_limit_bytes=61 * 2**20
        ),
        name="backward_two_layers",
        cost_estimate=pl.CostEstimate(flops=32_000_000_000, bytes_accessed=600_000_000, transcendentals=0),
    )(cot, y, gain, lens, tables, res, wa, wg, wd, xn, hn, qkv, ctx, gu, hid)


def place_body(fin, in_out, out_out, held, wide_in, wide_out, load_sem, save_sem):
    steps = KV_HEADS // 2
    q_two, ff_two = 2 * Q_SLAB, 2 * FF_SLAB
    ff0 = Q_COLS + 2 * KV_COLS

    def fetch(step):
        return pltpu.make_async_copy(fin.at[pl.ds(2 * step, 2)], held.at[step % 2], load_sem.at[step % 2])

    def saves(step):
        slot = step % 2
        moves = []
        for i, (src, lo, dst, to, size) in enumerate((
            (wide_in, 0, in_out, step * q_two, q_two),
            (wide_in, q_two, in_out, Q_COLS + step * 128, 128),
            (wide_in, q_two + 128, in_out, Q_COLS + KV_COLS + step * 128, 128),
            (wide_in, q_two + 256, in_out, ff0 + step * ff_two, ff_two),
            (wide_in, q_two + 256 + ff_two, in_out, ff0 + FF + step * ff_two, ff_two),
            (wide_out, 0, out_out, step * q_two, q_two),
            (wide_out, q_two, out_out, Q_COLS + step * ff_two, ff_two),
        )):
            moves.append(pltpu.make_async_copy(
                src.at[slot, :, pl.ds(lo, size)], dst.at[:, pl.ds(to, size)], save_sem.at[slot, i]))
        return moves

    fetch(0).start()
    a_at = 3 * FF_SLAB
    for step in range(steps):
        slot = step % 2
        if step + 1 < steps:
            fetch(step + 1).start()
        fetch(step).wait()
        if step >= 2:
            for move in saves(step - 2):
                move.wait()
        for i in range(2):
            q_to = i * Q_SLAB
            wide_in[slot, :, q_to:q_to + Q_SLAB] = held[slot, i, :, a_at:a_at + Q_SLAB].astype(F32)
            wide_out[slot, :, q_to:q_to + Q_SLAB] = held[slot, i, :, a_at + AO_AT:a_at + A_COLS].astype(F32)
            for k, (src_ref, to) in enumerate(((wide_in, q_two + 256), (wide_in, q_two + 256 + ff_two), (wide_out, q_two))):
                at = to + i * FF_SLAB
                src_ref[slot, :, at:at + FF_SLAB] = held[slot, i, :, k * FF_SLAB:(k + 1) * FF_SLAB].astype(F32)
        one = held[slot, 0, :, a_at + KV_AT:a_at + AO_AT].astype(F32)
        two = held[slot, 1, :, a_at + KV_AT:a_at + AO_AT].astype(F32)
        low = low_lanes(one.shape)
        wide_in[slot, :, q_two:q_two + 128] = jnp.where(low, one, pltpu.roll(two, 64, 1))
        wide_in[slot, :, q_two + 128:q_two + 256] = jnp.where(low, pltpu.roll(one, 64, 1), two)
        for move in saves(step):
            move.start()
    for step in range(max(steps - 2, 0), steps):
        for move in saves(step):
            move.wait()


def place_call(fin, in_cols, out_cols):
    rows = fin.shape[1]
    hbm = pl.BlockSpec(memory_space=pl.ANY)
    q_two, ff_two = 2 * Q_SLAB, 2 * FF_SLAB
    return pl.pallas_call(
        place_body,
        out_shape=[jax.ShapeDtypeStruct((rows, in_cols), F32), jax.ShapeDtypeStruct((rows, out_cols), F32)],
        in_specs=[hbm],
        out_specs=[hbm, hbm],
        scratch_shapes=[
            pltpu.VMEM((2, 2, rows, SLAB), BF16),
            pltpu.VMEM((2, rows, q_two + 256 + 2 * ff_two), F32),
            pltpu.VMEM((2, rows, q_two + ff_two), F32),
            pltpu.SemaphoreType.DMA((2,)),
            pltpu.SemaphoreType.DMA((2, 7)),
        ],
        compiler_params=pltpu.CompilerParams(vmem_limit_bytes=32 * 2**20),
        name="place_columns",
    )(fin)


def rope_blocks():
    half_dim = HEAD_DIM // 2
    inverse = 500000.0 ** (-(jnp.arange(half_dim, dtype=F32) * 2.0 / HEAD_DIM))
    angles = jnp.arange(SLOT, dtype=F32)[:, None] * inverse[None, :]
    cos, sin = jnp.cos(angles), jnp.sin(angles)
    one, zero = jnp.ones((SLOT, HEAD_DIM), F32), jnp.zeros((SLOT, HEAD_DIM), F32)
    rows = [
        jnp.concatenate([cos] * 4, 1),
        jnp.concatenate([-sin, sin] * 2, 1),
        jnp.concatenate([cos, cos, one], 1),
        jnp.concatenate([-sin, sin, zero], 1),
    ]
    return jnp.stack([jnp.tile(block, (2, 1)) for block in rows])


def local(ends_in, in_weight, out_weight, norm_gain, seq_len):
    core = lax.axis_index("section")
    replicas = lax.axis_size("dp") // LINE
    own_length = jnp.where(core == 0, seq_len[0], seq_len[1])
    lens_block = jnp.full((8, 128), own_length.astype(F32))
    rope = rope_blocks()
    (wa, wg, wd, xn, hn, qkv, ctx, gu, hid, res, y1, cot, gains, lens) = forward_call(
        ends_in[0], lens_block, norm_gain[0], rope, in_weight[0], out_weight[0]
    )
    fin, ends_out, gain_sum, _, _ = backward_call(
        replicas, cot, y1, gains, lens, rope, res, wa, wg, wd, xn, hn, qkv, ctx, gu, hid
    )
    own_gain = lax.dynamic_slice_in_dim(gain_sum, 2 * core, 2, 0)
    if replicas > 1:
        groups = [[r * LINE + p for r in range(replicas)] for p in range(LINE)]
        fin = lax.psum_scatter(fin, "dp", scatter_dimension=1, tiled=True, axis_index_groups=groups)
        own_gain = lax.psum(own_gain, "dp", axis_index_groups=groups)
    in_grad, out_grad = place_call(fin, in_weight.shape[2], out_weight.shape[2])
    size = own_gain.shape[1] // lax.axis_size("dp")
    own_gain = lax.dynamic_slice_in_dim(own_gain, lax.axis_index("dp") * size, size, 1)
    return ends_out[None], in_grad[None], out_grad[None], own_gain[None]


def solution(mesh):
    in_specs = (
        P("section", ("shard", "dp"), None),
        P("section", "shard", None),
        P("section", "shard", None),
        P("section", None, None),
        P(("shard", "dp")),
    )
    out_specs = (
        P("section", ("shard", "dp"), None),
        P("section", ("shard", "dp"), None),
        P("section", ("shard", "dp"), None),
        P("section", None, ("shard", "dp")),
    )
    return jax.shard_map(local, mesh=mesh, in_specs=in_specs, out_specs=out_specs, check_vma=False)
```

```python
import functools

import jax
import jax.numpy as jnp
from jax import lax
from jax.experimental import pallas as pl
from jax.experimental.pallas import tpu as pltpu
from jax.sharding import PartitionSpec as P

HEADS = 32
KV_HEADS = 8
GROUP = HEADS // KV_HEADS
HEAD_DIM = 64
FF = 8192
EPSILON = 1e-05
BF16 = jnp.bfloat16
F32 = jnp.float32
CORES = 2
LINE = KV_HEADS // CORES
SHARDS = 4
SLOT = 64
SUBS = 2
Q_SLAB = GROUP * HEAD_DIM
QKV_SLAB = Q_SLAB + 2 * HEAD_DIM
FF_SLAB = FF // KV_HEADS
Q_COLS = HEADS * HEAD_DIM
KV_COLS = KV_HEADS * HEAD_DIM


class Here:
    def __init__(self):
        self.core = lax.axis_index("section")
        self.shard = lax.axis_index("shard")
        self.depth = lax.axis_index("dp")
        self.place = lax.rem(self.depth, LINE)
        self.twin = {"section": 1 - self.core}
        self.x_shard = self.shard + 1 - 2 * lax.rem(self.shard, 2)
        self.y_shard = lax.rem(self.shard + 2, SHARDS)
        self.far_shard = SHARDS - 1 - self.shard
        self.x_peer = {"shard": self.x_shard}
        self.y_peer = {"shard": self.y_shard}
        self.above = {"dp": self.depth + 1}
        self.below = {"dp": self.depth - 1}
        self.has_above = self.place < LINE - 1
        self.has_below = self.place > 0

    def greet(self):
        barrier = pltpu.get_barrier_semaphore()
        for peer in (self.twin, self.x_peer, self.y_peer):
            pl.semaphore_signal(barrier, inc=1, device_id=peer)

        @pl.when(self.has_above)
        def _():
            pl.semaphore_signal(barrier, inc=1, device_id=self.above)

        @pl.when(self.has_below)
        def _():
            pl.semaphore_signal(barrier, inc=1, device_id=self.below)

        pl.semaphore_wait(barrier, jnp.where(self.has_above & self.has_below, 5, 4))


def remote(src, dst, send, recv, device):
    return pltpu.make_async_remote_copy(src, dst, send, recv, device_id=device)


def rows_at(ref, start, size):
    return ref.at[pl.ds(pl.multiple_of(start, size), size)]


def line_gather(here, buf, sems, meanwhile=(), subs=SUBS):
    up_send, dn_send, sib_send, z_recv, sib_recv = sems
    rows = buf.shape[0] // (LINE * CORES)
    size = rows // subs
    core, place = here.core, here.place
    meanwhile = list(meanwhile) + [None] * (LINE + 1)

    def part(where, whose, sub):
        return rows_at(buf, (whose * LINE + where) * rows + sub * size, size)

    def up(where, sub):
        mine = part(where, core, sub)
        return remote(mine, mine, up_send.at[where, sub], z_recv.at[where, sub], here.above)

    def down(where, sub):
        mine = part(where, core, sub)
        return remote(mine, mine, dn_send.at[where, sub], z_recv.at[where, sub], here.below)

    def across(where, whose, sub):
        mine = part(where, whose, sub)
        return remote(mine, mine, sib_send.at[where, sub], sib_recv.at[where, sub], here.twin)

    for sub in range(subs):
        @pl.when(here.has_above)
        def _():
            up(place, sub).start()

        @pl.when(here.has_below)
        def _():
            down(place, sub).start()

    for sub in range(subs):
        across(place, core, sub).start()
    for step in range(1, LINE):
        if meanwhile[step - 1] is not None:
            meanwhile[step - 1]()
        for sub in range(subs):
            @pl.when(place >= step)
            def _():
                up(place - step, sub).wait_recv()

                @pl.when(here.has_above)
                def _():
                    up(place - step, sub).start()

                across(place - step, core, sub).start()

            @pl.when(place + step < LINE)
            def _():
                down(place + step, sub).wait_recv()

                @pl.when(here.has_below)
                def _():
                    down(place + step, sub).start()

                across(place + step, core, sub).start()

    if meanwhile[LINE - 1] is not None:
        meanwhile[LINE - 1]()
    for where in range(LINE):
        for sub in range(subs):
            across(where, 1 - core, sub).wait_recv()

    for where in range(LINE):
        for sub in range(subs):
            across(where, core, sub).wait_send()

            @pl.when((where <= place) & here.has_above)
            def _():
                up(where, sub).wait_send()

            @pl.when((where >= place) & here.has_below)
            def _():
                down(where, sub).wait_send()


def line_reduce(here, out, ours, theirs, bufs, sems, terms, meanwhile=()):
    sib_buf, rx_up, rx_dn, tx_up, tx_dn = bufs
    sib_send, sib_recv, up_send, up_recv, dn_send, dn_recv = sems
    rows, width = out.shape
    size = width // SUBS
    place, core = here.place, here.core
    meanwhile = list(meanwhile) + [None] * (LINE + 1)

    def cols(sub):
        return slice(sub * size, (sub + 1) * size)

    def part(ref, where, sub):
        return ref.at[pl.ds(pl.multiple_of(where * rows, rows), rows), pl.ds(sub * size, size)]

    def read(ref, where, sub):
        return ref[pl.ds(pl.multiple_of(where * rows, rows), rows), cols(sub)].astype(F32)

    def across(where, sub):
        return remote(part(theirs, where, sub), part(sib_buf, where, sub),
                      sib_send.at[where, sub], sib_recv.at[where, sub], here.twin)

    def up(where, sub):
        return remote(part(tx_up, where, sub), part(rx_up, where, sub),
                      up_send.at[where, sub], up_recv.at[where, sub], here.above)

    def down(where, sub):
        return remote(part(tx_dn, where, sub), part(rx_dn, where, sub),
                      dn_send.at[where, sub], dn_recv.at[where, sub], here.below)

    def summed(where, sub):
        return read(ours, where, sub) + read(sib_buf, where, sub)

    def put(ref, where, sub, value):
        ref[pl.ds(pl.multiple_of(where * rows, rows), rows), cols(sub)] = value.astype(BF16)

    def begin(sub):
        terms(1 - core, theirs, sub)
        for step in range(LINE - 1, 0, -1):
            @pl.when(place + step < LINE)
            def _():
                across(place + step, sub).start()

            @pl.when(place >= step)
            def _():
                across(place - step, sub).start()

        across(place, sub).start()
        terms(core, ours, sub)

    def turn_on(step, sub):
        @pl.when(place + step < LINE)
        def _():
            where = place + step
            across(where, sub).wait_recv()

            @pl.when(here.has_below)
            def _():
                up(where, sub).wait_recv()
                put(tx_up, where, sub, summed(where, sub) + read(rx_up, where, sub))

            @pl.when(place == 0)
            def _():
                put(tx_up, where, sub, summed(where, sub))

            up(where, sub).start()

        @pl.when(place >= step)
        def _():
            where = place - step
            across(where, sub).wait_recv()

            @pl.when(here.has_above)
            def _():
                down(where, sub).wait_recv()
                put(tx_dn, where, sub, summed(where, sub) + read(rx_dn, where, sub))

            @pl.when(place == LINE - 1)
            def _():
                put(tx_dn, where, sub, summed(where, sub))

            down(where, sub).start()

    for sub in range(SUBS):
        begin(sub)
        turn_on(LINE - 1, sub)
    for step in range(LINE - 2, -1, -1):
        if meanwhile[LINE - 2 - step] is not None:
            meanwhile[LINE - 2 - step]()
        if step > 0:
            for sub in range(SUBS):
                turn_on(step, sub)

    for sub in range(SUBS):
        across(place, sub).wait_recv()
        out[:, cols(sub)] = summed(place, sub)

        @pl.when(here.has_below)
        def _():
            up(place, sub).wait_recv()
            out[:, cols(sub)] += read(rx_up, place, sub)

        @pl.when(here.has_above)
        def _():
            down(place, sub).wait_recv()
            out[:, cols(sub)] += read(rx_dn, place, sub)

    for where in range(LINE):
        for sub in range(SUBS):
            across(where, sub).wait_send()

            @pl.when(where > place)
            def _():
                up(where, sub).wait_send()

            @pl.when(where < place)
            def _():
                down(where, sub).wait_send()


def dot(a, b):
    return jnp.dot(a, b, preferred_element_type=F32)


def dot_last(a, b):
    return lax.dot_general(a, b, (((1,), (1,)), ((), ())), preferred_element_type=F32)


def dot_rows(a, b):
    return lax.dot_general(a, b, (((0,), (0,)), ((), ())), preferred_element_type=F32)


def low_lanes(shape, size=HEAD_DIM):
    return lax.rem(lax.broadcasted_iota(jnp.int32, shape, 1), 2 * size) < size


def turn(block, cosine, sine):
    half = HEAD_DIM // 2
    other = jnp.where(low_lanes(block.shape, half), pltpu.roll(block, 128 - half, 1), pltpu.roll(block, half, 1))
    return block * cosine + other * sine


def spread_heads(wide):
    low = low_lanes((wide.shape[0], 128))
    parts = []
    for pair in range(GROUP // 2):
        block = wide[:, pair * 128:(pair + 1) * 128]
        parts.append(jnp.where(low, block, 0.0))
        parts.append(jnp.where(low, pltpu.roll(block, 64, 1), 0.0))
    return jnp.concatenate(parts, 0)


def join_heads(tall, from_high):
    rows = tall.shape[0] // GROUP
    low = low_lanes((rows, 128))
    parts = []
    for pair in range(GROUP // 2):
        one = tall[2 * pair * rows:(2 * pair + 1) * rows]
        two = tall[(2 * pair + 1) * rows:(2 * pair + 2) * rows]
        if from_high:
            parts.append(jnp.where(low, pltpu.roll(one, 64, 1), two))
        else:
            parts.append(jnp.where(low, one, pltpu.roll(two, 64, 1)))
    return jnp.concatenate(parts, 1)


def two_slot_probs(spread, kv, lens, pair):
    rows = 2 * SLOT
    q_at = lax.broadcasted_iota(jnp.int32, (rows, rows), 0)
    k_at = lax.broadcasted_iota(jnp.int32, (rows, rows), 1)
    first = lens[pl.ds(pl.multiple_of(16 * pair, 8), 8), :][:1]
    second = lens[pl.ds(pl.multiple_of(16 * pair + 8, 8), 8), :][:1]
    k_len = jnp.where(lax.broadcasted_iota(jnp.int32, (1, rows), 1) < SLOT, first, second)
    k_pos = jnp.where(k_at < SLOT, k_at, k_at - SLOT).astype(F32)
    allowed = (q_at >= k_at) & ((q_at < SLOT) | (k_at >= SLOT)) & (k_pos < k_len)
    allowed = jnp.concatenate([jnp.where(allowed, 1.0, 0.0)] * GROUP, 0)
    scores = dot_last(spread, kv) * HEAD_DIM**-0.5
    scores = jnp.where(allowed > 0.5, scores, -1e30)
    terms = jnp.exp(scores - jnp.max(scores, -1, keepdims=True))
    return terms / jnp.sum(terms, -1, keepdims=True)


def root(values):
    return lax.rsqrt(jnp.mean(values * values, -1, keepdims=True) + EPSILON)


Q_AT, KV_AT, AO_AT = 0, Q_SLAB, Q_SLAB + 2 * HEAD_DIM
A_COLS = AO_AT + Q_SLAB


def forward_body(
    ends, lens_in, gain_in, tables, w_in, w_out,
    wa_out, wg_out, wd_out, xn_out, hn_out, qkv_out, ctx_out, gu_out, hid_out, res_out, dm_out, cot_out, gain_out, lens,
    cross, k_pair, v_pair, kv_mine, kv_twin, wa, wg, wd, seq, hnb, qkv, ctx, gu, hid, theirs, ours, res, total, dm,
    sib_buf, rx_up, rx_dn, tx_up, tx_dn,
    loc_sem, push_send, push_recv, hop_send, hop_recv, misc, misc_send, misc_recv, save, w_save,
    *line_sems,
):
    gather_sems, len_sems, dm_sems, reduce_sems = line_sems[:5], line_sems[5:10], line_sems[10:15], line_sems[15:]
    here = Here()
    core, shard, place = here.core, here.shard, here.place
    width = ends.shape[1]
    part = w_in.shape[0]
    here.greet()

    own_rows = pl.ds(pl.multiple_of(shard * part, part), part)

    def cut(ref, base, size, head):
        return ref.at[:, pl.ds(pl.multiple_of(base + head * size, size), size)]

    ff0 = Q_COLS + 2 * KV_COLS
    slabs = [
        (lambda h: cut(w_in, 0, Q_SLAB, h), lambda l: wa.at[l, own_rows, pl.ds(Q_AT, Q_SLAB)]),
        (lambda h: cut(w_out, 0, Q_SLAB, h), lambda l: wa.at[l, own_rows, pl.ds(AO_AT, Q_SLAB)]),
        (None, lambda l: wa.at[l, own_rows, pl.ds(KV_AT, 2 * HEAD_DIM)]),
        (lambda h: cut(w_in, ff0, FF_SLAB, h), lambda l: wg.at[l, own_rows, pl.ds(0, FF_SLAB)]),
        (lambda h: cut(w_in, ff0 + FF, FF_SLAB, h), lambda l: wg.at[l, own_rows, pl.ds(FF_SLAB, FF_SLAB)]),
        (lambda h: cut(w_out, Q_COLS, FF_SLAB, h), lambda l: wd.at[l, own_rows]),
    ]
    my_head, twin_head = place * CORES + core, place * CORES + 1 - core

    def own_copy(i, layer):
        src, dst = slabs[i]
        return pltpu.make_async_copy(kv_mine if src is None else src(my_head), dst(layer), loc_sem.at[i])

    def twin_copy(i, layer):
        src, dst = slabs[i]
        return remote(kv_twin if src is None else src(twin_head), dst(layer), push_send.at[i], push_recv.at[i], here.twin)

    k_copy = pltpu.make_async_copy(cut(w_in, Q_COLS, 128, place), k_pair, misc.at[0])
    v_copy = pltpu.make_async_copy(cut(w_in, Q_COLS + KV_COLS, 128, place), v_pair, misc.at[1])
    k_copy.start()
    v_copy.start()
    for i in (0, 1):
        twin_copy(i, core).start()
        own_copy(i, core).start()
    other_rows = pl.ds(pl.multiple_of((1 - core) * SLOT, SLOT), SLOT)
    cross_copy = remote(ends.at[other_rows], cross, misc_send.at[0], misc_recv.at[0], here.twin)
    cross_copy.start()
    gain_copy = remote(gain_in, gain_out.at[core], misc_send.at[1], misc_recv.at[1], here.twin)
    gain_copy.start()
    gain_out[core] = gain_in[...]
    k_copy.wait()
    v_copy.wait()
    low = low_lanes(k_pair.shape)
    k, v = k_pair[...].astype(F32), v_pair[...].astype(F32)
    kv0 = jnp.where(low, k, pltpu.roll(v, 64, 1)).astype(BF16)
    kv1 = jnp.where(low, pltpu.roll(k, 64, 1), v).astype(BF16)
    kv_mine[...] = jnp.where(core == 0, kv0, kv1)
    kv_twin[...] = jnp.where(core == 0, kv1, kv0)
    for i in (2, 3, 4, 5):
        twin_copy(i, core).start()
        own_copy(i, core).start()

    PIECES = ((wa, (0, 1, 2)), (wg, (3, 4)), (wd, (5,)))
    half = part // 2

    def own_ready(layer, piece):
        @pl.when(core == layer)
        def _():
            for i in PIECES[piece][1]:
                own_copy(i, layer).wait()

        @pl.when(core != layer)
        def _():
            for i in PIECES[piece][1]:
                twin_copy(i, layer).wait_recv()

    def hop(layer, piece, which, rows, size, peer):
        ref = PIECES[piece][0].at[layer, pl.ds(pl.multiple_of(rows, size), size)]
        return remote(ref, ref, hop_send.at[layer, piece, which], hop_recv.at[layer, piece, which], peer)

    def hops(layer, piece):
        return (
            hop(layer, piece, 0, shard * part, part, here.x_peer),
            hop(layer, piece, 1, shard * part, part, here.y_peer),
            hop(layer, piece, 2, here.x_shard * part, half, here.y_peer),
            hop(layer, piece, 3, here.y_shard * part + half, half, here.x_peer),
        )

    def hop_one(layer, piece):
        own_ready(layer, piece)
        one, two, _, _ = hops(layer, piece)
        one.start()
        two.start()

    def hop_two(layer, piece):
        one, two, three, four = hops(layer, piece)
        one.wait_recv()
        three.start()
        two.wait_recv()
        four.start()

    def all_in(layer, piece):
        _, _, three, four = hops(layer, piece)
        three.wait_recv()
        four.wait_recv()

    hop_one(0, 0)

    rows8 = lens_in.shape[0]
    lens[pl.ds(pl.multiple_of((core * LINE + place) * rows8, rows8), rows8), :] = lens_in[...]
    line_gather(here, lens, len_sems, (), 1)
    cross_copy.wait()
    gain_copy.wait()
    first = core == 0
    ours0, others0 = ends[:SLOT].astype(F32), ends[SLOT:].astype(F32)
    crossed = cross[...].astype(F32)
    x = jnp.where(first, ours0, crossed)
    own_len = lens[pl.ds(pl.multiple_of((core * LINE + place) * 8, 8), 8), :][:1]
    live = lax.broadcasted_iota(jnp.int32, (SLOT, 128), 0).astype(F32) < own_len
    valid = jnp.where(live, 1.0, 0.0)[:, :1]
    cot_out[...] = (jnp.where(first, crossed, others0) * valid).astype(BF16)
    res[0] = x

    def own_block(ref):
        return ref.at[pl.ds(pl.multiple_of((core * LINE + place) * SLOT, SLOT), SLOT), :]

    def weight_out(layer, piece):
        dst = (wa_out, wg_out, wd_out)[piece].at[layer]
        return pltpu.make_async_copy(PIECES[piece][0].at[layer], dst, w_save.at[layer, piece])

    reduce_bufs = (sib_buf, rx_up, rx_dn, tx_up, tx_dn)
    half_rows = LINE * SLOT

    def layer(index):
        saves = []

        def keep(src, dst):
            copy = pltpu.make_async_copy(src, dst, save.at[index, len(saves)])
            copy.start()
            saves.append(copy)

        x = res[2 * index]
        own_block(seq)[...] = (x * root(x) * gain_out[index, 0:1]).astype(BF16)
        if index == 0:
            line_gather(here, seq, gather_sems, (None, None, lambda: (hop_two(0, 0), hop_one(0, 1))))
        else:
            line_gather(here, seq, gather_sems, (None, lambda: hop_one(1, 2)))
        keep(seq, xn_out.at[index])
        all_in(index, 0)
        weight_out(index, 0).start()

        def attend(pair, _):
            at = pl.ds(pl.multiple_of(pair * 2 * SLOT, 2 * SLOT), 2 * SLOT)
            wide = dot(seq[at, :], wa[index, :, :AO_AT])
            kv = turn(wide[:, KV_AT:AO_AT], tables[2], tables[3])
            q = jnp.concatenate(
                [turn(wide[:, 128 * i:128 * (i + 1)], tables[0], tables[1]) for i in range(GROUP // 2)], 1
            )
            kv_low = kv.astype(BF16)
            qkv[at, :Q_SLAB] = q.astype(BF16)
            qkv[at, KV_AT:AO_AT] = kv_low
            probs = two_slot_probs(spread_heads(q).astype(BF16), kv_low, lens, pair).astype(BF16)
            ctx[at, :] = join_heads(dot(probs, kv_low), True).astype(BF16)
            return 0

        lax.fori_loop(0, LINE, attend, 0)
        keep(qkv, qkv_out.at[index])
        keep(ctx, ctx_out.at[index])

        def reduce(src, weights, cols, meanwhile):
            def terms(whose, dst, sub):
                rows = pl.ds(pl.multiple_of(whose * half_rows, half_rows), half_rows)
                size = width // SUBS
                for lo in range(sub * size, (sub + 1) * size, 512):
                    at = slice(lo, lo + 512)
                    dst[:, at] = dot_last(src[rows, :], weights[index, at, cols]).astype(dst.dtype)

            line_reduce(here, total, ours, theirs, reduce_bufs, reduce_sems, terms, meanwhile)

        saves[0].wait()
        reduce(ctx, wa, slice(AO_AT, A_COLS), () if index == 0 else (None, None, lambda: hop_two(1, 1)))
        middle = x + total[...]
        res[1 + 2 * index] = middle
        own_block(hnb)[...] = (middle * root(middle) * gain_out[index, 1:2]).astype(BF16)
        if index == 0:
            line_gather(here, hnb, gather_sems, (None, lambda: hop_one(0, 2), None, lambda: hop_two(0, 1)))
            own_block(dm)[...] = cot_out[...]
            line_gather(here, dm, dm_sems)
            pltpu.make_async_copy(dm, dm_out, misc.at[0]).start()
        else:
            line_gather(here, hnb, gather_sems, (None, None, lambda: hop_two(1, 2)))
        keep(hnb, hn_out.at[index])
        all_in(index, 1)
        weight_out(index, 1).start()

        def gate_up(n, _):
            at = pl.ds(pl.multiple_of(n * 256, 256), 256)
            at_up = pl.ds(pl.multiple_of(FF_SLAB + n * 256, 256), 256)
            gate = dot(hnb[...], wg[index, :, at])
            up = dot(hnb[...], wg[index, :, at_up])
            gu[:, at] = gate
            gu[:, at_up] = up
            hid[:, at] = (gate * jax.nn.sigmoid(gate) * up).astype(BF16)
            return 0

        lax.fori_loop(0, FF_SLAB // 256, gate_up, 0)
        keep(gu, gu_out.at[index])
        keep(hid, hid_out.at[index])
        if index == 0:
            hop_one(1, 0)
            hop_two(0, 2)
            hop_one(1, 1)
        all_in(index, 2)
        weight_out(index, 2).start()
        saves[3].wait()
        if index == 0:
            reduce(hid, wd, slice(None), (None, lambda: hop_two(1, 0)))
            res[2] = (res[1] + total[...]).astype(BF16).astype(F32)
        for i in (1, 2, 4, 5):
            saves[i].wait()

    layer(0)
    layer(1)
    pltpu.make_async_copy(dm, dm_out, misc.at[0]).wait()
    for i in range(4):
        pltpu.make_async_copy(res.at[i], res_out.at[i], misc.at[i]).start()
    for i in range(4):
        pltpu.make_async_copy(res.at[i], res_out.at[i], misc.at[i]).wait()
    for i in range(6):
        twin_copy(i, core).wait_send()
    for index in range(2):
        for piece in range(3):
            weight_out(index, piece).wait()
            for move in hops(index, piece):
                move.wait_send()


def forward_call(ends, lens, gain, tables, w_in, w_out):
    width = ends.shape[1]
    rows = LINE * CORES * SLOT
    hbm = pl.BlockSpec(memory_space=pl.ANY)
    vmem = pl.BlockSpec(memory_space=pltpu.VMEM)
    shape = jax.ShapeDtypeStruct
    dma = pltpu.SemaphoreType.DMA
    line = dma((LINE, SUBS))
    block = pltpu.VMEM((LINE * SLOT, width), BF16)
    return pl.pallas_call(
        forward_body,
        out_shape=[
            shape((2, width, A_COLS), BF16),
            shape((2, width, 2 * FF_SLAB), BF16),
            shape((2, width, FF_SLAB), BF16),
            shape((2, rows, width), BF16),
            shape((2, rows, width), BF16),
            shape((2, rows, AO_AT), BF16),
            shape((2, rows, Q_SLAB), BF16),
            shape((2, rows, 2 * FF_SLAB), F32),
            shape((2, rows, FF_SLAB), BF16),
            shape((4, SLOT, width), F32),
            shape((rows, width), BF16),
            shape((SLOT, width), BF16),
            shape((2, 2, width), F32),
            shape((LINE * CORES * 8, 128), F32),
        ],
        in_specs=[vmem, vmem, vmem, vmem, hbm, hbm],
        out_specs=[hbm] * 11 + [vmem] * 3,
        scratch_shapes=[
            pltpu.VMEM((SLOT, width), BF16),
            pltpu.VMEM((w_in.shape[0], 128), BF16),
            pltpu.VMEM((w_in.shape[0], 128), BF16),
            pltpu.VMEM((w_in.shape[0], 128), BF16),
            pltpu.VMEM((w_in.shape[0], 128), BF16),
            pltpu.VMEM((2, width, A_COLS), BF16),
            pltpu.VMEM((2, width, 2 * FF_SLAB), BF16),
            pltpu.VMEM((2, width, FF_SLAB), BF16),
            pltpu.VMEM((rows, width), BF16),
            pltpu.VMEM((rows, width), BF16),
            pltpu.VMEM((rows, AO_AT), BF16),
            pltpu.VMEM((rows, Q_SLAB), BF16),
            pltpu.VMEM((rows, 2 * FF_SLAB), F32),
            pltpu.VMEM((rows, FF_SLAB), BF16),
            block,
            pltpu.VMEM((LINE * SLOT, width), F32),
            pltpu.VMEM((4, SLOT, width), F32),
            pltpu.VMEM((SLOT, width), F32),
            pltpu.VMEM((rows, width), BF16),
            block, block, block, block, block,
            dma((6,)), dma((6,)), dma((6,)), dma((2, 3, 4)), dma((2, 3, 4)),
            dma((4,)), dma((2,)), dma((2,)), dma((2, 6)), dma((2, 3)),
        ] + [line] * 21,
        compiler_params=pltpu.CompilerParams(
            collective_id=0, has_side_effects=True, vmem_limit_bytes=60 * 2**20
        ),
        name="forward_two_layers",
        cost_estimate=pl.CostEstimate(flops=16_000_000_000, bytes_accessed=600_000_000, transcendentals=0),
    )(ends, lens, gain, tables, w_in, w_out)


def spread_heads_high(wide):
    low = low_lanes((wide.shape[0], 128))
    parts = []
    for pair in range(GROUP // 2):
        block = wide[:, pair * 128:(pair + 1) * 128]
        parts.append(jnp.where(low, 0.0, pltpu.roll(block, 64, 1)))
        parts.append(jnp.where(low, 0.0, block))
    return jnp.concatenate(parts, 0)


CHUNKS = ((0, FF_SLAB), (FF_SLAB, FF_SLAB), (2 * FF_SLAB, FF_SLAB), (3 * FF_SLAB, A_COLS))
SLAB = 3 * FF_SLAB + A_COLS
FAR_SLOT = (1, 0, 0, 1)
WINDOW, EACH = 16, 16


def backward_body(
    replicas,
    cot_in, gain, lens, tables, res_in, dm_in, wa_in, wg_in, wd_in, xn_in, hn_in, qkv_in, ctx_in, gu_in, hid_in,
    fin, ends_out, gain_out, far_rx, near_rx,
    wa, wg, wd, xn, hn, qkv, ctx, gu, hid, dm, da, dgu, dqkv, theirs, ours, total, res,
    sib_buf, rx_up, rx_dn, tx_up, tx_dn, tx_far, tx_x, tx_y, tx_fin, stage, gain_loc, gain_x, gain_y, gain_line,
    end_tx, end_rx,
    load_sem, gu_sem, res_sem, far_send, far_recv, near_send, near_recv, fin_send, fin_recv, stage_sem, misc_send, misc_recv,
    *line_sems,
):
    gather_sems, gain_sems, reduce_sems = line_sems[:5], line_sems[5:10], line_sems[10:]
    here = Here()
    core, shard, place = here.core, here.shard, here.place
    width = cot_in.shape[1]
    part = width // SHARDS
    half = part // 2
    half_rows = LINE * SLOT
    base = here.depth - place

    barrier = pltpu.get_barrier_semaphore()
    for peer in (here.x_peer, here.y_peer):
        pl.semaphore_signal(barrier, inc=1, device_id=peer)
    for other in range(CORES):
        for where in range(LINE):
            @pl.when((core != other) | (place != where))
            def _():
                pl.semaphore_signal(barrier, inc=1, device_id={"section": other, "dp": base + where})

    pl.semaphore_wait(barrier, 2 + CORES * LINE - 1)

    NAMES = ("dm", "wd", "wg", "wa", "hid", "qkv", "ctx", "hn", "xn")
    VIEWS = {
        "wd": (wd_in, lambda l: wd), "wg": (wg_in, lambda l: wg), "wa": (wa_in, lambda l: wa),
        "hid": (hid_in, lambda l: hid), "qkv": (qkv_in, lambda l: qkv.at[l]), "ctx": (ctx_in, lambda l: ctx.at[l]),
        "hn": (hn_in, lambda l: hn), "xn": (xn_in, lambda l: xn),
    }

    def load(name, layer):
        if name == "dm":
            return pltpu.make_async_copy(dm_in, dm.at[1], load_sem.at[1, 0])
        src, dst = VIEWS[name]
        return pltpu.make_async_copy(src.at[layer], dst(layer), load_sem.at[layer, NAMES.index(name)])

    def gu_loads(layer, tile):
        return [
            pltpu.make_async_copy(
                gu_in.at[layer, :, pl.ds(i * FF_SLAB + tile * 256, 256)],
                gu.at[tile % 2, :, pl.ds(i * 256, 256)], gu_sem.at[tile % 2, i])
            for i in range(2)
        ]

    for tile in range(2):
        for copy in gu_loads(1, tile):
            copy.start()
    for name in NAMES:
        load(name, 1).start()

    ready = set()

    def need(name, layer):
        if (name, layer) not in ready:
            ready.add((name, layer))
            load(name, layer).wait()

    gain_loc[...] = jnp.zeros_like(gain_loc)

    pending = {}

    waiting = []

    def pump(count):
        for _ in range(min(count, len(waiting))):
            waiting.pop(0).start()

    def claim(key):
        moves = pending.pop(key, ())
        for move in moves:
            if move in waiting:
                waiting.remove(move)
                move.start()
        for move in moves:
            move.wait_send()

    def products(layer, chunk, block, put):
        at = pl.ds(pl.multiple_of(block * part, part), part)
        need("hn" if chunk < 2 else "hid" if chunk == 2 else "xn", layer)

        def tiles(lhs, rhs, size, to):
            for lo in range(0, size, 512):
                hi = min(lo + 512, size)
                put(slice(to + lo, to + hi), dot_rows(lhs[:, at], rhs[:, lo:hi]))

        if chunk < 2:
            tiles(hn, dgu.at[layer, :, pl.ds(chunk * FF_SLAB, FF_SLAB)], FF_SLAB, 0)
        elif chunk == 2:
            tiles(dm.at[layer], hid, FF_SLAB, 0)
        else:
            tiles(xn, dqkv.at[layer], AO_AT, 0)
            tiles(da.at[layer], ctx.at[layer], Q_SLAB, AO_AT)

    def far_moves(layer, chunk):
        lo, size = CHUNKS[chunk]
        src = tx_far.at[FAR_SLOT[chunk]]
        cols = pl.ds(0, size)
        return [
            remote(src.at[pl.ds(i * half, half), cols], far_rx.at[layer, i, :, pl.ds(lo, size)],
                   far_send.at[layer, chunk, i], far_recv.at[layer, chunk, i], peer)
            for i, peer in ((0, here.x_peer), (1, here.y_peer))
        ]

    def near_moves(layer, chunk):
        lo, size = CHUNKS[chunk]
        cols = pl.ds(0, size)
        return [
            remote(src.at[chunk % 2, :, cols], near_rx.at[layer, i, :, pl.ds(lo, size)],
                   near_send.at[layer, chunk, i], near_recv.at[layer, chunk, i], peer)
            for i, (src, peer) in enumerate(((tx_x, here.x_peer), (tx_y, here.y_peer)))
        ]

    def stage_far(layer, chunk, i):
        lo, size = CHUNKS[chunk]
        return pltpu.make_async_copy(
            far_rx.at[layer, i, :, pl.ds(lo, size)], stage.at[i, pl.ds(0, half), pl.ds(0, size)], stage_sem.at[i])

    def stage_near(layer, chunk, i):
        lo, size = CHUNKS[chunk]
        return pltpu.make_async_copy(
            near_rx.at[layer, i, :, pl.ds(lo, size)], stage.at[i, :, pl.ds(0, size)], stage_sem.at[i])

    def step_one(layer, chunk):
        claim(("far", FAR_SLOT[chunk]))

        def put(cols, value):
            tx_far[FAR_SLOT[chunk], :, cols] = value.astype(BF16)

        products(layer, chunk, here.far_shard, put)
        moves = far_moves(layer, chunk)
        for move in moves:
            move.start()
        pending["far", FAR_SLOT[chunk]] = moves

    def step_two(layer, chunk):
        arrivals = far_moves(layer, chunk)
        for i in (1, 0):
            arrivals[i].wait_recv()
            stage_far(layer, chunk, i).start()
        claim(("near", chunk % 2))
        moves = near_moves(layer, chunk)

        def put_x(cols, value):
            tx_x[chunk % 2, :half, cols] = value[:half].astype(BF16)
            tx_x[chunk % 2, half:, cols] = (value[half:] + stage[1, :half, cols].astype(F32)).astype(BF16)

        def put_y(cols, value):
            tx_y[chunk % 2, :half, cols] = (value[:half] + stage[0, :half, cols].astype(F32)).astype(BF16)
            tx_y[chunk % 2, half:, cols] = value[half:].astype(BF16)

        stage_far(layer, chunk, 1).wait()
        products(layer, chunk, here.x_shard, put_x)
        moves[0].start()
        stage_far(layer, chunk, 0).wait()
        products(layer, chunk, here.y_shard, put_y)
        moves[1].start()
        pending["near", chunk % 2] = moves

    piece = part // (replicas * LINE)

    def fin_moves(layer, chunk):
        lo, size = CHUNKS[chunk]
        head = place * CORES + core
        moves = []
        for rep in range(replicas):
            for turn_by in (2, 3, 1, 0):
                where = lax.rem(place + turn_by, LINE)
                src = tx_fin.at[chunk % 2, pl.ds(pl.multiple_of((rep * LINE + where) * piece, piece), piece), pl.ds(0, size)]
                dst = fin.at[head, pl.ds(rep * piece, piece), pl.ds(lo, size)]
                same = (core == layer) & (place == where)
                move = remote(src, dst, fin_send.at[layer, chunk, rep, turn_by], fin_recv.at[rep, head, chunk],
                              {"section": layer, "dp": base + where})
                stay = pltpu.make_async_copy(src, dst, fin_send.at[layer, chunk, rep, turn_by])
                moves.append((same, move, stay))
        return moves

    class Leave:
        def __init__(self, entry):
            self.same, self.move, self.stay = entry

        def start(self):
            @pl.when(self.same)
            def _():
                self.stay.start()

            @pl.when(jnp.logical_not(self.same))
            def _():
                self.move.start()

        def wait_send(self):
            @pl.when(self.same)
            def _():
                self.stay.wait()

            @pl.when(jnp.logical_not(self.same))
            def _():
                self.move.wait_send()

    def step_three(layer, chunk):
        arrivals = near_moves(layer, chunk)
        for i in range(2):
            arrivals[i].wait_recv()
            stage_near(layer, chunk, i).start()
        claim(("fin", chunk % 2))
        stage_near(layer, chunk, 0).wait()
        stage_near(layer, chunk, 1).wait()

        def put(cols, value):
            tx_fin[chunk % 2, :, cols] = (
                value + stage[0, :, cols].astype(F32) + stage[1, :, cols].astype(F32)
            ).astype(BF16)

        products(layer, chunk, shard, put)
        moves = [Leave(entry) for entry in fin_moves(layer, chunk)]
        waiting.extend(moves)
        if layer == 0:
            pump(len(waiting))
        pending["fin", chunk % 2] = moves

    def steps(*todo):
        def run():
            pump(EACH)
            for kind, layer, chunk in todo:
                (step_one, step_two, step_three)[kind - 1](layer, chunk)
                if layer == 1 and kind == 3 and chunk == 0:
                    load("hn", 0).start()
                if layer == 1 and kind == 3 and chunk == 3:
                    load("xn", 0).start()
        return run

    reduce_bufs = (sib_buf, rx_up, rx_dn, tx_up, tx_dn)

    def own_block(ref, layer):
        return ref.at[layer, pl.ds(pl.multiple_of((core * LINE + place) * SLOT, SLOT), SLOT), :]

    def reduce(slot, src, weights, cols, meanwhile):
        res_load(slot).start()

        def terms(whose, dst, sub):
            rows = pl.ds(pl.multiple_of(whose * half_rows, half_rows), half_rows)
            size = width // SUBS
            for lo in range(sub * size, (sub + 1) * size, 512):
                at = slice(lo, lo + 512)
                dst[:, at] = dot_last(src[rows, :], weights[at, cols]).astype(dst.dtype)

        line_reduce(here, total, ours, theirs, reduce_bufs, reduce_sems, terms, meanwhile)

    def res_load(slot):
        return pltpu.make_async_copy(res_in.at[slot], res, res_sem.at[slot])

    def norm_back(gain_row, slot):
        res_load(slot).wait()
        values = res[...]
        scale = root(values)
        grad = total[...]
        hat = grad * gain_row
        gain_loc[slot:slot + 1, :] = jnp.sum(grad * values * scale, 0, keepdims=True)
        inner = jnp.mean(hat * values, -1, keepdims=True)
        return scale * hat - values * (scale * scale * scale * inner)

    def layer_back(layer, grad_out, jobs):
        if layer == 1:
            need("dm", 1)
        else:
            own_block(dm, layer)[...] = grad_out.astype(BF16)
            line_gather(here, dm.at[layer], gather_sems, jobs[0])
        pump(WINDOW)
        step_one(layer, 2)
        need("wd", layer)
        tiles = FF_SLAB // 256
        for tile in range(tiles):
            at = slice(tile * 256, tile * 256 + 256)
            at_up = slice(FF_SLAB + tile * 256, FF_SLAB + tile * 256 + 256)
            grad = dot(dm[layer], wd[:, at])
            for copy in gu_loads(layer, tile):
                copy.wait()
            gate, up = gu[tile % 2, :, :256], gu[tile % 2, :, 256:]
            sig = jax.nn.sigmoid(gate)
            dgu[layer, :, at] = (grad * up * sig * (1.0 + gate * (1.0 - sig))).astype(BF16)
            dgu[layer, :, at_up] = (grad * gate * sig).astype(BF16)
            ahead = (layer, tile + 2) if tile + 2 < tiles else (layer - 1, tile + 2 - tiles)
            if ahead[0] >= 0:
                for copy in gu_loads(*ahead):
                    copy.start()
        if layer == 1:
            load("wd", 0).start()
        step_one(layer, 0)
        need("wg", layer)
        reduce(2 * layer + 1, dgu.at[layer], wg, slice(None), jobs[1])
        if layer == 1:
            load("wg", 0).start()
        grad_mid = grad_out + norm_back(gain[layer, 1:2], 2 * layer + 1)
        own_block(da, layer)[...] = grad_mid.astype(BF16)
        line_gather(here, da.at[layer], gather_sems, jobs[2])
        pump(WINDOW)
        need("wa", layer)
        need("qkv", layer)
        need("ctx", layer)

        def attend(pair, _):
            at = pl.ds(pl.multiple_of(pair * 2 * SLOT, 2 * SLOT), 2 * SLOT)
            grad_ctx = dot(da[layer, at, :], wa[:, AO_AT:A_COLS]).astype(BF16).astype(F32)
            kv = qkv[layer, at, KV_AT:AO_AT]
            q = spread_heads(qkv[layer, at, :Q_SLAB].astype(F32)).astype(BF16)
            probs = two_slot_probs(q, kv, lens, pair)
            grad_high = spread_heads_high(grad_ctx).astype(BF16)
            grad_probs = dot_last(grad_high, kv)
            inner = jnp.sum(grad_probs * probs, -1, keepdims=True)
            grad_scores = (probs * (grad_probs - inner)).astype(BF16)
            grad_q = join_heads(dot(grad_scores, kv), False) * HEAD_DIM**-0.5
            grad_kv = dot_rows(grad_scores, q) * HEAD_DIM**-0.5 + dot_rows(probs.astype(BF16), grad_high)
            for i in range(GROUP // 2):
                cols = slice(128 * i, 128 * (i + 1))
                dqkv[layer, at, cols] = turn(grad_q[:, cols], tables[0], -tables[1]).astype(BF16)
            dqkv[layer, at, KV_AT:AO_AT] = turn(grad_kv, tables[2], -tables[3]).astype(BF16)
            return 0

        lax.fori_loop(0, LINE, attend, 0)
        reduce(2 * layer, dqkv.at[layer], wa, slice(0, AO_AT), jobs[3])
        if layer == 1:
            load("wa", 0).start()
            load("qkv", 0).start()
            load("ctx", 0).start()
        return grad_mid + norm_back(gain[layer, 0:1], 2 * layer)

    dx1 = layer_back(1, cot_in[...].astype(F32), (
        (),
        (steps((1, 1, 1)), steps((2, 1, 2))),
        (None, steps((2, 1, 1))),
        (steps((1, 1, 3), (2, 1, 0)), steps((3, 1, 2))),
    ))
    load("hid", 0).start()

    dx0 = layer_back(0, dx1.astype(BF16).astype(F32), (
        (steps((3, 1, 1)), None, steps((3, 1, 0), (2, 1, 3))),
        (steps((3, 1, 3), (1, 0, 1)), steps((2, 0, 2))),
        (None, steps((2, 0, 1))),
        (steps((1, 0, 3), (2, 0, 0)), steps((3, 0, 2))),
    ))

    again_wd = pltpu.make_async_copy(wd_in.at[1], wd, load_sem.at[1, NAMES.index("wd")])
    again_hid = pltpu.make_async_copy(hid_in.at[1], hid, load_sem.at[1, NAMES.index("hid")])
    again_wd.start()
    again_hid.start()
    gain_x_move = remote(gain_loc, gain_x, misc_send.at[1], misc_recv.at[1], here.x_peer)
    gain_x_move.start()
    steps((3, 0, 1))()
    gain_x_move.wait()
    gain_loc[...] += gain_x[...]
    gain_y_move = remote(gain_loc, gain_y, misc_send.at[2], misc_recv.at[2], here.y_peer)
    gain_y_move.start()
    steps((2, 0, 3))()
    gain_y_move.wait()
    cols = pl.ds(pl.multiple_of(shard * part, part), part)
    own_gains = pl.ds(pl.multiple_of((core * LINE + place) * 8, 8), 8)
    gain_line[own_gains, :] = gain_loc[:, cols] + gain_y[:, cols]
    line_gather(here, gain_line, gain_sems, (), 1)
    gain_sum = gain_line[0:8, :]
    for i in range(1, LINE * CORES):
        gain_sum += gain_line[8 * i:8 * i + 8, :]
    gain_out[...] = gain_sum

    again_wd.wait()
    again_hid.wait()
    reduce(3, hid, wd, slice(None), (None, steps((3, 0, 0))))
    res_load(3).wait()

    first = core == 0
    dx0 = dx0.astype(BF16).astype(F32)
    y1 = (res[...] + total[...]).astype(BF16).astype(F32)
    end_tx[...] = jnp.where(first, y1, dx0).astype(BF16)
    end_move = remote(end_tx, end_rx, misc_send.at[0], misc_recv.at[0], here.twin)
    end_move.start()
    steps((3, 0, 3))()
    end_move.wait()
    crossed = end_rx[...].astype(F32)
    ends_out[:SLOT] = jnp.where(first, dx0, crossed).astype(BF16)
    ends_out[SLOT:] = jnp.where(first, crossed, y1).astype(BF16)
    for key in list(pending):
        claim(key)
    for rep in range(replicas):
        for where in range(LINE):
            for other in range(CORES):
                head = where * CORES + other

                @pl.when((core != other) | (place != where))
                def _():
                    for chunk, (lo, size) in enumerate(CHUNKS):
                        src = tx_fin.at[0, pl.ds(0, piece), pl.ds(0, size)]
                        dst = fin.at[head, pl.ds(rep * piece, piece), pl.ds(lo, size)]
                        remote(src, dst, fin_send.at[0, 0, 0, 0], fin_recv.at[rep, head, chunk],
                               {"section": 1 - core, "dp": base + where}).wait_recv()


def backward_call(replicas, cot, gain, lens, tables, res, dm, wa, wg, wd, xn, hn, qkv, ctx, gu, hid):
    width = cot.shape[1]
    rows = LINE * CORES * SLOT
    part = width // SHARDS
    hbm = pl.BlockSpec(memory_space=pl.ANY)
    vmem = pl.BlockSpec(memory_space=pltpu.VMEM)
    shape = jax.ShapeDtypeStruct
    dma = pltpu.SemaphoreType.DMA
    line = dma((LINE, SUBS))
    vm = pltpu.VMEM
    block = vm((LINE * SLOT, width), BF16)
    move = vm((2, part, FF_SLAB), BF16)
    return pl.pallas_call(
        functools.partial(backward_body, replicas),
        out_shape=[
            shape((KV_HEADS, part // LINE, SLAB), BF16),
            shape((CORES * SLOT, width), BF16),
            shape((8, part), F32),
            shape((2, 2, part // 2, SLAB), BF16),
            shape((2, 2, part, SLAB), BF16),
        ],
        in_specs=[vmem] * 4 + [hbm] * 11,
        out_specs=[hbm, vmem, vmem, hbm, hbm],
        scratch_shapes=[
            vm((width, A_COLS), BF16), vm((width, 2 * FF_SLAB), BF16), vm((width, FF_SLAB), BF16),
            vm((rows, width), BF16), vm((rows, width), BF16), vm((2, rows, AO_AT), BF16), vm((2, rows, Q_SLAB), BF16),
            vm((2, rows, 512), F32), vm((rows, FF_SLAB), BF16),
            vm((2, rows, width), BF16), vm((2, rows, width), BF16),
            vm((2, rows, 2 * FF_SLAB), BF16), vm((2, rows, AO_AT), BF16),
            block, vm((LINE * SLOT, width), F32), vm((SLOT, width), F32), vm((SLOT, width), F32),
            block, block, block, block, block,
            move, move, move, move, move,
            vm((8, width), F32), vm((8, width), F32), vm((8, width), F32), vm((8 * LINE * CORES, part), F32),
            vm((SLOT, width), BF16), vm((SLOT, width), BF16),
            dma((2, 9)), dma((2, 2)), dma((4,)), dma((2, 4, 2)), dma((2, 4, 2)), dma((2, 4, 2)), dma((2, 4, 2)),
            dma((2, 4, replicas, LINE)), dma((replicas, KV_HEADS, 4)), dma((2,)), dma((3,)), dma((3,)),
        ] + [line] * 16,
        compiler_params=pltpu.CompilerParams(
            collective_id=1, has_side_effects=True, vmem_limit_bytes=61 * 2**20
        ),
        name="backward_two_layers",
        cost_estimate=pl.CostEstimate(flops=32_000_000_000, bytes_accessed=600_000_000, transcendentals=0),
    )(cot, gain, lens, tables, res, dm, wa, wg, wd, xn, hn, qkv, ctx, gu, hid)


def place_body(fin, in_out, out_out, held, wide_in, wide_out, load_sem, save_sem):
    steps = KV_HEADS // 2
    q_two, ff_two = 2 * Q_SLAB, 2 * FF_SLAB
    ff0 = Q_COLS + 2 * KV_COLS

    def fetch(step):
        return pltpu.make_async_copy(fin.at[pl.ds(2 * step, 2)], held.at[step % 2], load_sem.at[step % 2])

    def saves(step):
        slot = step % 2
        moves = []
        for i, (src, lo, dst, to, size) in enumerate((
            (wide_in, 0, in_out, step * q_two, q_two),
            (wide_in, q_two, in_out, Q_COLS + step * 128, 128),
            (wide_in, q_two + 128, in_out, Q_COLS + KV_COLS + step * 128, 128),
            (wide_in, q_two + 256, in_out, ff0 + step * ff_two, ff_two),
            (wide_in, q_two + 256 + ff_two, in_out, ff0 + FF + step * ff_two, ff_two),
            (wide_out, 0, out_out, step * q_two, q_two),
            (wide_out, q_two, out_out, Q_COLS + step * ff_two, ff_two),
        )):
            moves.append(pltpu.make_async_copy(
                src.at[slot, :, pl.ds(lo, size)], dst.at[:, pl.ds(to, size)], save_sem.at[slot, i]))
        return moves

    fetch(0).start()
    a_at = 3 * FF_SLAB
    for step in range(steps):
        slot = step % 2
        if step + 1 < steps:
            fetch(step + 1).start()
        fetch(step).wait()
        if step >= 2:
            for move in saves(step - 2):
                move.wait()
        for i in range(2):
            q_to = i * Q_SLAB
            wide_in[slot, :, q_to:q_to + Q_SLAB] = held[slot, i, :, a_at:a_at + Q_SLAB].astype(F32)
            wide_out[slot, :, q_to:q_to + Q_SLAB] = held[slot, i, :, a_at + AO_AT:a_at + A_COLS].astype(F32)
            for k, (src_ref, to) in enumerate(((wide_in, q_two + 256), (wide_in, q_two + 256 + ff_two), (wide_out, q_two))):
                at = to + i * FF_SLAB
                src_ref[slot, :, at:at + FF_SLAB] = held[slot, i, :, k * FF_SLAB:(k + 1) * FF_SLAB].astype(F32)
        one = held[slot, 0, :, a_at + KV_AT:a_at + AO_AT].astype(F32)
        two = held[slot, 1, :, a_at + KV_AT:a_at + AO_AT].astype(F32)
        low = low_lanes(one.shape)
        wide_in[slot, :, q_two:q_two + 128] = jnp.where(low, one, pltpu.roll(two, 64, 1))
        wide_in[slot, :, q_two + 128:q_two + 256] = jnp.where(low, pltpu.roll(one, 64, 1), two)
        for move in saves(step):
            move.start()
    for step in range(max(steps - 2, 0), steps):
        for move in saves(step):
            move.wait()


def place_call(fin, in_cols, out_cols):
    rows = fin.shape[1]
    hbm = pl.BlockSpec(memory_space=pl.ANY)
    q_two, ff_two = 2 * Q_SLAB, 2 * FF_SLAB
    return pl.pallas_call(
        place_body,
        out_shape=[jax.ShapeDtypeStruct((rows, in_cols), F32), jax.ShapeDtypeStruct((rows, out_cols), F32)],
        in_specs=[hbm],
        out_specs=[hbm, hbm],
        scratch_shapes=[
            pltpu.VMEM((2, 2, rows, SLAB), BF16),
            pltpu.VMEM((2, rows, q_two + 256 + 2 * ff_two), F32),
            pltpu.VMEM((2, rows, q_two + ff_two), F32),
            pltpu.SemaphoreType.DMA((2,)),
            pltpu.SemaphoreType.DMA((2, 7)),
        ],
        compiler_params=pltpu.CompilerParams(vmem_limit_bytes=32 * 2**20),
        name="place_columns",
    )(fin)


def rope_blocks():
    half_dim = HEAD_DIM // 2
    inverse = 500000.0 ** (-(jnp.arange(half_dim, dtype=F32) * 2.0 / HEAD_DIM))
    angles = jnp.arange(SLOT, dtype=F32)[:, None] * inverse[None, :]
    cos, sin = jnp.cos(angles), jnp.sin(angles)
    one, zero = jnp.ones((SLOT, HEAD_DIM), F32), jnp.zeros((SLOT, HEAD_DIM), F32)
    rows = [
        jnp.concatenate([cos] * 4, 1),
        jnp.concatenate([-sin, sin] * 2, 1),
        jnp.concatenate([cos, cos, one], 1),
        jnp.concatenate([-sin, sin, zero], 1),
    ]
    return jnp.stack([jnp.tile(block, (2, 1)) for block in rows])


def local(ends_in, in_weight, out_weight, norm_gain, seq_len):
    core = lax.axis_index("section")
    replicas = lax.axis_size("dp") // LINE
    own_length = jnp.where(core == 0, seq_len[0], seq_len[1])
    lens_block = jnp.full((8, 128), own_length.astype(F32))
    rope = rope_blocks()
    (wa, wg, wd, xn, hn, qkv, ctx, gu, hid, res, dm, cot, gains, lens) = forward_call(
        ends_in[0], lens_block, norm_gain[0], rope, in_weight[0], out_weight[0]
    )
    fin, ends_out, gain_sum, _, _ = backward_call(
        replicas, cot, gains, lens, rope, res, dm, wa, wg, wd, xn, hn, qkv, ctx, gu, hid
    )
    own_gain = lax.dynamic_slice_in_dim(gain_sum, 2 * core, 2, 0)
    if replicas > 1:
        groups = [[r * LINE + p for r in range(replicas)] for p in range(LINE)]
        fin = lax.psum_scatter(fin, "dp", scatter_dimension=1, tiled=True, axis_index_groups=groups)
        own_gain = lax.psum(own_gain, "dp", axis_index_groups=groups)
    in_grad, out_grad = place_call(fin, in_weight.shape[2], out_weight.shape[2])
    size = own_gain.shape[1] // lax.axis_size("dp")
    own_gain = lax.dynamic_slice_in_dim(own_gain, lax.axis_index("dp") * size, size, 1)
    return ends_out[None], in_grad[None], out_grad[None], own_gain[None]


def solution(mesh):
    in_specs = (
        P("section", ("shard", "dp"), None),
        P("section", "shard", None),
        P("section", "shard", None),
        P("section", None, None),
        P(("shard", "dp")),
    )
    out_specs = (
        P("section", ("shard", "dp"), None),
        P("section", ("shard", "dp"), None),
        P("section", ("shard", "dp"), None),
        P("section", None, ("shard", "dp")),
    )
    return jax.shard_map(local, mesh=mesh, in_specs=in_specs, out_specs=out_specs, check_vma=False)
```

```python
import functools

import jax
import jax.numpy as jnp
from jax import lax
from jax.experimental import pallas as pl
from jax.experimental.pallas import tpu as pltpu
from jax.sharding import PartitionSpec as P

HEADS = 32
KV_HEADS = 8
GROUP = HEADS // KV_HEADS
HEAD_DIM = 64
FF = 8192
EPSILON = 1e-05
BF16 = jnp.bfloat16
F32 = jnp.float32
CORES = 2
LINE = KV_HEADS // CORES
SHARDS = 4
SLOT = 64
SUBS = 2
Q_SLAB = GROUP * HEAD_DIM
QKV_SLAB = Q_SLAB + 2 * HEAD_DIM
FF_SLAB = FF // KV_HEADS
Q_COLS = HEADS * HEAD_DIM
KV_COLS = KV_HEADS * HEAD_DIM


class Here:
    def __init__(self):
        self.core = lax.axis_index("section")
        self.shard = lax.axis_index("shard")
        self.depth = lax.axis_index("dp")
        self.place = lax.rem(self.depth, LINE)
        self.twin = {"section": 1 - self.core}
        self.x_shard = self.shard + 1 - 2 * lax.rem(self.shard, 2)
        self.y_shard = lax.rem(self.shard + 2, SHARDS)
        self.far_shard = SHARDS - 1 - self.shard
        self.x_peer = {"shard": self.x_shard}
        self.y_peer = {"shard": self.y_shard}
        self.above = {"dp": self.depth + 1}
        self.below = {"dp": self.depth - 1}
        self.has_above = self.place < LINE - 1
        self.has_below = self.place > 0

    def greet(self):
        barrier = pltpu.get_barrier_semaphore()
        for peer in (self.twin, self.x_peer, self.y_peer):
            pl.semaphore_signal(barrier, inc=1, device_id=peer)

        @pl.when(self.has_above)
        def _():
            pl.semaphore_signal(barrier, inc=1, device_id=self.above)

        @pl.when(self.has_below)
        def _():
            pl.semaphore_signal(barrier, inc=1, device_id=self.below)

        pl.semaphore_wait(barrier, jnp.where(self.has_above & self.has_below, 5, 4))


def remote(src, dst, send, recv, device):
    return pltpu.make_async_remote_copy(src, dst, send, recv, device_id=device)


def rows_at(ref, start, size):
    return ref.at[pl.ds(pl.multiple_of(start, size), size)]


def line_gather(here, buf, sems, meanwhile=(), subs=SUBS):
    up_send, dn_send, sib_send, z_recv, sib_recv = sems
    rows = buf.shape[0] // (LINE * CORES)
    size = rows // subs
    core, place = here.core, here.place
    meanwhile = list(meanwhile) + [None] * (LINE + 1)

    def part(where, whose, sub):
        return rows_at(buf, (whose * LINE + where) * rows + sub * size, size)

    def up(where, sub):
        mine = part(where, core, sub)
        return remote(mine, mine, up_send.at[where, sub], z_recv.at[where, sub], here.above)

    def down(where, sub):
        mine = part(where, core, sub)
        return remote(mine, mine, dn_send.at[where, sub], z_recv.at[where, sub], here.below)

    def across(where, whose, sub):
        mine = part(where, whose, sub)
        return remote(mine, mine, sib_send.at[where, sub], sib_recv.at[where, sub], here.twin)

    for sub in range(subs):
        @pl.when(here.has_above)
        def _():
            up(place, sub).start()

        @pl.when(here.has_below)
        def _():
            down(place, sub).start()

    for sub in range(subs):
        across(place, core, sub).start()
    for step in range(1, LINE):
        if meanwhile[step - 1] is not None:
            meanwhile[step - 1]()
        for sub in range(subs):
            @pl.when(place >= step)
            def _():
                up(place - step, sub).wait_recv()

                @pl.when(here.has_above)
                def _():
                    up(place - step, sub).start()

                across(place - step, core, sub).start()

            @pl.when(place + step < LINE)
            def _():
                down(place + step, sub).wait_recv()

                @pl.when(here.has_below)
                def _():
                    down(place + step, sub).start()

                across(place + step, core, sub).start()

    if meanwhile[LINE - 1] is not None:
        meanwhile[LINE - 1]()
    for where in range(LINE):
        for sub in range(subs):
            across(where, 1 - core, sub).wait_recv()

    for where in range(LINE):
        for sub in range(subs):
            across(where, core, sub).wait_send()

            @pl.when((where <= place) & here.has_above)
            def _():
                up(where, sub).wait_send()

            @pl.when((where >= place) & here.has_below)
            def _():
                down(where, sub).wait_send()


def line_reduce_steps(here, out, ours, theirs, bufs, sems, terms):
    sib_buf, rx_up, rx_dn, tx_up, tx_dn = bufs
    sib_send, sib_recv, up_send, up_recv, dn_send, dn_recv = sems
    rows, width = out.shape
    size = width // SUBS
    place, core = here.place, here.core

    def cols(sub):
        return slice(sub * size, (sub + 1) * size)

    def part(ref, where, sub):
        return ref.at[pl.ds(pl.multiple_of(where * rows, rows), rows), pl.ds(sub * size, size)]

    def read(ref, where, sub):
        return ref[pl.ds(pl.multiple_of(where * rows, rows), rows), cols(sub)].astype(F32)

    def across(where, sub):
        return remote(part(theirs, where, sub), part(sib_buf, where, sub),
                      sib_send.at[where, sub], sib_recv.at[where, sub], here.twin)

    def up(where, sub):
        return remote(part(tx_up, where, sub), part(rx_up, where, sub),
                      up_send.at[where, sub], up_recv.at[where, sub], here.above)

    def down(where, sub):
        return remote(part(tx_dn, where, sub), part(rx_dn, where, sub),
                      dn_send.at[where, sub], dn_recv.at[where, sub], here.below)

    def summed(where, sub):
        return read(ours, where, sub) + read(sib_buf, where, sub)

    def put(ref, where, sub, value):
        ref[pl.ds(pl.multiple_of(where * rows, rows), rows), cols(sub)] = value.astype(BF16)

    def begin(sub):
        terms(1 - core, theirs, sub)
        for step in range(LINE - 1, 0, -1):
            @pl.when(place + step < LINE)
            def _():
                across(place + step, sub).start()

            @pl.when(place >= step)
            def _():
                across(place - step, sub).start()

        across(place, sub).start()
        terms(core, ours, sub)

    def turn_on(step, sub):
        @pl.when(place + step < LINE)
        def _():
            where = place + step
            across(where, sub).wait_recv()

            @pl.when(here.has_below)
            def _():
                up(where, sub).wait_recv()
                put(tx_up, where, sub, summed(where, sub) + read(rx_up, where, sub))

            @pl.when(place == 0)
            def _():
                put(tx_up, where, sub, summed(where, sub))

            up(where, sub).start()

        @pl.when(place >= step)
        def _():
            where = place - step
            across(where, sub).wait_recv()

            @pl.when(here.has_above)
            def _():
                down(where, sub).wait_recv()
                put(tx_dn, where, sub, summed(where, sub) + read(rx_dn, where, sub))

            @pl.when(place == LINE - 1)
            def _():
                put(tx_dn, where, sub, summed(where, sub))

            down(where, sub).start()

    for sub in range(SUBS):
        begin(sub)
        turn_on(LINE - 1, sub)
    for step in range(LINE - 2, -1, -1):
        yield
        if step > 0:
            for sub in range(SUBS):
                turn_on(step, sub)

    for sub in range(SUBS):
        across(place, sub).wait_recv()
        out[:, cols(sub)] = summed(place, sub)

        @pl.when(here.has_below)
        def _():
            up(place, sub).wait_recv()
            out[:, cols(sub)] += read(rx_up, place, sub)

        @pl.when(here.has_above)
        def _():
            down(place, sub).wait_recv()
            out[:, cols(sub)] += read(rx_dn, place, sub)

    for where in range(LINE):
        for sub in range(SUBS):
            across(where, sub).wait_send()

            @pl.when(where > place)
            def _():
                up(where, sub).wait_send()

            @pl.when(where < place)
            def _():
                down(where, sub).wait_send()


def line_reduce(here, out, ours, theirs, bufs, sems, terms, meanwhile=()):
    jobs = list(meanwhile)
    for _ in line_reduce_steps(here, out, ours, theirs, bufs, sems, terms):
        if jobs:
            job = jobs.pop(0)
            if job is not None:
                job()


def dot(a, b):
    return jnp.dot(a, b, preferred_element_type=F32)


def dot_last(a, b):
    return lax.dot_general(a, b, (((1,), (1,)), ((), ())), preferred_element_type=F32)


def dot_rows(a, b):
    return lax.dot_general(a, b, (((0,), (0,)), ((), ())), preferred_element_type=F32)


def low_lanes(shape, size=HEAD_DIM):
    return lax.rem(lax.broadcasted_iota(jnp.int32, shape, 1), 2 * size) < size


def turn(block, cosine, sine):
    half = HEAD_DIM // 2
    other = jnp.where(low_lanes(block.shape, half), pltpu.roll(block, 128 - half, 1), pltpu.roll(block, half, 1))
    return block * cosine + other * sine


def spread_heads(wide):
    low = low_lanes((wide.shape[0], 128))
    parts = []
    for pair in range(GROUP // 2):
        block = wide[:, pair * 128:(pair + 1) * 128]
        parts.append(jnp.where(low, block, 0.0))
        parts.append(jnp.where(low, pltpu.roll(block, 64, 1), 0.0))
    return jnp.concatenate(parts, 0)


def join_heads(tall, from_high):
    rows = tall.shape[0] // GROUP
    low = low_lanes((rows, 128))
    parts = []
    for pair in range(GROUP // 2):
        one = tall[2 * pair * rows:(2 * pair + 1) * rows]
        two = tall[(2 * pair + 1) * rows:(2 * pair + 2) * rows]
        if from_high:
            parts.append(jnp.where(low, pltpu.roll(one, 64, 1), two))
        else:
            parts.append(jnp.where(low, one, pltpu.roll(two, 64, 1)))
    return jnp.concatenate(parts, 1)


def two_slot_probs(spread, kv, lens, pair):
    rows = 2 * SLOT
    q_at = lax.broadcasted_iota(jnp.int32, (rows, rows), 0)
    k_at = lax.broadcasted_iota(jnp.int32, (rows, rows), 1)
    first = lens[pl.ds(pl.multiple_of(16 * pair, 8), 8), :][:1]
    second = lens[pl.ds(pl.multiple_of(16 * pair + 8, 8), 8), :][:1]
    k_len = jnp.where(lax.broadcasted_iota(jnp.int32, (1, rows), 1) < SLOT, first, second)
    k_pos = jnp.where(k_at < SLOT, k_at, k_at - SLOT).astype(F32)
    allowed = (q_at >= k_at) & ((q_at < SLOT) | (k_at >= SLOT)) & (k_pos < k_len)
    allowed = jnp.concatenate([jnp.where(allowed, 1.0, 0.0)] * GROUP, 0)
    scores = dot_last(spread, kv) * HEAD_DIM**-0.5
    scores = jnp.where(allowed > 0.5, scores, -1e30)
    terms = jnp.exp(scores - jnp.max(scores, -1, keepdims=True))
    return terms / jnp.sum(terms, -1, keepdims=True)


def root(values):
    return lax.rsqrt(jnp.mean(values * values, -1, keepdims=True) + EPSILON)


Q_AT, KV_AT, AO_AT = 0, Q_SLAB, Q_SLAB + 2 * HEAD_DIM
A_COLS = AO_AT + Q_SLAB


def forward_body(
    ends, lens_in, gain_in, tables, w_in, w_out,
    wa_out, wg_out, wd_out, xn_out, hn_out, qkv_out, ctx_out, gu_out, hid_out, res_out, dm_out, cot_out, gain_out, lens,
    cross, k_pair, v_pair, kv_mine, kv_twin, wa, wg, wd, seq, hnb, qkv, ctx, gu, hid, theirs, ours, res, total, dm,
    sib_buf, rx_up, rx_dn, tx_up, tx_dn,
    loc_sem, push_send, push_recv, hop_send, hop_recv, misc, misc_send, misc_recv, save, w_save,
    *line_sems,
):
    gather_sems, len_sems, dm_sems, reduce_sems = line_sems[:5], line_sems[5:10], line_sems[10:15], line_sems[15:]
    here = Here()
    core, shard, place = here.core, here.shard, here.place
    width = ends.shape[1]
    part = w_in.shape[0]
    here.greet()

    own_rows = pl.ds(pl.multiple_of(shard * part, part), part)

    def cut(ref, base, size, head):
        return ref.at[:, pl.ds(pl.multiple_of(base + head * size, size), size)]

    ff0 = Q_COLS + 2 * KV_COLS
    slabs = [
        (lambda h: cut(w_in, 0, Q_SLAB, h), lambda l: wa.at[l, own_rows, pl.ds(Q_AT, Q_SLAB)]),
        (lambda h: cut(w_out, 0, Q_SLAB, h), lambda l: wa.at[l, own_rows, pl.ds(AO_AT, Q_SLAB)]),
        (None, lambda l: wa.at[l, own_rows, pl.ds(KV_AT, 2 * HEAD_DIM)]),
        (lambda h: cut(w_in, ff0, FF_SLAB, h), lambda l: wg.at[l, own_rows, pl.ds(0, FF_SLAB)]),
        (lambda h: cut(w_in, ff0 + FF, FF_SLAB, h), lambda l: wg.at[l, own_rows, pl.ds(FF_SLAB, FF_SLAB)]),
        (lambda h: cut(w_out, Q_COLS, FF_SLAB, h), lambda l: wd.at[l, own_rows]),
    ]
    my_head, twin_head = place * CORES + core, place * CORES + 1 - core

    def own_copy(i, layer):
        src, dst = slabs[i]
        return pltpu.make_async_copy(kv_mine if src is None else src(my_head), dst(layer), loc_sem.at[i])

    def twin_copy(i, layer):
        src, dst = slabs[i]
        return remote(kv_twin if src is None else src(twin_head), dst(layer), push_send.at[i], push_recv.at[i], here.twin)

    k_copy = pltpu.make_async_copy(cut(w_in, Q_COLS, 128, place), k_pair, misc.at[0])
    v_copy = pltpu.make_async_copy(cut(w_in, Q_COLS + KV_COLS, 128, place), v_pair, misc.at[1])
    k_copy.start()
    v_copy.start()
    for i in (0, 1):
        twin_copy(i, core).start()
        own_copy(i, core).start()
    other_rows = pl.ds(pl.multiple_of((1 - core) * SLOT, SLOT), SLOT)
    cross_copy = remote(ends.at[other_rows], cross, misc_send.at[0], misc_recv.at[0], here.twin)
    cross_copy.start()
    gain_copy = remote(gain_in, gain_out.at[core], misc_send.at[1], misc_recv.at[1], here.twin)
    gain_copy.start()
    gain_out[core] = gain_in[...]
    k_copy.wait()
    v_copy.wait()
    low = low_lanes(k_pair.shape)
    k, v = k_pair[...].astype(F32), v_pair[...].astype(F32)
    kv0 = jnp.where(low, k, pltpu.roll(v, 64, 1)).astype(BF16)
    kv1 = jnp.where(low, pltpu.roll(k, 64, 1), v).astype(BF16)
    kv_mine[...] = jnp.where(core == 0, kv0, kv1)
    kv_twin[...] = jnp.where(core == 0, kv1, kv0)
    for i in (2, 3, 4, 5):
        twin_copy(i, core).start()
        own_copy(i, core).start()

    PIECES = ((wa, (0, 1, 2)), (wg, (3, 4)), (wd, (5,)))
    half = part // 2

    def own_ready(layer, piece):
        @pl.when(core == layer)
        def _():
            for i in PIECES[piece][1]:
                own_copy(i, layer).wait()

        @pl.when(core != layer)
        def _():
            for i in PIECES[piece][1]:
                twin_copy(i, layer).wait_recv()

    def hop(layer, piece, which, rows, size, peer):
        ref = PIECES[piece][0].at[layer, pl.ds(pl.multiple_of(rows, size), size)]
        return remote(ref, ref, hop_send.at[layer, piece, which], hop_recv.at[layer, piece, which], peer)

    def hops(layer, piece):
        return (
            hop(layer, piece, 0, shard * part, part, here.x_peer),
            hop(layer, piece, 1, shard * part, part, here.y_peer),
            hop(layer, piece, 2, here.x_shard * part, half, here.y_peer),
            hop(layer, piece, 3, here.y_shard * part + half, half, here.x_peer),
        )

    def hop_one(layer, piece):
        own_ready(layer, piece)
        one, two, _, _ = hops(layer, piece)
        one.start()
        two.start()

    def hop_two(layer, piece):
        one, two, three, four = hops(layer, piece)
        one.wait_recv()
        three.start()
        two.wait_recv()
        four.start()

    def all_in(layer, piece):
        _, _, three, four = hops(layer, piece)
        three.wait_recv()
        four.wait_recv()

    hop_one(0, 0)

    rows8 = lens_in.shape[0]
    lens[pl.ds(pl.multiple_of((core * LINE + place) * rows8, rows8), rows8), :] = lens_in[...]
    line_gather(here, lens, len_sems, (), 1)
    cross_copy.wait()
    gain_copy.wait()
    first = core == 0
    ours0, others0 = ends[:SLOT].astype(F32), ends[SLOT:].astype(F32)
    crossed = cross[...].astype(F32)
    x = jnp.where(first, ours0, crossed)
    own_len = lens[pl.ds(pl.multiple_of((core * LINE + place) * 8, 8), 8), :][:1]
    live = lax.broadcasted_iota(jnp.int32, (SLOT, 128), 0).astype(F32) < own_len
    valid = jnp.where(live, 1.0, 0.0)[:, :1]
    cot_out[...] = (jnp.where(first, crossed, others0) * valid).astype(BF16)
    res[0] = x

    def own_block(ref):
        return ref.at[pl.ds(pl.multiple_of((core * LINE + place) * SLOT, SLOT), SLOT), :]

    def weight_out(layer, piece):
        dst = (wa_out, wg_out, wd_out)[piece].at[layer]
        return pltpu.make_async_copy(PIECES[piece][0].at[layer], dst, w_save.at[layer, piece])

    reduce_bufs = (sib_buf, rx_up, rx_dn, tx_up, tx_dn)
    half_rows = LINE * SLOT

    def layer(index):
        saves = []

        def keep(src, dst):
            copy = pltpu.make_async_copy(src, dst, save.at[index, len(saves)])
            copy.start()
            saves.append(copy)

        x = res[2 * index]
        own_block(seq)[...] = (x * root(x) * gain_out[index, 0:1]).astype(BF16)
        if index == 0:
            line_gather(here, seq, gather_sems, (None, None, lambda: (hop_two(0, 0), hop_one(0, 1))))
        else:
            line_gather(here, seq, gather_sems, (None, lambda: hop_one(1, 2)))
        keep(seq, xn_out.at[index])
        all_in(index, 0)
        weight_out(index, 0).start()

        def attend(pair, _):
            at = pl.ds(pl.multiple_of(pair * 2 * SLOT, 2 * SLOT), 2 * SLOT)
            wide = dot(seq[at, :], wa[index, :, :AO_AT])
            kv = turn(wide[:, KV_AT:AO_AT], tables[2], tables[3])
            q = jnp.concatenate(
                [turn(wide[:, 128 * i:128 * (i + 1)], tables[0], tables[1]) for i in range(GROUP // 2)], 1
            )
            kv_low = kv.astype(BF16)
            qkv[at, :Q_SLAB] = q.astype(BF16)
            qkv[at, KV_AT:AO_AT] = kv_low
            probs = two_slot_probs(spread_heads(q).astype(BF16), kv_low, lens, pair).astype(BF16)
            ctx[at, :] = join_heads(dot(probs, kv_low), True).astype(BF16)
            return 0

        lax.fori_loop(0, LINE, attend, 0)
        keep(qkv, qkv_out.at[index])
        keep(ctx, ctx_out.at[index])

        def reduce(src, weights, cols, meanwhile):
            def terms(whose, dst, sub):
                rows = pl.ds(pl.multiple_of(whose * half_rows, half_rows), half_rows)
                size = width // SUBS
                for lo in range(sub * size, (sub + 1) * size, 512):
                    at = slice(lo, lo + 512)
                    dst[:, at] = dot_last(src[rows, :], weights[index, at, cols]).astype(dst.dtype)

            line_reduce(here, total, ours, theirs, reduce_bufs, reduce_sems, terms, meanwhile)

        saves[0].wait()
        reduce(ctx, wa, slice(AO_AT, A_COLS), () if index == 0 else (None, None, lambda: hop_two(1, 1)))
        middle = x + total[...]
        res[1 + 2 * index] = middle
        own_block(hnb)[...] = (middle * root(middle) * gain_out[index, 1:2]).astype(BF16)
        if index == 0:
            line_gather(here, hnb, gather_sems, (None, lambda: hop_one(0, 2), None, lambda: hop_two(0, 1)))
            own_block(dm)[...] = cot_out[...]
            line_gather(here, dm, dm_sems)
            pltpu.make_async_copy(dm, dm_out, misc.at[0]).start()
        else:
            line_gather(here, hnb, gather_sems, (None, None, lambda: hop_two(1, 2)))
        keep(hnb, hn_out.at[index])
        all_in(index, 1)
        weight_out(index, 1).start()

        def gate_up(n, _):
            at = pl.ds(pl.multiple_of(n * 256, 256), 256)
            at_up = pl.ds(pl.multiple_of(FF_SLAB + n * 256, 256), 256)
            gate = dot(hnb[...], wg[index, :, at])
            up = dot(hnb[...], wg[index, :, at_up])
            gu[:, at] = gate
            gu[:, at_up] = up
            hid[:, at] = (gate * jax.nn.sigmoid(gate) * up).astype(BF16)
            return 0

        lax.fori_loop(0, FF_SLAB // 256, gate_up, 0)
        keep(gu, gu_out.at[index])
        keep(hid, hid_out.at[index])
        if index == 0:
            hop_one(1, 0)
            hop_two(0, 2)
            hop_one(1, 1)
        all_in(index, 2)
        weight_out(index, 2).start()
        saves[3].wait()
        if index == 0:
            reduce(hid, wd, slice(None), (None, lambda: hop_two(1, 0)))
            res[2] = (res[1] + total[...]).astype(BF16).astype(F32)
        for i in (1, 2, 4, 5):
            saves[i].wait()

    layer(0)
    layer(1)
    pltpu.make_async_copy(dm, dm_out, misc.at[0]).wait()
    for i in range(4):
        pltpu.make_async_copy(res.at[i], res_out.at[i], misc.at[i]).start()
    for i in range(4):
        pltpu.make_async_copy(res.at[i], res_out.at[i], misc.at[i]).wait()
    for i in range(6):
        twin_copy(i, core).wait_send()
    for index in range(2):
        for piece in range(3):
            weight_out(index, piece).wait()
            for move in hops(index, piece):
                move.wait_send()


def forward_call(ends, lens, gain, tables, w_in, w_out):
    width = ends.shape[1]
    rows = LINE * CORES * SLOT
    hbm = pl.BlockSpec(memory_space=pl.ANY)
    vmem = pl.BlockSpec(memory_space=pltpu.VMEM)
    shape = jax.ShapeDtypeStruct
    dma = pltpu.SemaphoreType.DMA
    line = dma((LINE, SUBS))
    block = pltpu.VMEM((LINE * SLOT, width), BF16)
    return pl.pallas_call(
        forward_body,
        out_shape=[
            shape((2, width, A_COLS), BF16),
            shape((2, width, 2 * FF_SLAB), BF16),
            shape((2, width, FF_SLAB), BF16),
            shape((2, rows, width), BF16),
            shape((2, rows, width), BF16),
            shape((2, rows, AO_AT), BF16),
            shape((2, rows, Q_SLAB), BF16),
            shape((2, rows, 2 * FF_SLAB), F32),
            shape((2, rows, FF_SLAB), BF16),
            shape((4, SLOT, width), F32),
            shape((rows, width), BF16),
            shape((SLOT, width), BF16),
            shape((2, 2, width), F32),
            shape((LINE * CORES * 8, 128), F32),
        ],
        in_specs=[vmem, vmem, vmem, vmem, hbm, hbm],
        out_specs=[hbm] * 11 + [vmem] * 3,
        scratch_shapes=[
            pltpu.VMEM((SLOT, width), BF16),
            pltpu.VMEM((w_in.shape[0], 128), BF16),
            pltpu.VMEM((w_in.shape[0], 128), BF16),
            pltpu.VMEM((w_in.shape[0], 128), BF16),
            pltpu.VMEM((w_in.shape[0], 128), BF16),
            pltpu.VMEM((2, width, A_COLS), BF16),
            pltpu.VMEM((2, width, 2 * FF_SLAB), BF16),
            pltpu.VMEM((2, width, FF_SLAB), BF16),
            pltpu.VMEM((rows, width), BF16),
            pltpu.VMEM((rows, width), BF16),
            pltpu.VMEM((rows, AO_AT), BF16),
            pltpu.VMEM((rows, Q_SLAB), BF16),
            pltpu.VMEM((rows, 2 * FF_SLAB), F32),
            pltpu.VMEM((rows, FF_SLAB), BF16),
            block,
            pltpu.VMEM((LINE * SLOT, width), F32),
            pltpu.VMEM((4, SLOT, width), F32),
            pltpu.VMEM((SLOT, width), F32),
            pltpu.VMEM((rows, width), BF16),
            block, block, block, block, block,
            dma((6,)), dma((6,)), dma((6,)), dma((2, 3, 4)), dma((2, 3, 4)),
            dma((4,)), dma((2,)), dma((2,)), dma((2, 6)), dma((2, 3)),
        ] + [line] * 21,
        compiler_params=pltpu.CompilerParams(
            collective_id=0, has_side_effects=True, vmem_limit_bytes=60 * 2**20
        ),
        name="forward_two_layers",
        cost_estimate=pl.CostEstimate(flops=16_000_000_000, bytes_accessed=600_000_000, transcendentals=0),
    )(ends, lens, gain, tables, w_in, w_out)


def spread_heads_high(wide):
    low = low_lanes((wide.shape[0], 128))
    parts = []
    for pair in range(GROUP // 2):
        block = wide[:, pair * 128:(pair + 1) * 128]
        parts.append(jnp.where(low, 0.0, pltpu.roll(block, 64, 1)))
        parts.append(jnp.where(low, 0.0, block))
    return jnp.concatenate(parts, 0)


CHUNKS = ((0, FF_SLAB), (FF_SLAB, FF_SLAB), (2 * FF_SLAB, FF_SLAB), (3 * FF_SLAB, A_COLS))
SLAB = 3 * FF_SLAB + A_COLS
FAR_SLOT = (1, 0, 0, 1)
WINDOW, EACH = 16, 16


def backward_body(
    replicas,
    cot_in, gain, lens, tables, res_in, dm_in, wa_in, wg_in, wd_in, xn_in, hn_in, qkv_in, ctx_in, gu_in, hid_in,
    fin, ends_out, gain_out, far_rx, near_rx,
    wa, wg, wd, xn, hn, qkv, ctx, gu, hid, dm, da, dgu, dqkv, theirs, ours, total, res, y_total,
    sib_buf, rx_up, rx_dn, tx_up, tx_dn, tx_far, tx_x, tx_y, tx_fin, stage, gain_loc, gain_x, gain_y, gain_line,
    end_tx, end_rx,
    load_sem, gu_sem, res_sem, far_send, far_recv, near_send, near_recv, fin_send, fin_recv, stage_sem, misc_send, misc_recv,
    *line_sems,
):
    gather_sems, gain_sems, reduce_sems, y_sems = line_sems[:5], line_sems[5:10], line_sems[10:16], line_sems[16:]
    here = Here()
    core, shard, place = here.core, here.shard, here.place
    width = cot_in.shape[1]
    part = width // SHARDS
    half = part // 2
    half_rows = LINE * SLOT
    base = here.depth - place

    barrier = pltpu.get_barrier_semaphore()
    for peer in (here.x_peer, here.y_peer):
        pl.semaphore_signal(barrier, inc=1, device_id=peer)
    for other in range(CORES):
        for where in range(LINE):
            @pl.when((core != other) | (place != where))
            def _():
                pl.semaphore_signal(barrier, inc=1, device_id={"section": other, "dp": base + where})

    pl.semaphore_wait(barrier, 2 + CORES * LINE - 1)

    NAMES = ("dm", "wd", "wg", "wa", "hid", "qkv", "ctx", "hn", "xn")
    VIEWS = {
        "wd": (wd_in, lambda l: wd), "wg": (wg_in, lambda l: wg), "wa": (wa_in, lambda l: wa),
        "hid": (hid_in, lambda l: hid), "qkv": (qkv_in, lambda l: qkv.at[l]), "ctx": (ctx_in, lambda l: ctx.at[l]),
        "hn": (hn_in, lambda l: hn), "xn": (xn_in, lambda l: xn),
    }

    def load(name, layer):
        if name == "dm":
            return pltpu.make_async_copy(dm_in, dm.at[1], load_sem.at[1, 0])
        src, dst = VIEWS[name]
        return pltpu.make_async_copy(src.at[layer], dst(layer), load_sem.at[layer, NAMES.index(name)])

    def gu_loads(layer, tile):
        return [
            pltpu.make_async_copy(
                gu_in.at[layer, :, pl.ds(i * FF_SLAB + tile * 256, 256)],
                gu.at[tile % 2, :, pl.ds(i * 256, 256)], gu_sem.at[tile % 2, i])
            for i in range(2)
        ]

    for name in ("dm", "hid", "wd"):
        load(name, 1).start()
    for tile in range(2):
        for copy in gu_loads(1, tile):
            copy.start()
    for name in ("hn", "wg", "wa", "qkv", "ctx"):
        load(name, 1).start()

    ready = set()

    def need(name, layer):
        if (name, layer) not in ready:
            ready.add((name, layer))
            load(name, layer).wait()

    gain_loc[...] = jnp.zeros_like(gain_loc)

    pending = {}

    waiting = []

    def pump(count):
        for _ in range(min(count, len(waiting))):
            waiting.pop(0).start()

    def claim(key):
        moves = pending.pop(key, ())
        for move in moves:
            if move in waiting:
                waiting.remove(move)
                move.start()
        for move in moves:
            move.wait_send()

    def products(layer, chunk, block, put):
        at = pl.ds(pl.multiple_of(block * part, part), part)
        need("hn" if chunk < 2 else "hid" if chunk == 2 else "xn", layer)

        def tiles(lhs, rhs, size, to):
            for lo in range(0, size, 512):
                hi = min(lo + 512, size)
                put(slice(to + lo, to + hi), dot_rows(lhs[:, at], rhs[:, lo:hi]))

        if chunk < 2:
            tiles(hn, dgu.at[layer, :, pl.ds(chunk * FF_SLAB, FF_SLAB)], FF_SLAB, 0)
        elif chunk == 2:
            tiles(dm.at[layer], hid, FF_SLAB, 0)
        else:
            tiles(xn, dqkv.at[layer], AO_AT, 0)
            tiles(da.at[layer], ctx.at[layer], Q_SLAB, AO_AT)

    def far_moves(layer, chunk):
        lo, size = CHUNKS[chunk]
        src = tx_far.at[FAR_SLOT[chunk]]
        cols = pl.ds(0, size)
        return [
            remote(src.at[pl.ds(i * half, half), cols], far_rx.at[layer, i, :, pl.ds(lo, size)],
                   far_send.at[layer, chunk, i], far_recv.at[layer, chunk, i], peer)
            for i, peer in ((0, here.x_peer), (1, here.y_peer))
        ]

    def near_moves(layer, chunk):
        lo, size = CHUNKS[chunk]
        cols = pl.ds(0, size)
        return [
            remote(src.at[chunk % 2, :, cols], near_rx.at[layer, i, :, pl.ds(lo, size)],
                   near_send.at[layer, chunk, i], near_recv.at[layer, chunk, i], peer)
            for i, (src, peer) in enumerate(((tx_x, here.x_peer), (tx_y, here.y_peer)))
        ]

    def stage_far(layer, chunk, i):
        lo, size = CHUNKS[chunk]
        return pltpu.make_async_copy(
            far_rx.at[layer, i, :, pl.ds(lo, size)], stage.at[i, pl.ds(0, half), pl.ds(0, size)], stage_sem.at[i])

    def stage_near(layer, chunk, i):
        lo, size = CHUNKS[chunk]
        return pltpu.make_async_copy(
            near_rx.at[layer, i, :, pl.ds(lo, size)], stage.at[i, :, pl.ds(0, size)], stage_sem.at[i])

    def step_one(layer, chunk):
        claim(("far", FAR_SLOT[chunk]))

        def put(cols, value):
            tx_far[FAR_SLOT[chunk], :, cols] = value.astype(BF16)

        products(layer, chunk, here.far_shard, put)
        moves = far_moves(layer, chunk)
        for move in moves:
            move.start()
        pending["far", FAR_SLOT[chunk]] = moves

    def step_two(layer, chunk):
        arrivals = far_moves(layer, chunk)
        for i in (1, 0):
            arrivals[i].wait_recv()
            stage_far(layer, chunk, i).start()
        claim(("near", chunk % 2))
        moves = near_moves(layer, chunk)

        def put_x(cols, value):
            tx_x[chunk % 2, :half, cols] = value[:half].astype(BF16)
            tx_x[chunk % 2, half:, cols] = (value[half:] + stage[1, :half, cols].astype(F32)).astype(BF16)

        def put_y(cols, value):
            tx_y[chunk % 2, :half, cols] = (value[:half] + stage[0, :half, cols].astype(F32)).astype(BF16)
            tx_y[chunk % 2, half:, cols] = value[half:].astype(BF16)

        stage_far(layer, chunk, 1).wait()
        products(layer, chunk, here.x_shard, put_x)
        moves[0].start()
        stage_far(layer, chunk, 0).wait()
        products(layer, chunk, here.y_shard, put_y)
        moves[1].start()
        pending["near", chunk % 2] = moves

    piece = part // (replicas * LINE)

    def fin_moves(layer, chunk):
        lo, size = CHUNKS[chunk]
        head = place * CORES + core
        moves = []
        for rep in range(replicas):
            for turn_by in (2, 3, 1, 0):
                where = lax.rem(place + turn_by, LINE)
                src = tx_fin.at[chunk % 2, pl.ds(pl.multiple_of((rep * LINE + where) * piece, piece), piece), pl.ds(0, size)]
                dst = fin.at[head, pl.ds(rep * piece, piece), pl.ds(lo, size)]
                same = (core == layer) & (place == where)
                move = remote(src, dst, fin_send.at[layer, chunk, rep, turn_by], fin_recv.at[rep, head, chunk],
                              {"section": layer, "dp": base + where})
                stay = pltpu.make_async_copy(src, dst, fin_send.at[layer, chunk, rep, turn_by])
                moves.append((same, move, stay))
        return moves

    class Leave:
        def __init__(self, entry):
            self.same, self.move, self.stay = entry

        def start(self):
            @pl.when(self.same)
            def _():
                self.stay.start()

            @pl.when(jnp.logical_not(self.same))
            def _():
                self.move.start()

        def wait_send(self):
            @pl.when(self.same)
            def _():
                self.stay.wait()

            @pl.when(jnp.logical_not(self.same))
            def _():
                self.move.wait_send()

    def step_three(layer, chunk):
        arrivals = near_moves(layer, chunk)
        for i in range(2):
            arrivals[i].wait_recv()
            stage_near(layer, chunk, i).start()
        claim(("fin", chunk % 2))
        stage_near(layer, chunk, 0).wait()
        stage_near(layer, chunk, 1).wait()

        def put(cols, value):
            tx_fin[chunk % 2, :, cols] = (
                value + stage[0, :, cols].astype(F32) + stage[1, :, cols].astype(F32)
            ).astype(BF16)

        products(layer, chunk, shard, put)
        moves = [Leave(entry) for entry in fin_moves(layer, chunk)]
        waiting.extend(moves)
        if layer == 0:
            pump(len(waiting))
        pending["fin", chunk % 2] = moves

    def steps(*todo):
        def run():
            pump(EACH)
            for kind, layer, chunk in todo:
                (step_one, step_two, step_three)[kind - 1](layer, chunk)
                if layer == 1 and kind == 3 and chunk == 0:
                    load("hn", 0).start()
                if layer == 1 and kind == 3 and chunk == 3:
                    load("xn", 0).start()
        return run

    reduce_bufs = (sib_buf, rx_up, rx_dn, tx_up, tx_dn)

    def own_block(ref, layer):
        return ref.at[layer, pl.ds(pl.multiple_of((core * LINE + place) * SLOT, SLOT), SLOT), :]

    def terms_of(src, weights, cols):
        def terms(whose, dst, sub):
            rows = pl.ds(pl.multiple_of(whose * half_rows, half_rows), half_rows)
            size = width // SUBS
            for lo in range(sub * size, (sub + 1) * size, 512):
                at = slice(lo, lo + 512)
                dst[:, at] = dot_last(src[rows, :], weights[at, cols]).astype(dst.dtype)
        return terms

    def reduce(slot, src, weights, cols, meanwhile):
        res_load(slot).start()
        line_reduce(here, total, ours, theirs, reduce_bufs, reduce_sems, terms_of(src, weights, cols), meanwhile)

    lower, upper = pl.ds(0, half_rows), pl.ds(half_rows, half_rows)
    y_bufs = (dm.at[0, lower], dm.at[0, upper], da.at[0, lower], da.at[0, upper], dgu.at[0, lower])
    y_theirs, y_ours = dgu.at[0, upper], xn.at[lower]
    y_steps = line_reduce_steps(here, y_total, y_ours, y_theirs, y_bufs, y_sems, terms_of(hid, wd, slice(None)))

    def y_step():
        next(y_steps, None)

    def res_load(slot):
        return pltpu.make_async_copy(res_in.at[slot], res, res_sem.at[slot])

    def norm_back(gain_row, slot):
        res_load(slot).wait()
        values = res[...]
        scale = root(values)
        grad = total[...]
        hat = grad * gain_row
        gain_loc[slot:slot + 1, :] = jnp.sum(grad * values * scale, 0, keepdims=True)
        inner = jnp.mean(hat * values, -1, keepdims=True)
        return scale * hat - values * (scale * scale * scale * inner)

    def layer_back(layer, grad_out, jobs):
        if layer == 1:
            need("dm", 1)
        else:
            own_block(dm, layer)[...] = grad_out.astype(BF16)
            line_gather(here, dm.at[layer], gather_sems, jobs[0])
        pump(WINDOW)
        step_one(layer, 2)
        need("wd", layer)
        tiles = FF_SLAB // 256
        for tile in range(tiles):
            at = slice(tile * 256, tile * 256 + 256)
            at_up = slice(FF_SLAB + tile * 256, FF_SLAB + tile * 256 + 256)
            grad = dot(dm[layer], wd[:, at])
            for copy in gu_loads(layer, tile):
                copy.wait()
            gate, up = gu[tile % 2, :, :256], gu[tile % 2, :, 256:]
            sig = jax.nn.sigmoid(gate)
            dgu[layer, :, at] = (grad * up * sig * (1.0 + gate * (1.0 - sig))).astype(BF16)
            dgu[layer, :, at_up] = (grad * gate * sig).astype(BF16)
            ahead = (layer, tile + 2) if tile + 2 < tiles else (layer - 1, tile + 2 - tiles)
            if ahead[0] >= 0:
                for copy in gu_loads(*ahead):
                    copy.start()
        step_one(layer, 0)
        need("wg", layer)
        reduce(2 * layer + 1, dgu.at[layer], wg, slice(None), jobs[1])
        if layer == 1:
            load("wg", 0).start()
            load("wd", 0).start()
        grad_mid = grad_out + norm_back(gain[layer, 1:2], 2 * layer + 1)
        own_block(da, layer)[...] = grad_mid.astype(BF16)
        line_gather(here, da.at[layer], gather_sems, jobs[2])
        pump(WINDOW)
        need("wa", layer)
        need("qkv", layer)
        need("ctx", layer)

        def attend(pair, _):
            at = pl.ds(pl.multiple_of(pair * 2 * SLOT, 2 * SLOT), 2 * SLOT)
            grad_ctx = dot(da[layer, at, :], wa[:, AO_AT:A_COLS]).astype(BF16).astype(F32)
            kv = qkv[layer, at, KV_AT:AO_AT]
            q = spread_heads(qkv[layer, at, :Q_SLAB].astype(F32)).astype(BF16)
            probs = two_slot_probs(q, kv, lens, pair)
            grad_high = spread_heads_high(grad_ctx).astype(BF16)
            grad_probs = dot_last(grad_high, kv)
            inner = jnp.sum(grad_probs * probs, -1, keepdims=True)
            grad_scores = (probs * (grad_probs - inner)).astype(BF16)
            grad_q = join_heads(dot(grad_scores, kv), False) * HEAD_DIM**-0.5
            grad_kv = dot_rows(grad_scores, q) * HEAD_DIM**-0.5 + dot_rows(probs.astype(BF16), grad_high)
            for i in range(GROUP // 2):
                cols = slice(128 * i, 128 * (i + 1))
                dqkv[layer, at, cols] = turn(grad_q[:, cols], tables[0], -tables[1]).astype(BF16)
            dqkv[layer, at, KV_AT:AO_AT] = turn(grad_kv, tables[2], -tables[3]).astype(BF16)
            return 0

        lax.fori_loop(0, LINE, attend, 0)
        reduce(2 * layer, dqkv.at[layer], wa, slice(0, AO_AT), jobs[3])
        if layer == 1:
            load("wa", 0).start()
            load("qkv", 0).start()
            load("ctx", 0).start()
        return grad_mid + norm_back(gain[layer, 0:1], 2 * layer)

    dx1 = layer_back(1, cot_in[...].astype(F32), (
        (),
        (lambda: (steps((1, 1, 1))(), y_step()), steps((2, 1, 2)), y_step),
        (y_step, steps((2, 1, 1)), lambda: (y_step(), load("xn", 1).start())),
        (steps((1, 1, 3), (2, 1, 0)), steps((3, 1, 2))),
    ))
    load("hid", 0).start()
    dx0 = layer_back(0, dx1.astype(BF16).astype(F32), (
        (steps((3, 1, 1)), None, steps((3, 1, 0), (2, 1, 3))),
        (steps((3, 1, 3), (1, 0, 1)), steps((2, 0, 2))),
        (None, steps((2, 0, 1))),
        (steps((1, 0, 3), (2, 0, 0)), steps((3, 0, 2))),
    ))

    res_load(3).start()

    gain_x_move = remote(gain_loc, gain_x, misc_send.at[1], misc_recv.at[1], here.x_peer)
    gain_x_move.start()
    steps((3, 0, 1))()
    gain_x_move.wait()
    gain_loc[...] += gain_x[...]
    gain_y_move = remote(gain_loc, gain_y, misc_send.at[2], misc_recv.at[2], here.y_peer)
    gain_y_move.start()
    steps((2, 0, 3))()
    gain_y_move.wait()
    cols = pl.ds(pl.multiple_of(shard * part, part), part)
    own_gains = pl.ds(pl.multiple_of((core * LINE + place) * 8, 8), 8)
    gain_line[own_gains, :] = gain_loc[:, cols] + gain_y[:, cols]
    line_gather(here, gain_line, gain_sems, (), 1)
    gain_sum = gain_line[0:8, :]
    for i in range(1, LINE * CORES):
        gain_sum += gain_line[8 * i:8 * i + 8, :]
    gain_out[...] = gain_sum

    res_load(3).wait()

    first = core == 0
    dx0 = dx0.astype(BF16).astype(F32)
    y1 = (res[...] + y_total[...]).astype(BF16).astype(F32)
    end_tx[...] = jnp.where(first, y1, dx0).astype(BF16)
    end_move = remote(end_tx, end_rx, misc_send.at[0], misc_recv.at[0], here.twin)
    end_move.start()
    steps((3, 0, 0))()
    end_move.wait()
    crossed = end_rx[...].astype(F32)
    ends_out[:SLOT] = jnp.where(first, dx0, crossed).astype(BF16)
    ends_out[SLOT:] = jnp.where(first, crossed, y1).astype(BF16)
    steps((3, 0, 3))()
    for key in list(pending):
        claim(key)
    for rep in range(replicas):
        for where in range(LINE):
            for other in range(CORES):
                head = where * CORES + other

                @pl.when((core != other) | (place != where))
                def _():
                    for chunk, (lo, size) in enumerate(CHUNKS):
                        src = tx_fin.at[0, pl.ds(0, piece), pl.ds(0, size)]
                        dst = fin.at[head, pl.ds(rep * piece, piece), pl.ds(lo, size)]
                        remote(src, dst, fin_send.at[0, 0, 0, 0], fin_recv.at[rep, head, chunk],
                               {"section": 1 - core, "dp": base + where}).wait_recv()


def backward_call(replicas, cot, gain, lens, tables, res, dm, wa, wg, wd, xn, hn, qkv, ctx, gu, hid):
    width = cot.shape[1]
    rows = LINE * CORES * SLOT
    part = width // SHARDS
    hbm = pl.BlockSpec(memory_space=pl.ANY)
    vmem = pl.BlockSpec(memory_space=pltpu.VMEM)
    shape = jax.ShapeDtypeStruct
    dma = pltpu.SemaphoreType.DMA
    line = dma((LINE, SUBS))
    vm = pltpu.VMEM
    block = vm((LINE * SLOT, width), BF16)
    move = vm((2, part, FF_SLAB), BF16)
    return pl.pallas_call(
        functools.partial(backward_body, replicas),
        out_shape=[
            shape((KV_HEADS, part // LINE, SLAB), BF16),
            shape((CORES * SLOT, width), BF16),
            shape((8, part), F32),
            shape((2, 2, part // 2, SLAB), BF16),
            shape((2, 2, part, SLAB), BF16),
        ],
        in_specs=[vmem] * 4 + [hbm] * 11,
        out_specs=[hbm, vmem, vmem, hbm, hbm],
        scratch_shapes=[
            vm((width, A_COLS), BF16), vm((width, 2 * FF_SLAB), BF16), vm((width, FF_SLAB), BF16),
            vm((rows, width), BF16), vm((rows, width), BF16), vm((2, rows, AO_AT), BF16), vm((2, rows, Q_SLAB), BF16),
            vm((2, rows, 512), F32), vm((rows, FF_SLAB), BF16),
            vm((2, rows, width), BF16), vm((2, rows, width), BF16),
            vm((2, rows, 2 * FF_SLAB), BF16), vm((2, rows, AO_AT), BF16),
            block, vm((LINE * SLOT, width), F32), vm((SLOT, width), F32), vm((SLOT, width), F32), vm((SLOT, width), F32),
            block, block, block, block, block,
            move, move, move, move, move,
            vm((8, width), F32), vm((8, width), F32), vm((8, width), F32), vm((8 * LINE * CORES, part), F32),
            vm((SLOT, width), BF16), vm((SLOT, width), BF16),
            dma((2, 9)), dma((2, 2)), dma((4,)), dma((2, 4, 2)), dma((2, 4, 2)), dma((2, 4, 2)), dma((2, 4, 2)),
            dma((2, 4, replicas, LINE)), dma((replicas, KV_HEADS, 4)), dma((2,)), dma((3,)), dma((3,)),
        ] + [line] * 22,
        compiler_params=pltpu.CompilerParams(
            collective_id=1, has_side_effects=True, vmem_limit_bytes=62 * 2**20
        ),
        name="backward_two_layers",
        cost_estimate=pl.CostEstimate(flops=32_000_000_000, bytes_accessed=600_000_000, transcendentals=0),
    )(cot, gain, lens, tables, res, dm, wa, wg, wd, xn, hn, qkv, ctx, gu, hid)


def place_body(fin, in_out, out_out, held, wide_in, wide_out, load_sem, save_sem):
    steps = KV_HEADS // 2
    q_two, ff_two = 2 * Q_SLAB, 2 * FF_SLAB
    ff0 = Q_COLS + 2 * KV_COLS

    def fetch(step):
        return pltpu.make_async_copy(fin.at[pl.ds(2 * step, 2)], held.at[step % 2], load_sem.at[step % 2])

    def saves(step):
        slot = step % 2
        moves = []
        for i, (src, lo, dst, to, size) in enumerate((
            (wide_in, 0, in_out, step * q_two, q_two),
            (wide_in, q_two, in_out, Q_COLS + step * 128, 128),
            (wide_in, q_two + 128, in_out, Q_COLS + KV_COLS + step * 128, 128),
            (wide_in, q_two + 256, in_out, ff0 + step * ff_two, ff_two),
            (wide_in, q_two + 256 + ff_two, in_out, ff0 + FF + step * ff_two, ff_two),
            (wide_out, 0, out_out, step * q_two, q_two),
            (wide_out, q_two, out_out, Q_COLS + step * ff_two, ff_two),
        )):
            moves.append(pltpu.make_async_copy(
                src.at[slot, :, pl.ds(lo, size)], dst.at[:, pl.ds(to, size)], save_sem.at[slot, i]))
        return moves

    fetch(0).start()
    a_at = 3 * FF_SLAB
    for step in range(steps):
        slot = step % 2
        if step + 1 < steps:
            fetch(step + 1).start()
        fetch(step).wait()
        if step >= 2:
            for move in saves(step - 2):
                move.wait()
        for i in range(2):
            q_to = i * Q_SLAB
            wide_in[slot, :, q_to:q_to + Q_SLAB] = held[slot, i, :, a_at:a_at + Q_SLAB].astype(F32)
            wide_out[slot, :, q_to:q_to + Q_SLAB] = held[slot, i, :, a_at + AO_AT:a_at + A_COLS].astype(F32)
            for k, (src_ref, to) in enumerate(((wide_in, q_two + 256), (wide_in, q_two + 256 + ff_two), (wide_out, q_two))):
                at = to + i * FF_SLAB
                src_ref[slot, :, at:at + FF_SLAB] = held[slot, i, :, k * FF_SLAB:(k + 1) * FF_SLAB].astype(F32)
        one = held[slot, 0, :, a_at + KV_AT:a_at + AO_AT].astype(F32)
        two = held[slot, 1, :, a_at + KV_AT:a_at + AO_AT].astype(F32)
        low = low_lanes(one.shape)
        wide_in[slot, :, q_two:q_two + 128] = jnp.where(low, one, pltpu.roll(two, 64, 1))
        wide_in[slot, :, q_two + 128:q_two + 256] = jnp.where(low, pltpu.roll(one, 64, 1), two)
        for move in saves(step):
            move.start()
    for step in range(max(steps - 2, 0), steps):
        for move in saves(step):
            move.wait()


def place_call(fin, in_cols, out_cols):
    rows = fin.shape[1]
    hbm = pl.BlockSpec(memory_space=pl.ANY)
    q_two, ff_two = 2 * Q_SLAB, 2 * FF_SLAB
    return pl.pallas_call(
        place_body,
        out_shape=[jax.ShapeDtypeStruct((rows, in_cols), F32), jax.ShapeDtypeStruct((rows, out_cols), F32)],
        in_specs=[hbm],
        out_specs=[hbm, hbm],
        scratch_shapes=[
            pltpu.VMEM((2, 2, rows, SLAB), BF16),
            pltpu.VMEM((2, rows, q_two + 256 + 2 * ff_two), F32),
            pltpu.VMEM((2, rows, q_two + ff_two), F32),
            pltpu.SemaphoreType.DMA((2,)),
            pltpu.SemaphoreType.DMA((2, 7)),
        ],
        compiler_params=pltpu.CompilerParams(vmem_limit_bytes=60 * 2**20),
        name="place_columns",
    )(fin)


def rope_blocks():
    half_dim = HEAD_DIM // 2
    inverse = 500000.0 ** (-(jnp.arange(half_dim, dtype=F32) * 2.0 / HEAD_DIM))
    angles = jnp.arange(SLOT, dtype=F32)[:, None] * inverse[None, :]
    cos, sin = jnp.cos(angles), jnp.sin(angles)
    one, zero = jnp.ones((SLOT, HEAD_DIM), F32), jnp.zeros((SLOT, HEAD_DIM), F32)
    rows = [
        jnp.concatenate([cos] * 4, 1),
        jnp.concatenate([-sin, sin] * 2, 1),
        jnp.concatenate([cos, cos, one], 1),
        jnp.concatenate([-sin, sin, zero], 1),
    ]
    return jnp.stack([jnp.tile(block, (2, 1)) for block in rows])


def local(ends_in, in_weight, out_weight, norm_gain, seq_len):
    core = lax.axis_index("section")
    replicas = lax.axis_size("dp") // LINE
    own_length = jnp.where(core == 0, seq_len[0], seq_len[1])
    lens_block = jnp.full((8, 128), own_length.astype(F32))
    rope = rope_blocks()
    (wa, wg, wd, xn, hn, qkv, ctx, gu, hid, res, dm, cot, gains, lens) = forward_call(
        ends_in[0], lens_block, norm_gain[0], rope, in_weight[0], out_weight[0]
    )
    fin, ends_out, gain_sum, _, _ = backward_call(
        replicas, cot, gains, lens, rope, res, dm, wa, wg, wd, xn, hn, qkv, ctx, gu, hid
    )
    own_gain = lax.dynamic_slice_in_dim(gain_sum, 2 * core, 2, 0)
    if replicas > 1:
        groups = [[r * LINE + p for r in range(replicas)] for p in range(LINE)]
        fin = lax.psum_scatter(fin, "dp", scatter_dimension=1, tiled=True, axis_index_groups=groups)
        own_gain = lax.psum(own_gain, "dp", axis_index_groups=groups)
    in_grad, out_grad = place_call(fin, in_weight.shape[2], out_weight.shape[2])
    size = own_gain.shape[1] // lax.axis_size("dp")
    own_gain = lax.dynamic_slice_in_dim(own_gain, lax.axis_index("dp") * size, size, 1)
    return ends_out[None], in_grad[None], out_grad[None], own_gain[None]


def solution(mesh):
    in_specs = (
        P("section", ("shard", "dp"), None),
        P("section", "shard", None),
        P("section", "shard", None),
        P("section", None, None),
        P(("shard", "dp")),
    )
    out_specs = (
        P("section", ("shard", "dp"), None),
        P("section", ("shard", "dp"), None),
        P("section", ("shard", "dp"), None),
        P("section", None, ("shard", "dp")),
    )
    return jax.shard_map(local, mesh=mesh, in_specs=in_specs, out_specs=out_specs, check_vma=False)
```

```python
import functools

import jax
import jax.numpy as jnp
from jax import lax
from jax.experimental import pallas as pl
from jax.experimental.pallas import tpu as pltpu
from jax.sharding import PartitionSpec as P

HEADS = 32
KV_HEADS = 8
GROUP = HEADS // KV_HEADS
HEAD_DIM = 64
FF = 8192
EPSILON = 1e-05
BF16 = jnp.bfloat16
F32 = jnp.float32
CORES = 2
LINE = KV_HEADS // CORES
SHARDS = 4
SLOT = 64
SUBS = 2
Q_SLAB = GROUP * HEAD_DIM
QKV_SLAB = Q_SLAB + 2 * HEAD_DIM
FF_SLAB = FF // KV_HEADS
Q_COLS = HEADS * HEAD_DIM
KV_COLS = KV_HEADS * HEAD_DIM


class Here:
    def __init__(self):
        self.core = lax.axis_index("section")
        self.shard = lax.axis_index("shard")
        self.depth = lax.axis_index("dp")
        self.place = lax.rem(self.depth, LINE)
        self.twin = {"section": 1 - self.core}
        self.x_shard = self.shard + 1 - 2 * lax.rem(self.shard, 2)
        self.y_shard = lax.rem(self.shard + 2, SHARDS)
        self.far_shard = SHARDS - 1 - self.shard
        self.x_peer = {"shard": self.x_shard}
        self.y_peer = {"shard": self.y_shard}
        self.above = {"dp": self.depth + 1}
        self.below = {"dp": self.depth - 1}
        self.has_above = self.place < LINE - 1
        self.has_below = self.place > 0

    def greet(self):
        barrier = pltpu.get_barrier_semaphore()
        for peer in (self.twin, self.x_peer, self.y_peer):
            pl.semaphore_signal(barrier, inc=1, device_id=peer)

        @pl.when(self.has_above)
        def _():
            pl.semaphore_signal(barrier, inc=1, device_id=self.above)

        @pl.when(self.has_below)
        def _():
            pl.semaphore_signal(barrier, inc=1, device_id=self.below)

        pl.semaphore_wait(barrier, jnp.where(self.has_above & self.has_below, 5, 4))


def remote(src, dst, send, recv, device):
    return pltpu.make_async_remote_copy(src, dst, send, recv, device_id=device)


def rows_at(ref, start, size):
    return ref.at[pl.ds(pl.multiple_of(start, size), size)]


def line_gather(here, buf, sems, meanwhile=(), subs=SUBS):
    up_send, dn_send, sib_send, z_recv, sib_recv = sems
    rows = buf.shape[0] // (LINE * CORES)
    size = rows // subs
    core, place = here.core, here.place
    meanwhile = list(meanwhile) + [None] * (LINE + 1)

    def part(where, whose, sub):
        return rows_at(buf, (whose * LINE + where) * rows + sub * size, size)

    def up(where, sub):
        mine = part(where, core, sub)
        return remote(mine, mine, up_send.at[where, sub], z_recv.at[where, sub], here.above)

    def down(where, sub):
        mine = part(where, core, sub)
        return remote(mine, mine, dn_send.at[where, sub], z_recv.at[where, sub], here.below)

    def across(where, whose, sub):
        mine = part(where, whose, sub)
        return remote(mine, mine, sib_send.at[where, sub], sib_recv.at[where, sub], here.twin)

    for sub in range(subs):
        @pl.when(here.has_above)
        def _():
            up(place, sub).start()

        @pl.when(here.has_below)
        def _():
            down(place, sub).start()

    for sub in range(subs):
        across(place, core, sub).start()
    for step in range(1, LINE):
        if meanwhile[step - 1] is not None:
            meanwhile[step - 1]()
        for sub in range(subs):
            @pl.when(place >= step)
            def _():
                up(place - step, sub).wait_recv()

                @pl.when(here.has_above)
                def _():
                    up(place - step, sub).start()

                across(place - step, core, sub).start()

            @pl.when(place + step < LINE)
            def _():
                down(place + step, sub).wait_recv()

                @pl.when(here.has_below)
                def _():
                    down(place + step, sub).start()

                across(place + step, core, sub).start()

    if meanwhile[LINE - 1] is not None:
        meanwhile[LINE - 1]()
    for where in range(LINE):
        for sub in range(subs):
            across(where, 1 - core, sub).wait_recv()

    for where in range(LINE):
        for sub in range(subs):
            across(where, core, sub).wait_send()

            @pl.when((where <= place) & here.has_above)
            def _():
                up(where, sub).wait_send()

            @pl.when((where >= place) & here.has_below)
            def _():
                down(where, sub).wait_send()


def line_reduce_steps(here, out, ours, theirs, bufs, sems, terms):
    sib_buf, rx_up, rx_dn, tx_up, tx_dn = bufs
    sib_send, sib_recv, up_send, up_recv, dn_send, dn_recv = sems
    rows, width = out.shape
    size = width // SUBS
    place, core = here.place, here.core

    def cols(sub):
        return slice(sub * size, (sub + 1) * size)

    def part(ref, where, sub):
        return ref.at[pl.ds(pl.multiple_of(where * rows, rows), rows), pl.ds(sub * size, size)]

    def read(ref, where, sub):
        return ref[pl.ds(pl.multiple_of(where * rows, rows), rows), cols(sub)].astype(F32)

    def across(where, sub):
        return remote(part(theirs, where, sub), part(sib_buf, where, sub),
                      sib_send.at[where, sub], sib_recv.at[where, sub], here.twin)

    def up(where, sub):
        return remote(part(tx_up, where, sub), part(rx_up, where, sub),
                      up_send.at[where, sub], up_recv.at[where, sub], here.above)

    def down(where, sub):
        return remote(part(tx_dn, where, sub), part(rx_dn, where, sub),
                      dn_send.at[where, sub], dn_recv.at[where, sub], here.below)

    def summed(where, sub):
        return read(ours, where, sub) + read(sib_buf, where, sub)

    def put(ref, where, sub, value):
        ref[pl.ds(pl.multiple_of(where * rows, rows), rows), cols(sub)] = value.astype(BF16)

    def begin(sub):
        terms(1 - core, theirs, sub)
        for step in range(LINE - 1, 0, -1):
            @pl.when(place + step < LINE)
            def _():
                across(place + step, sub).start()

            @pl.when(place >= step)
            def _():
                across(place - step, sub).start()

        across(place, sub).start()
        terms(core, ours, sub)

    def turn_on(step, sub):
        @pl.when(place + step < LINE)
        def _():
            where = place + step
            across(where, sub).wait_recv()

            @pl.when(here.has_below)
            def _():
                up(where, sub).wait_recv()
                put(tx_up, where, sub, summed(where, sub) + read(rx_up, where, sub))

            @pl.when(place == 0)
            def _():
                put(tx_up, where, sub, summed(where, sub))

            up(where, sub).start()

        @pl.when(place >= step)
        def _():
            where = place - step
            across(where, sub).wait_recv()

            @pl.when(here.has_above)
            def _():
                down(where, sub).wait_recv()
                put(tx_dn, where, sub, summed(where, sub) + read(rx_dn, where, sub))

            @pl.when(place == LINE - 1)
            def _():
                put(tx_dn, where, sub, summed(where, sub))

            down(where, sub).start()

    for sub in range(SUBS):
        begin(sub)
        turn_on(LINE - 1, sub)
    for step in range(LINE - 2, -1, -1):
        yield
        if step > 0:
            for sub in range(SUBS):
                turn_on(step, sub)

    for sub in range(SUBS):
        across(place, sub).wait_recv()
        out[:, cols(sub)] = summed(place, sub)

        @pl.when(here.has_below)
        def _():
            up(place, sub).wait_recv()
            out[:, cols(sub)] += read(rx_up, place, sub)

        @pl.when(here.has_above)
        def _():
            down(place, sub).wait_recv()
            out[:, cols(sub)] += read(rx_dn, place, sub)

    for where in range(LINE):
        for sub in range(SUBS):
            across(where, sub).wait_send()

            @pl.when(where > place)
            def _():
                up(where, sub).wait_send()

            @pl.when(where < place)
            def _():
                down(where, sub).wait_send()


def line_reduce(here, out, ours, theirs, bufs, sems, terms, meanwhile=()):
    jobs = list(meanwhile)
    for _ in line_reduce_steps(here, out, ours, theirs, bufs, sems, terms):
        if jobs:
            job = jobs.pop(0)
            if job is not None:
                job()


def dot(a, b):
    return jnp.dot(a, b, preferred_element_type=F32)


def dot_last(a, b):
    return lax.dot_general(a, b, (((1,), (1,)), ((), ())), preferred_element_type=F32)


def dot_rows(a, b):
    return lax.dot_general(a, b, (((0,), (0,)), ((), ())), preferred_element_type=F32)


def low_lanes(shape, size=HEAD_DIM):
    return lax.rem(lax.broadcasted_iota(jnp.int32, shape, 1), 2 * size) < size


def turn(block, cosine, sine):
    half = HEAD_DIM // 2
    other = jnp.where(low_lanes(block.shape, half), pltpu.roll(block, 128 - half, 1), pltpu.roll(block, half, 1))
    return block * cosine + other * sine


def spread_heads(wide):
    low = low_lanes((wide.shape[0], 128))
    parts = []
    for pair in range(GROUP // 2):
        block = wide[:, pair * 128:(pair + 1) * 128]
        parts.append(jnp.where(low, block, 0.0))
        parts.append(jnp.where(low, pltpu.roll(block, 64, 1), 0.0))
    return jnp.concatenate(parts, 0)


def join_heads(tall, from_high):
    rows = tall.shape[0] // GROUP
    low = low_lanes((rows, 128))
    parts = []
    for pair in range(GROUP // 2):
        one = tall[2 * pair * rows:(2 * pair + 1) * rows]
        two = tall[(2 * pair + 1) * rows:(2 * pair + 2) * rows]
        if from_high:
            parts.append(jnp.where(low, pltpu.roll(one, 64, 1), two))
        else:
            parts.append(jnp.where(low, one, pltpu.roll(two, 64, 1)))
    return jnp.concatenate(parts, 1)


def two_slot_probs(spread, kv, lens, pair):
    rows = 2 * SLOT
    q_at = lax.broadcasted_iota(jnp.int32, (rows, rows), 0)
    k_at = lax.broadcasted_iota(jnp.int32, (rows, rows), 1)
    first = lens[pl.ds(pl.multiple_of(16 * pair, 8), 8), :][:1]
    second = lens[pl.ds(pl.multiple_of(16 * pair + 8, 8), 8), :][:1]
    k_len = jnp.where(lax.broadcasted_iota(jnp.int32, (1, rows), 1) < SLOT, first, second)
    k_pos = jnp.where(k_at < SLOT, k_at, k_at - SLOT).astype(F32)
    allowed = (q_at >= k_at) & ((q_at < SLOT) | (k_at >= SLOT)) & (k_pos < k_len)
    allowed = jnp.concatenate([jnp.where(allowed, 1.0, 0.0)] * GROUP, 0)
    scores = dot_last(spread, kv) * HEAD_DIM**-0.5
    scores = jnp.where(allowed > 0.5, scores, -1e30)
    terms = jnp.exp(scores - jnp.max(scores, -1, keepdims=True))
    return terms / jnp.sum(terms, -1, keepdims=True)


def root(values):
    return lax.rsqrt(jnp.mean(values * values, -1, keepdims=True) + EPSILON)


Q_AT, KV_AT, AO_AT = 0, Q_SLAB, Q_SLAB + 2 * HEAD_DIM
A_COLS = AO_AT + Q_SLAB


def forward_body(
    ends, lens_in, gain_in, tables, w_in, w_out,
    wa_out, wg_out, wd_out, xn_out, hn_out, qkv_out, ctx_out, gu_out, hid_out, res_out, dm_out, cot_out, gain_out, lens,
    cross, k_pair, v_pair, kv_mine, kv_twin, wa, wg, wd, seq, hnb, qkv, ctx, gu, hid, theirs, ours, res, total, dm,
    sib_buf, rx_up, rx_dn, tx_up, tx_dn,
    loc_sem, push_send, push_recv, hop_send, hop_recv, misc, misc_send, misc_recv, save, w_save,
    *line_sems,
):
    gather_sems, len_sems, dm_sems, reduce_sems = line_sems[:5], line_sems[5:10], line_sems[10:15], line_sems[15:]
    here = Here()
    core, shard, place = here.core, here.shard, here.place
    width = ends.shape[1]
    part = w_in.shape[0]
    here.greet()

    own_rows = pl.ds(pl.multiple_of(shard * part, part), part)

    def cut(ref, base, size, head):
        return ref.at[:, pl.ds(pl.multiple_of(base + head * size, size), size)]

    ff0 = Q_COLS + 2 * KV_COLS
    slabs = [
        (lambda h: cut(w_in, 0, Q_SLAB, h), lambda l: wa.at[l, own_rows, pl.ds(Q_AT, Q_SLAB)]),
        (lambda h: cut(w_out, 0, Q_SLAB, h), lambda l: wa.at[l, own_rows, pl.ds(AO_AT, Q_SLAB)]),
        (None, lambda l: wa.at[l, own_rows, pl.ds(KV_AT, 2 * HEAD_DIM)]),
        (lambda h: cut(w_in, ff0, FF_SLAB, h), lambda l: wg.at[l, own_rows, pl.ds(0, FF_SLAB)]),
        (lambda h: cut(w_in, ff0 + FF, FF_SLAB, h), lambda l: wg.at[l, own_rows, pl.ds(FF_SLAB, FF_SLAB)]),
        (lambda h: cut(w_out, Q_COLS, FF_SLAB, h), lambda l: wd.at[l, own_rows]),
    ]
    my_head, twin_head = place * CORES + core, place * CORES + 1 - core

    def own_copy(i, layer):
        src, dst = slabs[i]
        return pltpu.make_async_copy(kv_mine if src is None else src(my_head), dst(layer), loc_sem.at[i])

    def twin_copy(i, layer):
        src, dst = slabs[i]
        return remote(kv_twin if src is None else src(twin_head), dst(layer), push_send.at[i], push_recv.at[i], here.twin)

    k_copy = pltpu.make_async_copy(cut(w_in, Q_COLS, 128, place), k_pair, misc.at[0])
    v_copy = pltpu.make_async_copy(cut(w_in, Q_COLS + KV_COLS, 128, place), v_pair, misc.at[1])
    k_copy.start()
    v_copy.start()
    for i in (0, 1):
        twin_copy(i, core).start()
        own_copy(i, core).start()
    other_rows = pl.ds(pl.multiple_of((1 - core) * SLOT, SLOT), SLOT)
    cross_copy = remote(ends.at[other_rows], cross, misc_send.at[0], misc_recv.at[0], here.twin)
    cross_copy.start()
    gain_copy = remote(gain_in, gain_out.at[core], misc_send.at[1], misc_recv.at[1], here.twin)
    gain_copy.start()
    gain_out[core] = gain_in[...]
    k_copy.wait()
    v_copy.wait()
    low = low_lanes(k_pair.shape)
    k, v = k_pair[...].astype(F32), v_pair[...].astype(F32)
    kv0 = jnp.where(low, k, pltpu.roll(v, 64, 1)).astype(BF16)
    kv1 = jnp.where(low, pltpu.roll(k, 64, 1), v).astype(BF16)
    kv_mine[...] = jnp.where(core == 0, kv0, kv1)
    kv_twin[...] = jnp.where(core == 0, kv1, kv0)
    for i in (2, 3, 4, 5):
        twin_copy(i, core).start()
        own_copy(i, core).start()

    PIECES = ((wa, (0, 1, 2)), (wg, (3, 4)), (wd, (5,)))
    half = part // 2

    def own_ready(layer, piece):
        @pl.when(core == layer)
        def _():
            for i in PIECES[piece][1]:
                own_copy(i, layer).wait()

        @pl.when(core != layer)
        def _():
            for i in PIECES[piece][1]:
                twin_copy(i, layer).wait_recv()

    def hop(layer, piece, which, rows, size, peer):
        ref = PIECES[piece][0].at[layer, pl.ds(pl.multiple_of(rows, size), size)]
        return remote(ref, ref, hop_send.at[layer, piece, which], hop_recv.at[layer, piece, which], peer)

    def hops(layer, piece):
        return (
            hop(layer, piece, 0, shard * part, part, here.x_peer),
            hop(layer, piece, 1, shard * part, part, here.y_peer),
            hop(layer, piece, 2, here.x_shard * part, half, here.y_peer),
            hop(layer, piece, 3, here.y_shard * part + half, half, here.x_peer),
        )

    def hop_one(layer, piece):
        own_ready(layer, piece)
        one, two, _, _ = hops(layer, piece)
        one.start()
        two.start()

    def hop_two(layer, piece):
        one, two, three, four = hops(layer, piece)
        one.wait_recv()
        three.start()
        two.wait_recv()
        four.start()

    def all_in(layer, piece):
        _, _, three, four = hops(layer, piece)
        three.wait_recv()
        four.wait_recv()

    hop_one(0, 0)

    rows8 = lens_in.shape[0]
    lens[pl.ds(pl.multiple_of((core * LINE + place) * rows8, rows8), rows8), :] = lens_in[...]
    line_gather(here, lens, len_sems, (), 1)
    cross_copy.wait()
    gain_copy.wait()
    first = core == 0
    ours0, others0 = ends[:SLOT].astype(F32), ends[SLOT:].astype(F32)
    crossed = cross[...].astype(F32)
    x = jnp.where(first, ours0, crossed)
    own_len = lens[pl.ds(pl.multiple_of((core * LINE + place) * 8, 8), 8), :][:1]
    live = lax.broadcasted_iota(jnp.int32, (SLOT, 128), 0).astype(F32) < own_len
    valid = jnp.where(live, 1.0, 0.0)[:, :1]
    cot_out[...] = (jnp.where(first, crossed, others0) * valid).astype(BF16)
    res[0] = x

    def own_block(ref):
        return ref.at[pl.ds(pl.multiple_of((core * LINE + place) * SLOT, SLOT), SLOT), :]

    def weight_out(layer, piece):
        dst = (wa_out, wg_out, wd_out)[piece].at[layer]
        return pltpu.make_async_copy(PIECES[piece][0].at[layer], dst, w_save.at[layer, piece])

    reduce_bufs = (sib_buf, rx_up, rx_dn, tx_up, tx_dn)
    half_rows = LINE * SLOT

    def layer(index):
        saves = []

        def keep(src, dst):
            copy = pltpu.make_async_copy(src, dst, save.at[index, len(saves)])
            copy.start()
            saves.append(copy)

        x = res[2 * index]
        own_block(seq)[...] = (x * root(x) * gain_out[index, 0:1]).astype(BF16)
        if index == 0:
            line_gather(here, seq, gather_sems, (None, None, lambda: (hop_two(0, 0), hop_one(0, 1))))
        else:
            line_gather(here, seq, gather_sems, (None, lambda: hop_one(1, 2)))
        keep(seq, xn_out.at[index])
        all_in(index, 0)
        weight_out(index, 0).start()

        def attend(pair, _):
            at = pl.ds(pl.multiple_of(pair * 2 * SLOT, 2 * SLOT), 2 * SLOT)
            wide = dot(seq[at, :], wa[index, :, :AO_AT])
            kv = turn(wide[:, KV_AT:AO_AT], tables[2], tables[3])
            q = jnp.concatenate(
                [turn(wide[:, 128 * i:128 * (i + 1)], tables[0], tables[1]) for i in range(GROUP // 2)], 1
            )
            kv_low = kv.astype(BF16)
            qkv[at, :Q_SLAB] = q.astype(BF16)
            qkv[at, KV_AT:AO_AT] = kv_low
            probs = two_slot_probs(spread_heads(q).astype(BF16), kv_low, lens, pair).astype(BF16)
            ctx[at, :] = join_heads(dot(probs, kv_low), True).astype(BF16)
            return 0

        lax.fori_loop(0, LINE, attend, 0)
        keep(qkv, qkv_out.at[index])
        keep(ctx, ctx_out.at[index])

        def reduce(src, weights, cols, meanwhile):
            def terms(whose, dst, sub):
                rows = pl.ds(pl.multiple_of(whose * half_rows, half_rows), half_rows)
                size = width // SUBS
                for lo in range(sub * size, (sub + 1) * size, 512):
                    at = slice(lo, lo + 512)
                    dst[:, at] = dot_last(src[rows, :], weights[index, at, cols]).astype(dst.dtype)

            line_reduce(here, total, ours, theirs, reduce_bufs, reduce_sems, terms, meanwhile)

        saves[0].wait()
        reduce(ctx, wa, slice(AO_AT, A_COLS), () if index == 0 else (None, None, lambda: hop_two(1, 1)))
        middle = x + total[...]
        res[1 + 2 * index] = middle
        own_block(hnb)[...] = (middle * root(middle) * gain_out[index, 1:2]).astype(BF16)
        if index == 0:
            line_gather(here, hnb, gather_sems, (None, lambda: hop_one(0, 2), None, lambda: hop_two(0, 1)))
            own_block(dm)[...] = cot_out[...]
            line_gather(here, dm, dm_sems)
            pltpu.make_async_copy(dm, dm_out, misc.at[0]).start()
        else:
            line_gather(here, hnb, gather_sems, (None, None, lambda: hop_two(1, 2)))
        keep(hnb, hn_out.at[index])
        all_in(index, 1)
        weight_out(index, 1).start()

        def gate_up(n, _):
            at = pl.ds(pl.multiple_of(n * 256, 256), 256)
            at_up = pl.ds(pl.multiple_of(FF_SLAB + n * 256, 256), 256)
            gate = dot(hnb[...], wg[index, :, at])
            up = dot(hnb[...], wg[index, :, at_up])
            gu[:, at] = gate
            gu[:, at_up] = up
            hid[:, at] = (gate * jax.nn.sigmoid(gate) * up).astype(BF16)
            return 0

        lax.fori_loop(0, FF_SLAB // 256, gate_up, 0)
        keep(gu, gu_out.at[index])
        keep(hid, hid_out.at[index])
        if index == 0:
            hop_one(1, 0)
            hop_two(0, 2)
            hop_one(1, 1)
        all_in(index, 2)
        weight_out(index, 2).start()
        saves[3].wait()
        if index == 0:
            reduce(hid, wd, slice(None), (None, lambda: hop_two(1, 0)))
            res[2] = (res[1] + total[...]).astype(BF16).astype(F32)
        for i in (1, 2, 4, 5):
            saves[i].wait()

    layer(0)
    layer(1)
    pltpu.make_async_copy(dm, dm_out, misc.at[0]).wait()
    for i in range(4):
        pltpu.make_async_copy(res.at[i], res_out.at[i], misc.at[i]).start()
    for i in range(4):
        pltpu.make_async_copy(res.at[i], res_out.at[i], misc.at[i]).wait()
    for i in range(6):
        twin_copy(i, core).wait_send()
    for index in range(2):
        for piece in range(3):
            weight_out(index, piece).wait()
            for move in hops(index, piece):
                move.wait_send()


def forward_call(ends, lens, gain, tables, w_in, w_out):
    width = ends.shape[1]
    rows = LINE * CORES * SLOT
    hbm = pl.BlockSpec(memory_space=pl.ANY)
    vmem = pl.BlockSpec(memory_space=pltpu.VMEM)
    shape = jax.ShapeDtypeStruct
    dma = pltpu.SemaphoreType.DMA
    line = dma((LINE, SUBS))
    block = pltpu.VMEM((LINE * SLOT, width), BF16)
    return pl.pallas_call(
        forward_body,
        out_shape=[
            shape((2, width, A_COLS), BF16),
            shape((2, width, 2 * FF_SLAB), BF16),
            shape((2, width, FF_SLAB), BF16),
            shape((2, rows, width), BF16),
            shape((2, rows, width), BF16),
            shape((2, rows, AO_AT), BF16),
            shape((2, rows, Q_SLAB), BF16),
            shape((2, rows, 2 * FF_SLAB), F32),
            shape((2, rows, FF_SLAB), BF16),
            shape((4, SLOT, width), F32),
            shape((rows, width), BF16),
            shape((SLOT, width), BF16),
            shape((2, 2, width), F32),
            shape((LINE * CORES * 8, 128), F32),
        ],
        in_specs=[vmem, vmem, vmem, vmem, hbm, hbm],
        out_specs=[hbm] * 11 + [vmem] * 3,
        scratch_shapes=[
            pltpu.VMEM((SLOT, width), BF16),
            pltpu.VMEM((w_in.shape[0], 128), BF16),
            pltpu.VMEM((w_in.shape[0], 128), BF16),
            pltpu.VMEM((w_in.shape[0], 128), BF16),
            pltpu.VMEM((w_in.shape[0], 128), BF16),
            pltpu.VMEM((2, width, A_COLS), BF16),
            pltpu.VMEM((2, width, 2 * FF_SLAB), BF16),
            pltpu.VMEM((2, width, FF_SLAB), BF16),
            pltpu.VMEM((rows, width), BF16),
            pltpu.VMEM((rows, width), BF16),
            pltpu.VMEM((rows, AO_AT), BF16),
            pltpu.VMEM((rows, Q_SLAB), BF16),
            pltpu.VMEM((rows, 2 * FF_SLAB), F32),
            pltpu.VMEM((rows, FF_SLAB), BF16),
            block,
            pltpu.VMEM((LINE * SLOT, width), F32),
            pltpu.VMEM((4, SLOT, width), F32),
            pltpu.VMEM((SLOT, width), F32),
            pltpu.VMEM((rows, width), BF16),
            block, block, block, block, block,
            dma((6,)), dma((6,)), dma((6,)), dma((2, 3, 4)), dma((2, 3, 4)),
            dma((4,)), dma((2,)), dma((2,)), dma((2, 6)), dma((2, 3)),
        ] + [line] * 21,
        compiler_params=pltpu.CompilerParams(
            collective_id=0, has_side_effects=True, vmem_limit_bytes=60 * 2**20
        ),
        name="forward_two_layers",
        cost_estimate=pl.CostEstimate(flops=16_000_000_000, bytes_accessed=600_000_000, transcendentals=0),
    )(ends, lens, gain, tables, w_in, w_out)


def spread_heads_high(wide):
    low = low_lanes((wide.shape[0], 128))
    parts = []
    for pair in range(GROUP // 2):
        block = wide[:, pair * 128:(pair + 1) * 128]
        parts.append(jnp.where(low, 0.0, pltpu.roll(block, 64, 1)))
        parts.append(jnp.where(low, 0.0, block))
    return jnp.concatenate(parts, 0)


CHUNKS = ((0, FF_SLAB), (FF_SLAB, FF_SLAB), (2 * FF_SLAB, FF_SLAB), (3 * FF_SLAB, A_COLS))
SLAB = 3 * FF_SLAB + A_COLS
FAR_SLOT = (1, 0, 0, 1)
WINDOW, EACH = 16, 16


def backward_body(
    replicas,
    cot_in, gain, lens, tables, res_in, dm_in, wa_in, wg_in, wd_in, xn_in, hn_in, qkv_in, ctx_in, gu_in, hid_in,
    fin, ends_out, gain_out, far_rx, near_rx,
    wa, wg, wd, xn, hn, qkv, ctx, gu, hid, dm, da, dgu, dqkv, theirs, ours, total, res, y_total,
    sib_buf, rx_up, rx_dn, tx_up, tx_dn, tx_far, tx_x, tx_y, tx_fin, stage, gain_loc, gain_x, gain_y, gain_line,
    end_tx, end_rx,
    load_sem, gu_sem, res_sem, far_send, far_recv, near_send, near_recv, fin_send, fin_recv, stage_sem, misc_send, misc_recv,
    *line_sems,
):
    gather_sems, gain_sems, reduce_sems, y_sems = line_sems[:5], line_sems[5:10], line_sems[10:16], line_sems[16:]
    here = Here()
    core, shard, place = here.core, here.shard, here.place
    width = cot_in.shape[1]
    part = width // SHARDS
    half = part // 2
    half_rows = LINE * SLOT
    base = here.depth - place

    barrier = pltpu.get_barrier_semaphore()
    for peer in (here.x_peer, here.y_peer):
        pl.semaphore_signal(barrier, inc=1, device_id=peer)
    for other in range(CORES):
        for where in range(LINE):
            @pl.when((core != other) | (place != where))
            def _():
                pl.semaphore_signal(barrier, inc=1, device_id={"section": other, "dp": base + where})

    pl.semaphore_wait(barrier, 2 + CORES * LINE - 1)

    NAMES = ("dm", "wd", "wg", "wa", "hid", "qkv", "ctx", "hn", "xn")
    VIEWS = {
        "wd": (wd_in, lambda l: wd), "wg": (wg_in, lambda l: wg), "wa": (wa_in, lambda l: wa),
        "hid": (hid_in, lambda l: hid), "qkv": (qkv_in, lambda l: qkv.at[l]), "ctx": (ctx_in, lambda l: ctx.at[l]),
        "hn": (hn_in, lambda l: hn), "xn": (xn_in, lambda l: xn),
    }

    def load(name, layer):
        if name == "dm":
            return pltpu.make_async_copy(dm_in, dm.at[1], load_sem.at[1, 0])
        src, dst = VIEWS[name]
        return pltpu.make_async_copy(src.at[layer], dst(layer), load_sem.at[layer, NAMES.index(name)])

    def gu_loads(layer, tile):
        return [
            pltpu.make_async_copy(
                gu_in.at[layer, :, pl.ds(i * FF_SLAB + tile * 256, 256)],
                gu.at[tile % 2, :, pl.ds(i * 256, 256)], gu_sem.at[tile % 2, i])
            for i in range(2)
        ]

    for name in ("dm", "hid", "wd"):
        load(name, 1).start()
    for tile in range(2):
        for copy in gu_loads(1, tile):
            copy.start()
    for name in ("hn", "wg", "wa", "qkv", "ctx"):
        load(name, 1).start()

    ready = set()

    def need(name, layer):
        if (name, layer) not in ready:
            ready.add((name, layer))
            load(name, layer).wait()

    gain_loc[...] = jnp.zeros_like(gain_loc)

    pending = {}

    waiting = []

    def pump(count):
        for _ in range(min(count, len(waiting))):
            waiting.pop(0).start()

    def claim(key):
        moves = pending.pop(key, ())
        for move in moves:
            if move in waiting:
                waiting.remove(move)
                move.start()
        for move in moves:
            move.wait_send()

    def products(layer, chunk, block, put):
        at = pl.ds(pl.multiple_of(block * part, part), part)
        need("hn" if chunk < 2 else "hid" if chunk == 2 else "xn", layer)

        def tiles(lhs, rhs, size, to):
            for lo in range(0, size, 512):
                hi = min(lo + 512, size)
                put(slice(to + lo, to + hi), dot_rows(lhs[:, at], rhs[:, lo:hi]))

        if chunk < 2:
            tiles(hn, dgu.at[layer, :, pl.ds(chunk * FF_SLAB, FF_SLAB)], FF_SLAB, 0)
        elif chunk == 2:
            tiles(dm.at[layer], hid, FF_SLAB, 0)
        else:
            tiles(xn, dqkv.at[layer], AO_AT, 0)
            tiles(da.at[layer], ctx.at[layer], Q_SLAB, AO_AT)

    def far_moves(layer, chunk):
        lo, size = CHUNKS[chunk]
        src = tx_far.at[FAR_SLOT[chunk]]
        cols = pl.ds(0, size)
        return [
            remote(src.at[pl.ds(i * half, half), cols], far_rx.at[layer, i, :, pl.ds(lo, size)],
                   far_send.at[layer, chunk, i], far_recv.at[layer, chunk, i], peer)
            for i, peer in ((0, here.x_peer), (1, here.y_peer))
        ]

    def near_moves(layer, chunk):
        lo, size = CHUNKS[chunk]
        cols = pl.ds(0, size)
        return [
            remote(src.at[chunk % 2, :, cols], near_rx.at[layer, i, :, pl.ds(lo, size)],
                   near_send.at[layer, chunk, i], near_recv.at[layer, chunk, i], peer)
            for i, (src, peer) in enumerate(((tx_x, here.x_peer), (tx_y, here.y_peer)))
        ]

    def stage_far(layer, chunk, i):
        lo, size = CHUNKS[chunk]
        return pltpu.make_async_copy(
            far_rx.at[layer, i, :, pl.ds(lo, size)], stage.at[i, pl.ds(0, half), pl.ds(0, size)], stage_sem.at[i])

    def stage_near(layer, chunk, i):
        lo, size = CHUNKS[chunk]
        return pltpu.make_async_copy(
            near_rx.at[layer, i, :, pl.ds(lo, size)], stage.at[i, :, pl.ds(0, size)], stage_sem.at[i])

    def step_one(layer, chunk):
        claim(("far", FAR_SLOT[chunk]))

        def put(cols, value):
            tx_far[FAR_SLOT[chunk], :, cols] = value.astype(BF16)

        products(layer, chunk, here.far_shard, put)
        moves = far_moves(layer, chunk)
        for move in moves:
            move.start()
        pending["far", FAR_SLOT[chunk]] = moves

    def step_two(layer, chunk):
        arrivals = far_moves(layer, chunk)
        for i in (1, 0):
            arrivals[i].wait_recv()
            stage_far(layer, chunk, i).start()
        claim(("near", chunk % 2))
        moves = near_moves(layer, chunk)

        def put_x(cols, value):
            tx_x[chunk % 2, :half, cols] = value[:half].astype(BF16)
            tx_x[chunk % 2, half:, cols] = (value[half:] + stage[1, :half, cols].astype(F32)).astype(BF16)

        def put_y(cols, value):
            tx_y[chunk % 2, :half, cols] = (value[:half] + stage[0, :half, cols].astype(F32)).astype(BF16)
            tx_y[chunk % 2, half:, cols] = value[half:].astype(BF16)

        stage_far(layer, chunk, 1).wait()
        products(layer, chunk, here.x_shard, put_x)
        moves[0].start()
        stage_far(layer, chunk, 0).wait()
        products(layer, chunk, here.y_shard, put_y)
        moves[1].start()
        pending["near", chunk % 2] = moves

    piece = part // (replicas * LINE)

    def fin_moves(layer, chunk):
        lo, size = CHUNKS[chunk]
        head = place * CORES + core
        moves = []
        for rep in range(replicas):
            for turn_by in (2, 3, 1, 0):
                where = lax.rem(place + turn_by, LINE)
                src = tx_fin.at[chunk % 2, pl.ds(pl.multiple_of((rep * LINE + where) * piece, piece), piece), pl.ds(0, size)]
                dst = fin.at[head, pl.ds(rep * piece, piece), pl.ds(lo, size)]
                same = (core == layer) & (place == where)
                move = remote(src, dst, fin_send.at[layer, chunk, rep, turn_by], fin_recv.at[rep, head, chunk],
                              {"section": layer, "dp": base + where})
                stay = pltpu.make_async_copy(src, dst, fin_send.at[layer, chunk, rep, turn_by])
                moves.append((same, move, stay))
        return moves

    class Leave:
        def __init__(self, entry):
            self.same, self.move, self.stay = entry

        def start(self):
            @pl.when(self.same)
            def _():
                self.stay.start()

            @pl.when(jnp.logical_not(self.same))
            def _():
                self.move.start()

        def wait_send(self):
            @pl.when(self.same)
            def _():
                self.stay.wait()

            @pl.when(jnp.logical_not(self.same))
            def _():
                self.move.wait_send()

    def step_three(layer, chunk):
        arrivals = near_moves(layer, chunk)
        for i in range(2):
            arrivals[i].wait_recv()
            stage_near(layer, chunk, i).start()
        claim(("fin", chunk % 2))
        stage_near(layer, chunk, 0).wait()
        stage_near(layer, chunk, 1).wait()

        def put(cols, value):
            tx_fin[chunk % 2, :, cols] = (
                value + stage[0, :, cols].astype(F32) + stage[1, :, cols].astype(F32)
            ).astype(BF16)

        products(layer, chunk, shard, put)
        moves = [Leave(entry) for entry in fin_moves(layer, chunk)]
        waiting.extend(moves)
        if layer == 0:
            pump(len(waiting))
        pending["fin", chunk % 2] = moves

    def steps(*todo):
        def run():
            pump(EACH)
            for kind, layer, chunk in todo:
                (step_one, step_two, step_three)[kind - 1](layer, chunk)
                if layer == 1 and kind == 3 and chunk == 0:
                    load("hn", 0).start()
                if layer == 1 and kind == 3 and chunk == 3:
                    load("xn", 0).start()
        return run

    reduce_bufs = (sib_buf, rx_up, rx_dn, tx_up, tx_dn)

    def own_block(ref, layer):
        return ref.at[layer, pl.ds(pl.multiple_of((core * LINE + place) * SLOT, SLOT), SLOT), :]

    def terms_of(src, weights, cols):
        def terms(whose, dst, sub):
            rows = pl.ds(pl.multiple_of(whose * half_rows, half_rows), half_rows)
            size = width // SUBS
            for lo in range(sub * size, (sub + 1) * size, 512):
                at = slice(lo, lo + 512)
                dst[:, at] = dot_last(src[rows, :], weights[at, cols]).astype(dst.dtype)
        return terms

    def reduce(slot, src, weights, cols, meanwhile):
        res_load(slot).start()
        line_reduce(here, total, ours, theirs, reduce_bufs, reduce_sems, terms_of(src, weights, cols), meanwhile)

    lower, upper = pl.ds(0, half_rows), pl.ds(half_rows, half_rows)
    y_bufs = (dm.at[0, lower], dm.at[0, upper], da.at[0, lower], da.at[0, upper], dgu.at[0, lower])
    y_theirs, y_ours = dgu.at[0, upper], xn.at[lower]
    y_steps = line_reduce_steps(here, y_total, y_ours, y_theirs, y_bufs, y_sems, terms_of(hid, wd, slice(None)))

    def y_step():
        next(y_steps, None)

    def res_load(slot):
        return pltpu.make_async_copy(res_in.at[slot], res, res_sem.at[slot])

    def norm_back(gain_row, slot):
        res_load(slot).wait()
        values = res[...]
        scale = root(values)
        grad = total[...]
        hat = grad * gain_row
        gain_loc[slot:slot + 1, :] = jnp.sum(grad * values * scale, 0, keepdims=True)
        inner = jnp.mean(hat * values, -1, keepdims=True)
        return scale * hat - values * (scale * scale * scale * inner)

    def layer_back(layer, grad_out, jobs):
        if layer == 1:
            need("dm", 1)
        else:
            own_block(dm, layer)[...] = grad_out.astype(BF16)
            line_gather(here, dm.at[layer], gather_sems, jobs[0])
        pump(WINDOW)
        step_one(layer, 2)
        need("wd", layer)
        tiles = FF_SLAB // 256
        for tile in range(tiles):
            at = slice(tile * 256, tile * 256 + 256)
            at_up = slice(FF_SLAB + tile * 256, FF_SLAB + tile * 256 + 256)
            grad = dot(dm[layer], wd[:, at])
            for copy in gu_loads(layer, tile):
                copy.wait()
            gate, up = gu[tile % 2, :, :256], gu[tile % 2, :, 256:]
            sig = jax.nn.sigmoid(gate)
            dgu[layer, :, at] = (grad * up * sig * (1.0 + gate * (1.0 - sig))).astype(BF16)
            dgu[layer, :, at_up] = (grad * gate * sig).astype(BF16)
            ahead = (layer, tile + 2) if tile + 2 < tiles else (layer - 1, tile + 2 - tiles)
            if ahead[0] >= 0:
                for copy in gu_loads(*ahead):
                    copy.start()
        step_one(layer, 0)
        need("wg", layer)
        reduce(2 * layer + 1, dgu.at[layer], wg, slice(None), jobs[1])
        if layer == 1:
            load("wg", 0).start()
            load("wd", 0).start()
        grad_mid = grad_out + norm_back(gain[layer, 1:2], 2 * layer + 1)
        own_block(da, layer)[...] = grad_mid.astype(BF16)
        line_gather(here, da.at[layer], gather_sems, jobs[2])
        pump(WINDOW)
        need("wa", layer)
        need("qkv", layer)
        need("ctx", layer)

        def attend(pair, _):
            at = pl.ds(pl.multiple_of(pair * 2 * SLOT, 2 * SLOT), 2 * SLOT)
            grad_ctx = dot(da[layer, at, :], wa[:, AO_AT:A_COLS]).astype(BF16).astype(F32)
            kv = qkv[layer, at, KV_AT:AO_AT]
            q = spread_heads(qkv[layer, at, :Q_SLAB].astype(F32)).astype(BF16)
            probs = two_slot_probs(q, kv, lens, pair)
            grad_high = spread_heads_high(grad_ctx).astype(BF16)
            grad_probs = dot_last(grad_high, kv)
            inner = jnp.sum(grad_probs * probs, -1, keepdims=True)
            grad_scores = (probs * (grad_probs - inner)).astype(BF16)
            grad_q = join_heads(dot(grad_scores, kv), False) * HEAD_DIM**-0.5
            grad_kv = dot_rows(grad_scores, q) * HEAD_DIM**-0.5 + dot_rows(probs.astype(BF16), grad_high)
            for i in range(GROUP // 2):
                cols = slice(128 * i, 128 * (i + 1))
                dqkv[layer, at, cols] = turn(grad_q[:, cols], tables[0], -tables[1]).astype(BF16)
            dqkv[layer, at, KV_AT:AO_AT] = turn(grad_kv, tables[2], -tables[3]).astype(BF16)
            return 0

        lax.fori_loop(0, LINE, attend, 0)
        reduce(2 * layer, dqkv.at[layer], wa, slice(0, AO_AT), jobs[3])
        if layer == 1:
            load("wa", 0).start()
            load("qkv", 0).start()
            load("ctx", 0).start()
        return grad_mid + norm_back(gain[layer, 0:1], 2 * layer)

    dx1 = layer_back(1, cot_in[...].astype(F32), (
        (),
        (lambda: (steps((1, 1, 1))(), y_step()), steps((2, 1, 2)), y_step),
        (y_step, steps((2, 1, 1)), lambda: (y_step(), load("xn", 1).start())),
        (steps((1, 1, 3), (2, 1, 0)), steps((3, 1, 2))),
    ))
    load("hid", 0).start()
    dx0 = layer_back(0, dx1.astype(BF16).astype(F32), (
        (steps((3, 1, 1)), None, steps((3, 1, 0), (2, 1, 3))),
        (steps((3, 1, 3), (1, 0, 1)), steps((2, 0, 2))),
        (None, steps((2, 0, 1))),
        (steps((1, 0, 3), (2, 0, 0)), steps((3, 0, 2))),
    ))

    res_load(3).start()

    gain_x_move = remote(gain_loc, gain_x, misc_send.at[1], misc_recv.at[1], here.x_peer)
    gain_x_move.start()
    steps((3, 0, 1))()
    gain_x_move.wait()
    gain_loc[...] += gain_x[...]
    gain_y_move = remote(gain_loc, gain_y, misc_send.at[2], misc_recv.at[2], here.y_peer)
    gain_y_move.start()
    steps((2, 0, 3))()
    gain_y_move.wait()
    cols = pl.ds(pl.multiple_of(shard * part, part), part)
    own_gains = pl.ds(pl.multiple_of((core * LINE + place) * 8, 8), 8)
    gain_line[own_gains, :] = gain_loc[:, cols] + gain_y[:, cols]
    res_load(3).wait()
    first = core == 0
    dx0 = dx0.astype(BF16).astype(F32)
    y1 = (res[...] + y_total[...]).astype(BF16).astype(F32)
    end_tx[...] = jnp.where(first, y1, dx0).astype(BF16)
    end_move = remote(end_tx, end_rx, misc_send.at[0], misc_recv.at[0], here.twin)
    end_move.start()

    line_gather(here, gain_line, gain_sems, (steps((3, 0, 0)), None, steps((3, 0, 3))), 1)
    gain_sum = gain_line[0:8, :]
    for i in range(1, LINE * CORES):
        gain_sum += gain_line[8 * i:8 * i + 8, :]
    gain_out[...] = gain_sum
    end_move.wait()
    crossed = end_rx[...].astype(F32)
    ends_out[:SLOT] = jnp.where(first, dx0, crossed).astype(BF16)
    ends_out[SLOT:] = jnp.where(first, crossed, y1).astype(BF16)
    for key in list(pending):
        claim(key)
    for rep in range(replicas):
        for where in range(LINE):
            for other in range(CORES):
                head = where * CORES + other

                @pl.when((core != other) | (place != where))
                def _():
                    for chunk, (lo, size) in enumerate(CHUNKS):
                        src = tx_fin.at[0, pl.ds(0, piece), pl.ds(0, size)]
                        dst = fin.at[head, pl.ds(rep * piece, piece), pl.ds(lo, size)]
                        remote(src, dst, fin_send.at[0, 0, 0, 0], fin_recv.at[rep, head, chunk],
                               {"section": 1 - core, "dp": base + where}).wait_recv()


def backward_call(replicas, cot, gain, lens, tables, res, dm, wa, wg, wd, xn, hn, qkv, ctx, gu, hid):
    width = cot.shape[1]
    rows = LINE * CORES * SLOT
    part = width // SHARDS
    hbm = pl.BlockSpec(memory_space=pl.ANY)
    vmem = pl.BlockSpec(memory_space=pltpu.VMEM)
    shape = jax.ShapeDtypeStruct
    dma = pltpu.SemaphoreType.DMA
    line = dma((LINE, SUBS))
    vm = pltpu.VMEM
    block = vm((LINE * SLOT, width), BF16)
    move = vm((2, part, FF_SLAB), BF16)
    return pl.pallas_call(
        functools.partial(backward_body, replicas),
        out_shape=[
            shape((KV_HEADS, part // LINE, SLAB), BF16),
            shape((CORES * SLOT, width), BF16),
            shape((8, part), F32),
            shape((2, 2, part // 2, SLAB), BF16),
            shape((2, 2, part, SLAB), BF16),
        ],
        in_specs=[vmem] * 4 + [hbm] * 11,
        out_specs=[hbm, vmem, vmem, hbm, hbm],
        scratch_shapes=[
            vm((width, A_COLS), BF16), vm((width, 2 * FF_SLAB), BF16), vm((width, FF_SLAB), BF16),
            vm((rows, width), BF16), vm((rows, width), BF16), vm((2, rows, AO_AT), BF16), vm((2, rows, Q_SLAB), BF16),
            vm((2, rows, 512), F32), vm((rows, FF_SLAB), BF16),
            vm((2, rows, width), BF16), vm((2, rows, width), BF16),
            vm((2, rows, 2 * FF_SLAB), BF16), vm((2, rows, AO_AT), BF16),
            block, vm((LINE * SLOT, width), F32), vm((SLOT, width), F32), vm((SLOT, width), F32), vm((SLOT, width), F32),
            block, block, block, block, block,
            move, move, move, move, move,
            vm((8, width), F32), vm((8, width), F32), vm((8, width), F32), vm((8 * LINE * CORES, part), F32),
            vm((SLOT, width), BF16), vm((SLOT, width), BF16),
            dma((2, 9)), dma((2, 2)), dma((4,)), dma((2, 4, 2)), dma((2, 4, 2)), dma((2, 4, 2)), dma((2, 4, 2)),
            dma((2, 4, replicas, LINE)), dma((replicas, KV_HEADS, 4)), dma((2,)), dma((3,)), dma((3,)),
        ] + [line] * 22,
        compiler_params=pltpu.CompilerParams(
            collective_id=1, has_side_effects=True, vmem_limit_bytes=62 * 2**20
        ),
        name="backward_two_layers",
        cost_estimate=pl.CostEstimate(flops=32_000_000_000, bytes_accessed=600_000_000, transcendentals=0),
    )(cot, gain, lens, tables, res, dm, wa, wg, wd, xn, hn, qkv, ctx, gu, hid)


def place_body(fin, in_out, out_out, held, wide_in, wide_out, load_sem, save_sem):
    steps = KV_HEADS // 2
    q_two, ff_two = 2 * Q_SLAB, 2 * FF_SLAB
    ff0 = Q_COLS + 2 * KV_COLS

    def fetch(step):
        return pltpu.make_async_copy(fin.at[pl.ds(2 * step, 2)], held.at[step % 2], load_sem.at[step % 2])

    def saves(step):
        slot = step % 2
        moves = []
        for i, (src, lo, dst, to, size) in enumerate((
            (wide_in, 0, in_out, step * q_two, q_two),
            (wide_in, q_two, in_out, Q_COLS + step * 128, 128),
            (wide_in, q_two + 128, in_out, Q_COLS + KV_COLS + step * 128, 128),
            (wide_in, q_two + 256, in_out, ff0 + step * ff_two, ff_two),
            (wide_in, q_two + 256 + ff_two, in_out, ff0 + FF + step * ff_two, ff_two),
            (wide_out, 0, out_out, step * q_two, q_two),
            (wide_out, q_two, out_out, Q_COLS + step * ff_two, ff_two),
        )):
            moves.append(pltpu.make_async_copy(
                src.at[slot, :, pl.ds(lo, size)], dst.at[:, pl.ds(to, size)], save_sem.at[slot, i]))
        return moves

    fetch(0).start()
    a_at = 3 * FF_SLAB
    for step in range(steps):
        slot = step % 2
        if step + 1 < steps:
            fetch(step + 1).start()
        fetch(step).wait()
        if step >= 2:
            for move in saves(step - 2):
                move.wait()
        for i in range(2):
            q_to = i * Q_SLAB
            wide_in[slot, :, q_to:q_to + Q_SLAB] = held[slot, i, :, a_at:a_at + Q_SLAB].astype(F32)
            wide_out[slot, :, q_to:q_to + Q_SLAB] = held[slot, i, :, a_at + AO_AT:a_at + A_COLS].astype(F32)
            for k, (src_ref, to) in enumerate(((wide_in, q_two + 256), (wide_in, q_two + 256 + ff_two), (wide_out, q_two))):
                at = to + i * FF_SLAB
                src_ref[slot, :, at:at + FF_SLAB] = held[slot, i, :, k * FF_SLAB:(k + 1) * FF_SLAB].astype(F32)
        one = held[slot, 0, :, a_at + KV_AT:a_at + AO_AT].astype(F32)
        two = held[slot, 1, :, a_at + KV_AT:a_at + AO_AT].astype(F32)
        low = low_lanes(one.shape)
        wide_in[slot, :, q_two:q_two + 128] = jnp.where(low, one, pltpu.roll(two, 64, 1))
        wide_in[slot, :, q_two + 128:q_two + 256] = jnp.where(low, pltpu.roll(one, 64, 1), two)
        for move in saves(step):
            move.start()
    for step in range(max(steps - 2, 0), steps):
        for move in saves(step):
            move.wait()


def place_call(fin, in_cols, out_cols):
    rows = fin.shape[1]
    hbm = pl.BlockSpec(memory_space=pl.ANY)
    q_two, ff_two = 2 * Q_SLAB, 2 * FF_SLAB
    return pl.pallas_call(
        place_body,
        out_shape=[jax.ShapeDtypeStruct((rows, in_cols), F32), jax.ShapeDtypeStruct((rows, out_cols), F32)],
        in_specs=[hbm],
        out_specs=[hbm, hbm],
        scratch_shapes=[
            pltpu.VMEM((2, 2, rows, SLAB), BF16),
            pltpu.VMEM((2, rows, q_two + 256 + 2 * ff_two), F32),
            pltpu.VMEM((2, rows, q_two + ff_two), F32),
            pltpu.SemaphoreType.DMA((2,)),
            pltpu.SemaphoreType.DMA((2, 7)),
        ],
        compiler_params=pltpu.CompilerParams(vmem_limit_bytes=60 * 2**20),
        name="place_columns",
    )(fin)


def rope_blocks():
    half_dim = HEAD_DIM // 2
    inverse = 500000.0 ** (-(jnp.arange(half_dim, dtype=F32) * 2.0 / HEAD_DIM))
    angles = jnp.arange(SLOT, dtype=F32)[:, None] * inverse[None, :]
    cos, sin = jnp.cos(angles), jnp.sin(angles)
    one, zero = jnp.ones((SLOT, HEAD_DIM), F32), jnp.zeros((SLOT, HEAD_DIM), F32)
    rows = [
        jnp.concatenate([cos] * 4, 1),
        jnp.concatenate([-sin, sin] * 2, 1),
        jnp.concatenate([cos, cos, one], 1),
        jnp.concatenate([-sin, sin, zero], 1),
    ]
    return jnp.stack([jnp.tile(block, (2, 1)) for block in rows])


def local(ends_in, in_weight, out_weight, norm_gain, seq_len):
    core = lax.axis_index("section")
    replicas = lax.axis_size("dp") // LINE
    own_length = jnp.where(core == 0, seq_len[0], seq_len[1])
    lens_block = jnp.full((8, 128), own_length.astype(F32))
    rope = rope_blocks()
    (wa, wg, wd, xn, hn, qkv, ctx, gu, hid, res, dm, cot, gains, lens) = forward_call(
        ends_in[0], lens_block, norm_gain[0], rope, in_weight[0], out_weight[0]
    )
    fin, ends_out, gain_sum, _, _ = backward_call(
        replicas, cot, gains, lens, rope, res, dm, wa, wg, wd, xn, hn, qkv, ctx, gu, hid
    )
    own_gain = lax.dynamic_slice_in_dim(gain_sum, 2 * core, 2, 0)
    if replicas > 1:
        groups = [[r * LINE + p for r in range(replicas)] for p in range(LINE)]
        fin = lax.psum_scatter(fin, "dp", scatter_dimension=1, tiled=True, axis_index_groups=groups)
        own_gain = lax.psum(own_gain, "dp", axis_index_groups=groups)
    in_grad, out_grad = place_call(fin, in_weight.shape[2], out_weight.shape[2])
    size = own_gain.shape[1] // lax.axis_size("dp")
    own_gain = lax.dynamic_slice_in_dim(own_gain, lax.axis_index("dp") * size, size, 1)
    return ends_out[None], in_grad[None], out_grad[None], own_gain[None]


def solution(mesh):
    in_specs = (
        P("section", ("shard", "dp"), None),
        P("section", "shard", None),
        P("section", "shard", None),
        P("section", None, None),
        P(("shard", "dp")),
    )
    out_specs = (
        P("section", ("shard", "dp"), None),
        P("section", ("shard", "dp"), None),
        P("section", ("shard", "dp"), None),
        P("section", None, ("shard", "dp")),
    )
    return jax.shard_map(local, mesh=mesh, in_specs=in_specs, out_specs=out_specs, check_vma=False)
```
